512 devices in a mesh: space: 64 (over z_hi, x, y), filt: 8 (over z_lo, core).
Axes of the slice: x: 4, y: 4, z: 16 (z_hi: 4, z_lo: 4; z = z_hi * 4 + z_lo), core: 2. Of those that a mesh axis runs over, the one named last changes fastest.
Arguments:
- volume: bfloat16 [64, 128, 8, 128], P('filt', 'space'), may hold values from -6 to 6
- weight: bfloat16 [27, 64, 128], P(None, None, 'filt'), may hold values from -0.21875 to 0.21875
- bias: float32 [128], P('filt'), may hold values from -3 to 3
- grad_out: bfloat16 [128, 128, 8, 128], P('filt', 'space'), may hold values from -6 to 6
Outputs:
- output: bfloat16 [128, 128, 8, 128], P('filt', 'space')
- grad_volume: bfloat16 [64, 128, 8, 128], P('filt', 'space')
- grad_weight: float32 [27, 64, 128], P(None, None, 'filt')
- grad_bias: float32 [128], P('filt')
The draws below stay inside these ranges and needn't reach their ends.
All inputs are finite; a program needn't handle non-finite values.
Results may differ from the reference program's by a relative error of at most 0.0012.
Values may be sent and summed in bfloat16 or wider, within the bound.
No kernel may reach another device: no remote copies, remote signals or barrier semaphores. Data moves between devices by JAX's collectives and lax.ppermute only.
A program may use at most 64 MiB of HBM per device.

```python
import math
import jax
import jax.numpy as jnp
from jax import lax

CIN = 64
COUT = 128
HH = 8
WW = 128
DEPTH = 128


def raised(result, stream_key, source, target, parts, factor):
    def block_of(axis_at):
        return (jnp.arange(result.shape[axis_at]) // (result.shape[axis_at] // parts)).reshape((-1,) + (1,) * (result.ndim - 1 - axis_at))

    first = jax.random.permutation(stream_key, parts)[block_of(target)]
    other_side = (block_of(target) + parts // 2) % parts
    return jnp.where((block_of(source) == first) | (block_of(source) == other_side), factor * result, result)


def block_scale(own_key, dims, split, low, largest):
    def one(dim, blocks):
        heights = jax.random.uniform(jax.random.fold_in(jax.random.fold_in(own_key, 6), dim), (blocks,), jnp.float32, low / len(split), largest / len(split))
        return jnp.repeat(jnp.exp(heights), dims[dim] // blocks).reshape((-1,) + (1,) * (len(dims) - dim - 1))

    loudness = one(*split[0])
    for cut in split[1:]:
        loudness = loudness * one(*cut)
    return loudness


def gaussian(own_key, shape, deviation, limit, split=(), dtype=jnp.bfloat16):
    level = block_scale(own_key, shape, split, -0.22, 0.18) if split else 1.0
    entries = jax.random.normal(own_key, shape, jnp.float32) * deviation * level
    return jnp.minimum(jnp.maximum(entries, -limit), limit).astype(dtype)


def heavy_noise(stream_key, shape, width, reach, split, heavy, dtype=jnp.bfloat16):
    array = width * jax.random.normal(stream_key, shape, jnp.float32)
    if split:
        array = array * block_scale(stream_key, shape, split, -0.22, 0.18)
    return jnp.clip(raised(array, jax.random.fold_in(stream_key, 3), *heavy), -reach, reach).astype(dtype)


def setup_inputs(seed: int = 0) -> dict:
    splits = jax.random.split(jax.random.key(seed), 5)
    return {
        "volume": gaussian(splits[0], (CIN, DEPTH, HH, WW), 1.0, 6.0, ((0, 8), (1, 64))),
        "weight": heavy_noise(splits[1], (27, CIN, COUT), (27 * CIN) ** -0.5, 0.21875, ((2, 8),), (2, 1, 8, 2.0)),
        "bias": gaussian(splits[2], (COUT,), 0.5, 3.0, ((0, 8),), jnp.float32),
        "grad_out": gaussian(splits[3], (COUT, DEPTH, HH, WW), 1.0, 6.0, ((0, 8), (1, 64))),
    }


def reference(volume, weight, bias, grad_out):
    kernel = weight.reshape(3, 3, 3, CIN, COUT).transpose(4, 3, 0, 1, 2)
    numbers = ('NCDHW', 'OIDHW', 'NCDHW')
    conv = lax.conv_general_dilated(volume[None], kernel, (1, 1, 1), [(1, 1), (1, 1), (1, 1)], dimension_numbers=numbers, preferred_element_type=jnp.float32)[0]
    output = (conv + bias[:, None, None, None]).astype(jnp.bfloat16)
    flipped = weight.reshape(3, 3, 3, CIN, COUT).transpose(3, 4, 0, 1, 2)[:, :, ::-1, ::-1, ::-1]
    back = lax.conv_general_dilated(grad_out[None], flipped, (1, 1, 1), [(1, 1), (1, 1), (1, 1)], dimension_numbers=numbers, preferred_element_type=jnp.float32)[0]
    grad_volume = back.astype(jnp.bfloat16)
    padded = jnp.pad(volume, ((0, 0), (1, 1), (1, 1), (1, 1)))
    depth = volume.shape[1]
    flat_grad = grad_out.reshape(COUT, -1)
    taps = []
    for tap in range(27):
        a, b, c = (tap // 9, tap // 3 % 3, tap % 3)
        moved = padded[:, a:a + depth, b:b + HH, c:c + WW].reshape(CIN, -1)
        taps.append(jnp.dot(moved, flat_grad.T, preferred_element_type=jnp.float32))
    scale = 1.0 / math.sqrt(depth * HH * WW)
    grad_weight = jnp.stack(taps) * scale
    grad_bias = lax.optimization_barrier(jnp.sum(grad_out.astype(jnp.float32), axis=(1, 2, 3))) * scale
    return (output, grad_volume, grad_weight, grad_bias)
```

```python
import math

import jax
import jax.numpy as jnp
from jax import lax
from jax.experimental import pallas as pl
from jax.experimental.pallas import tpu as pltpu
from jax.sharding import PartitionSpec as P

F32 = jnp.float32
BF16 = jnp.bfloat16


def dot(left, right):
    return lax.dot_general(left, right, (((1,), (0,)), ((), ())), preferred_element_type=F32)


def dot_lanes(left, right):
    return lax.dot_general(left, right, (((1,), (1,)), ((), ())), preferred_element_type=F32)


def slide(rows, step):
    size = rows.shape[-1]
    axis = rows.ndim - 1
    turned = pltpu.roll(rows, (-step) % size, axis)
    lane = lax.broadcasted_iota(jnp.int32, rows.shape, axis)
    edge = size - 1 if step > 0 else 0
    return jnp.where(lane == edge, 0.0, turned)


def kernel(
    vol_ref, grad_ref, before_ref, after_ref, taps_ref,
    sums_ref, back_ref, out_ref, low_ref, high_ref,
    vpad, gpad, mid,
):
    depth, rows, chans, cols = vol_ref.shape
    outs = grad_ref.shape[2]
    blank = jnp.zeros((chans, cols), BF16)
    for d in range(depth):
        vpad[d, 0] = blank
        vpad[d, rows + 1] = blank
        vpad[d, 1 : rows + 1] = vol_ref[d]
    blank = jnp.zeros((3 * outs, cols), BF16)
    bias_sum = jnp.zeros((outs, cols), F32)
    for p in range(depth + 2):
        gpad[p, 0] = blank
        gpad[p, rows + 1] = blank
        for h in range(rows):
            if p == 0:
                line = before_ref[0, h]
            elif p == depth + 1:
                line = after_ref[0, h]
            else:
                line = grad_ref[p - 1, h]
            wide = line.astype(F32)
            if 0 < p < depth + 1:
                bias_sum = bias_sum + wide
            gpad[p, h + 1, 0:outs] = slide(wide, 1).astype(BF16)
            gpad[p, h + 1, outs : 2 * outs] = line
            gpad[p, h + 1, 2 * outs : 3 * outs] = slide(wide, -1).astype(BF16)
    taps = taps_ref[...]
    ahead = jnp.concatenate(
        [
            jnp.concatenate([taps[9 * a + 3 * b + c] for b in range(3)], axis=1)
            for a in range(3)
            for c in range(3)
        ],
        axis=0,
    )
    flat = taps.reshape(27 * outs, chans)
    behind = flat.astype(F32).T.astype(BF16)
    acc = jnp.zeros((27 * outs, chans), F32)
    for d in range(depth):
        for h in range(0, rows, 2):
            stack = jnp.concatenate(
                [vpad[d, h + k : h + k + 3].reshape(3 * chans, cols) for k in range(2)], axis=1
            )
            part = dot(ahead, stack)
            for k in range(2):
                mid[d, h + k] = part[:, k * cols : (k + 1) * cols]
            moved = jnp.concatenate(
                [
                    jnp.concatenate(
                        [gpad[d + 2 - a, h + k + 2 - b] for a in range(3) for b in range(3)], axis=0
                    )
                    for k in range(2)
                ],
                axis=1,
            )
            back = dot(behind, moved)
            for k in range(2):
                for f in range(chans // 8):
                    back_ref[f, d, h + k] = back[8 * f : 8 * f + 8, k * cols : (k + 1) * cols]
            cells = jnp.concatenate([vol_ref[d, h], vol_ref[d, h + 1]], axis=1)
            acc = acc + dot_lanes(moved, cells)
    for e in range(-1, depth + 1):
        for h in range(rows):
            total = None
            for d in range(depth):
                a = d - e + 1
                if 0 <= a <= 2:
                    piece = mid[d, h, 3 * outs * a : 3 * outs * (a + 1)]
                    total = piece if total is None else total + piece
            line = (
                total[outs : 2 * outs]
                + slide(total[0:outs], -1)
                + slide(total[2 * outs : 3 * outs], 1)
            )
            if e < 0:
                low_ref[h] = line
            elif e == depth:
                high_ref[h] = line
            else:
                out_ref[e, h] = line
    half = cols // 2
    bias_half = bias_sum[:, :half] + bias_sum[:, half:]
    for r in range(14):
        first = acc[2 * r * outs : (2 * r + 1) * outs]
        second = bias_half if r == 13 else acc[(2 * r + 1) * outs : (2 * r + 2) * outs]
        sums_ref[r] = jnp.concatenate([first, second], axis=1)
    for r in range(14, 16):
        sums_ref[r] = jnp.zeros((outs, cols), F32)


def compute(vol, grad, before, after, taps):
    depth, rows, chans, cols = vol.shape
    outs = grad.shape[2]
    shapes = (
        jax.ShapeDtypeStruct((16, outs, cols), F32),
        jax.ShapeDtypeStruct((chans // 8, depth, rows, 8, cols), F32),
        jax.ShapeDtypeStruct((depth, rows, outs, cols), F32),
        jax.ShapeDtypeStruct((rows, outs, cols), F32),
        jax.ShapeDtypeStruct((rows, outs, cols), F32),
    )
    whole = pl.BlockSpec(memory_space=pltpu.VMEM)
    return pl.pallas_call(
        kernel,
        out_shape=shapes,
        in_specs=[whole] * 5,
        out_specs=(whole,) * 5,
        scratch_shapes=[
            pltpu.VMEM((depth, rows + 2, chans, cols), BF16),
            pltpu.VMEM((depth + 2, rows + 2, 3 * outs, cols), BF16),
            pltpu.VMEM((depth, rows, 9 * outs, cols), F32),
        ],
        compiler_params=pltpu.CompilerParams(vmem_limit_bytes=40 * 1024 * 1024),
    )(vol, grad, before, after, taps)


XY_GROUPS = [[16 * z + k for k in range(16)] for z in range(4)]
Z_GROUPS = [[16 * z + k for z in range(4)] for k in range(16)]
UP = [(i, i + 1) for i in range(63)]
DOWN = [(i + 1, i) for i in range(63)]


def local(volume, weight, bias, grad_out):
    depth, rows, cols = volume.shape[1:]
    grad = grad_out.transpose(1, 2, 0, 3)
    before = lax.ppermute(grad[depth - 1 :], "space", UP)
    after = lax.ppermute(grad[:1], "space", DOWN)
    vol = lax.all_gather(volume.transpose(1, 2, 0, 3), "filt", axis=2, tiled=True)
    sums, back, out, low, high = compute(vol, grad, before, after, weight.transpose(0, 2, 1))
    from_above = lax.ppermute(low, "space", DOWN)
    from_below = lax.ppermute(high, "space", UP)
    parts = lax.all_to_all(sums, "space", 0, 0, axis_index_groups=XY_GROUPS)
    mine = lax.psum(jnp.sum(parts, axis=0), "space", axis_index_groups=Z_GROUPS)
    every = lax.all_to_all(
        jnp.broadcast_to(mine[None], (16,) + mine.shape), "space", 0, 0, axis_index_groups=XY_GROUPS
    )
    scale = 1.0 / math.sqrt(depth * lax.axis_size("space") * rows * cols)
    outs = grad_out.shape[0]
    every = every * scale
    halves = every.reshape(16, outs, 2, cols // 2)
    grad_weight = halves.transpose(0, 2, 3, 1).reshape(32, cols // 2, outs)[:27]
    grad_bias = jnp.sum(every[13, :, cols // 2 :], axis=1)
    shares = lax.all_to_all(back, "filt", 0, 0)
    grad_volume = jnp.sum(shares, axis=0).astype(BF16).transpose(2, 0, 1, 3)
    out = out + jnp.concatenate([from_below[None], from_above[None]], axis=0) + bias[None, None, :, None]
    output = out.astype(BF16).transpose(2, 0, 1, 3)
    return (output, grad_volume, grad_weight, grad_bias)


def solution(mesh):
    in_specs = (
        P("filt", "space", None, None),
        P(None, None, "filt"),
        P("filt"),
        P("filt", "space", None, None),
    )
    out_specs = (
        P("filt", "space", None, None),
        P("filt", "space", None, None),
        P(None, None, "filt"),
        P("filt"),
    )
    return jax.shard_map(local, mesh=mesh, in_specs=in_specs, out_specs=out_specs, check_vma=False)
```

```python
import math

import jax
import jax.numpy as jnp
from jax import lax
from jax.experimental import pallas as pl
from jax.experimental.pallas import tpu as pltpu
from jax.sharding import PartitionSpec as P

F32 = jnp.float32
BF16 = jnp.bfloat16


def dot(left, right):
    return lax.dot_general(left, right, (((1,), (0,)), ((), ())), preferred_element_type=F32)


def dot_lanes(left, right):
    return lax.dot_general(left, right, (((1,), (1,)), ((), ())), preferred_element_type=F32)


def slide(rows, step):
    size = rows.shape[-1]
    axis = rows.ndim - 1
    turned = pltpu.roll(rows, (-step) % size, axis)
    lane = lax.broadcasted_iota(jnp.int32, rows.shape, axis)
    edge = size - 1 if step > 0 else 0
    return jnp.where(lane == edge, 0.0, turned)


def kernel(
    vol_ref, grad_ref, before_ref, after_ref, taps_ref,
    sums_ref, back_ref, out_ref, low_ref, high_ref,
    vpad, gpad, mid,
):
    peers, depth, rows, share, cols = vol_ref.shape
    chans = peers * share
    outs = grad_ref.shape[2]
    blank = jnp.zeros((chans, cols), BF16)
    for d in range(depth):
        vpad[d, 0] = blank
        vpad[d, rows + 1] = blank
        for h in range(rows):
            vpad[d, h + 1] = jnp.concatenate([vol_ref[s, d, h] for s in range(peers)], axis=0)
    blank = jnp.zeros((3 * outs, cols), BF16)
    bias_sum = jnp.zeros((outs, cols), F32)
    for p in range(depth + 2):
        gpad[p, 0] = blank
        gpad[p, rows + 1] = blank
        for h in range(rows):
            if p == 0:
                line = before_ref[0, h]
            elif p == depth + 1:
                line = after_ref[0, h]
            else:
                line = grad_ref[p - 1, h]
            wide = line.astype(F32)
            if 0 < p < depth + 1:
                bias_sum = bias_sum + wide
            gpad[p, h + 1, 0:outs] = slide(wide, 1).astype(BF16)
            gpad[p, h + 1, outs : 2 * outs] = line
            gpad[p, h + 1, 2 * outs : 3 * outs] = slide(wide, -1).astype(BF16)
    taps = taps_ref[...]
    ahead = jnp.concatenate(
        [
            jnp.concatenate([taps[9 * a + 3 * b + c] for b in range(3)], axis=1)
            for a in range(3)
            for c in range(3)
        ],
        axis=0,
    )
    flat = taps.reshape(27 * outs, chans)
    behind = flat.astype(F32).T.astype(BF16)
    acc = jnp.zeros((27 * outs, chans), F32)
    for d in range(depth):
        for h in range(0, rows, 2):
            stack = jnp.concatenate(
                [vpad[d, h + k : h + k + 3].reshape(3 * chans, cols) for k in range(2)], axis=1
            )
            part = dot(ahead, stack)
            for k in range(2):
                mid[d, h + k] = part[:, k * cols : (k + 1) * cols]
            moved = jnp.concatenate(
                [
                    jnp.concatenate(
                        [gpad[d + 2 - a, h + k + 2 - b] for a in range(3) for b in range(3)], axis=0
                    )
                    for k in range(2)
                ],
                axis=1,
            )
            back = dot(behind, moved)
            for k in range(2):
                for f in range(chans // 8):
                    back_ref[f, d, h + k] = back[8 * f : 8 * f + 8, k * cols : (k + 1) * cols]
            cells = jnp.concatenate([vpad[d, h + 1], vpad[d, h + 2]], axis=1)
            acc = acc + dot_lanes(moved, cells)
    for e in range(-1, depth + 1):
        for h in range(rows):
            total = None
            for d in range(depth):
                a = d - e + 1
                if 0 <= a <= 2:
                    piece = mid[d, h, 3 * outs * a : 3 * outs * (a + 1)]
                    total = piece if total is None else total + piece
            line = (
                total[outs : 2 * outs]
                + slide(total[0:outs], -1)
                + slide(total[2 * outs : 3 * outs], 1)
            )
            if e < 0:
                low_ref[h] = line
            elif e == depth:
                high_ref[h] = line
            else:
                out_ref[e, h] = line
    half = cols // 2
    bias_half = bias_sum[:, :half] + bias_sum[:, half:]
    for r in range(14):
        first = acc[2 * r * outs : (2 * r + 1) * outs]
        second = bias_half if r == 13 else acc[(2 * r + 1) * outs : (2 * r + 2) * outs]
        sums_ref[r] = jnp.concatenate([first, second], axis=1)
    for r in range(14, 16):
        sums_ref[r] = jnp.zeros((outs, cols), F32)


def compute(vol, grad, before, after, taps):
    peers, depth, rows, share, cols = vol.shape
    chans = peers * share
    outs = grad.shape[2]
    shapes = (
        jax.ShapeDtypeStruct((16, outs, cols), F32),
        jax.ShapeDtypeStruct((chans // 8, depth, rows, 8, cols), F32),
        jax.ShapeDtypeStruct((depth, rows, outs, cols), F32),
        jax.ShapeDtypeStruct((rows, outs, cols), F32),
        jax.ShapeDtypeStruct((rows, outs, cols), F32),
    )
    whole = pl.BlockSpec(memory_space=pltpu.VMEM)
    return pl.pallas_call(
        kernel,
        out_shape=shapes,
        in_specs=[whole] * 5,
        out_specs=(whole,) * 5,
        scratch_shapes=[
            pltpu.VMEM((depth, rows + 2, chans, cols), BF16),
            pltpu.VMEM((depth + 2, rows + 2, 3 * outs, cols), BF16),
            pltpu.VMEM((depth, rows, 9 * outs, cols), F32),
        ],
        compiler_params=pltpu.CompilerParams(vmem_limit_bytes=40 * 1024 * 1024),
    )(vol, grad, before, after, taps)


XY_GROUPS = [[16 * z + k for k in range(16)] for z in range(4)]
Z_GROUPS = [[16 * z + k for z in range(4)] for k in range(16)]
EVEN = [(i, i ^ 1) for i in range(64)]
ODD = [(i, ((i + 1) ^ 1) - 1) for i in range(1, 63)]


def swap_edges(head, tail):
    odd = (lax.axis_index("space") % 2) == 1
    inner = lax.ppermute(jnp.where(odd, head, tail), "space", EVEN)
    outer = lax.ppermute(jnp.where(odd, tail, head), "space", ODD)
    return jnp.where(odd, inner, outer), jnp.where(odd, outer, inner)


def local(volume, weight, bias, grad_out):
    depth, rows, cols = volume.shape[1:]
    grad = grad_out.transpose(1, 2, 0, 3)
    before, after = swap_edges(grad[:1], grad[depth - 1 :])
    own = volume.transpose(1, 2, 0, 3)
    vol = lax.all_to_all(jnp.broadcast_to(own[None], (8,) + own.shape), "filt", 0, 0)
    sums, back, out, low, high = compute(vol, grad, before, after, weight.transpose(0, 2, 1))
    from_below, from_above = swap_edges(low, high)
    shares = lax.all_to_all(back, "filt", 0, 0)
    parts = lax.all_to_all(sums, "space", 0, 0, axis_index_groups=XY_GROUPS)
    mine = lax.psum(jnp.sum(parts, axis=0), "space", axis_index_groups=Z_GROUPS)
    mine, shares, from_below, from_above = lax.optimization_barrier(
        (mine, shares, from_below, from_above)
    )
    every = lax.all_to_all(
        jnp.broadcast_to(mine[None], (16,) + mine.shape), "space", 0, 0, axis_index_groups=XY_GROUPS
    )
    scale = 1.0 / math.sqrt(depth * lax.axis_size("space") * rows * cols)
    outs = grad_out.shape[0]
    every = every * scale
    halves = every.reshape(16, outs, 2, cols // 2)
    grad_weight = halves.transpose(0, 2, 3, 1).reshape(32, cols // 2, outs)[:27]
    grad_bias = jnp.sum(every[13, :, cols // 2 :], axis=1)
    grad_volume = jnp.sum(shares, axis=0).astype(BF16).transpose(2, 0, 1, 3)
    out = out + jnp.concatenate([from_below[None], from_above[None]], axis=0) + bias[None, None, :, None]
    output = out.astype(BF16).transpose(2, 0, 1, 3)
    return (output, grad_volume, grad_weight, grad_bias)


def solution(mesh):
    in_specs = (
        P("filt", "space", None, None),
        P(None, None, "filt"),
        P("filt"),
        P("filt", "space", None, None),
    )
    out_specs = (
        P("filt", "space", None, None),
        P("filt", "space", None, None),
        P(None, None, "filt"),
        P("filt"),
    )
    return jax.shard_map(local, mesh=mesh, in_specs=in_specs, out_specs=out_specs, check_vma=False)
```

```python
import math

import jax
import jax.numpy as jnp
from jax import lax
from jax.experimental import pallas as pl
from jax.experimental.pallas import tpu as pltpu
from jax.sharding import PartitionSpec as P

F32 = jnp.float32
BF16 = jnp.bfloat16
WHOLE = pl.BlockSpec(memory_space=pltpu.VMEM)
PARAMS = pltpu.CompilerParams(vmem_limit_bytes=40 * 1024 * 1024)


def dot(left, right):
    return lax.dot_general(left, right, (((1,), (0,)), ((), ())), preferred_element_type=F32)


def dot_lanes(left, right):
    return lax.dot_general(left, right, (((1,), (1,)), ((), ())), preferred_element_type=F32)


def slide(rows, step):
    size = rows.shape[-1]
    axis = rows.ndim - 1
    turned = pltpu.roll(rows, (-step) % size, axis)
    lane = lax.broadcasted_iota(jnp.int32, rows.shape, axis)
    edge = size - 1 if step > 0 else 0
    return jnp.where(lane == edge, 0.0, turned)


def gradients(vol_ref, grad_ref, before_ref, after_ref, taps_ref, sums_ref, pack_ref, gpad):
    peers, depth, rows, share, cols = vol_ref.shape
    outs = grad_ref.shape[2]
    blank = jnp.zeros((3 * outs, cols), BF16)
    bias_sum = jnp.zeros((outs, cols), F32)
    for p in range(depth + 2):
        gpad[p, 0] = blank
        gpad[p, rows + 1] = blank
        for h in range(rows):
            if p == 0:
                line = before_ref[h, 0:outs]
            elif p == depth + 1:
                line = after_ref[h, 0:outs]
            else:
                line = grad_ref[p - 1, h]
            wide = line.astype(F32)
            if 0 < p < depth + 1:
                bias_sum = bias_sum + wide
            gpad[p, h + 1, 0:outs] = slide(wide, 1).astype(BF16)
            gpad[p, h + 1, outs : 2 * outs] = line
            gpad[p, h + 1, 2 * outs : 3 * outs] = slide(wide, -1).astype(BF16)
    taps = taps_ref[...]
    chans = taps.shape[2]
    behind = taps.reshape(27 * outs, chans).astype(F32).T.astype(BF16)
    acc = jnp.zeros((27 * outs, chans), F32)
    for d in range(depth):
        for h in range(0, rows, 2):
            moved = jnp.concatenate(
                [
                    jnp.concatenate(
                        [gpad[d + 2 - a, h + k + 2 - b] for a in range(3) for b in range(3)], axis=0
                    )
                    for k in range(2)
                ],
                axis=1,
            )
            back = dot(behind, moved)
            for k in range(2):
                for f in range(peers):
                    value = back[share * f : share * (f + 1), k * cols : (k + 1) * cols]
                    high = value.astype(BF16)
                    pack_ref[f, 0, d, h + k] = high
                    pack_ref[f, 1, d, h + k] = (value - high.astype(F32)).astype(BF16)
            cells = jnp.concatenate(
                [
                    jnp.concatenate([vol_ref[s, d, h + k] for s in range(peers)], axis=0)
                    for k in range(2)
                ],
                axis=1,
            )
            acc = acc + dot_lanes(moved, cells)
    for h in range(rows):
        for d, side in enumerate((before_ref, after_ref)):
            line = side[h, outs : outs + share]
            for f in range(peers):
                pack_ref[f, 2, d, h] = line
    half = cols // 2
    bias_half = bias_sum[:, :half] + bias_sum[:, half:]
    for r in range(14):
        first = acc[2 * r * outs : (2 * r + 1) * outs]
        second = bias_half if r == 13 else acc[(2 * r + 1) * outs : (2 * r + 2) * outs]
        sums_ref[r] = jnp.concatenate([first, second], axis=1)
    for r in range(14, 16):
        sums_ref[r] = jnp.zeros((outs, cols), F32)


def finish(vol_ref, pack_ref, taps_ref, bias_ref, out_ref, back_ref, vpad):
    peers, depth, rows, share, cols = vol_ref.shape
    taps = taps_ref[...]
    outs, chans = taps.shape[1:]
    blank = jnp.zeros((chans, cols), BF16)
    for p in range(depth + 2):
        vpad[p, 0] = blank
        vpad[p, rows + 1] = blank
        for h in range(rows):
            if p == 0:
                lines = [pack_ref[s, 2, 0, h] for s in range(peers)]
            elif p == depth + 1:
                lines = [pack_ref[s, 2, 1, h] for s in range(peers)]
            else:
                lines = [vol_ref[s, p - 1, h] for s in range(peers)]
            vpad[p, h + 1] = jnp.concatenate(lines, axis=0)
    ahead = jnp.concatenate(
        [
            jnp.concatenate([taps[9 * a + 3 * b + c] for a in range(3) for b in range(3)], axis=1)
            for c in range(3)
        ],
        axis=0,
    )
    bias = jnp.broadcast_to(bias_ref[...], (outs, cols))
    for d in range(depth):
        lines = []
        for h in range(0, rows, 2):
            stack = jnp.concatenate(
                [
                    vpad[d : d + 3, h + k : h + k + 3].reshape(9 * chans, cols)
                    for k in range(2)
                ],
                axis=1,
            )
            part = dot(ahead, stack)
            for k in range(2):
                total = part[:, k * cols : (k + 1) * cols]
                lines.append(
                    total[outs : 2 * outs]
                    + slide(total[0:outs], -1)
                    + slide(total[2 * outs : 3 * outs], 1)
                    + bias
                )
        block = jnp.stack(lines)
        out_ref[:, d] = jnp.swapaxes(block, 0, 1).astype(BF16)
        lines = []
        for h in range(rows):
            total = None
            for s in range(peers):
                value = pack_ref[s, 0, d, h].astype(F32) + pack_ref[s, 1, d, h].astype(F32)
                total = value if total is None else total + value
            lines.append(total)
        back_ref[:, d] = jnp.swapaxes(jnp.stack(lines), 0, 1).astype(BF16)


def unpack(scale, every_ref, weight_ref, bias_ref):
    outs, cols = every_ref.shape[1:]
    half = cols // 2
    for t in range(27):
        r, side = t // 2, t % 2
        weight_ref[t] = every_ref[r, :, half * side : half * (side + 1)] * scale
    total = jnp.sum(every_ref[13, :, half:] * scale, axis=1, keepdims=True)
    wide = jnp.broadcast_to(total, (outs, cols))
    row = lax.broadcasted_iota(jnp.int32, (outs, cols), 0)
    lane = lax.broadcasted_iota(jnp.int32, (outs, cols), 1)
    flat = jnp.sum(jnp.where(row == lane, wide, 0.0), axis=0, keepdims=True)
    bias_ref[...] = flat[:, :outs]


XY_GROUPS = [[16 * z + k for k in range(16)] for z in range(4)]
Z_GROUPS = [[16 * z + k for z in range(4)] for k in range(16)]
EVEN = [(i, i ^ 1) for i in range(64)]
ODD = [(i, ((i + 1) ^ 1) - 1) for i in range(1, 63)]


def swap_edges(head, tail):
    odd = (lax.axis_index("space") % 2) == 1
    inner = lax.ppermute(jnp.where(odd, head, tail), "space", EVEN)
    outer = lax.ppermute(jnp.where(odd, tail, head), "space", ODD)
    return jnp.where(odd, inner, outer), jnp.where(odd, outer, inner)


def local(volume, weight, bias, grad_out):
    share, depth, rows, cols = volume.shape
    outs = grad_out.shape[0]
    chans = weight.shape[1]
    taps = weight.transpose(0, 2, 1)
    grad = grad_out.transpose(1, 2, 0, 3)
    own = volume.transpose(1, 2, 0, 3)
    both = jnp.concatenate([grad, own], axis=2)
    before, after = swap_edges(both[0], both[depth - 1])
    vol = lax.all_to_all(jnp.broadcast_to(own[None], (8,) + own.shape), "filt", 0, 0)
    sums, pack = pl.pallas_call(
        gradients,
        out_shape=(
            jax.ShapeDtypeStruct((16, outs, cols), F32),
            jax.ShapeDtypeStruct((8, 3, depth, rows, share, cols), BF16),
        ),
        in_specs=[WHOLE] * 5,
        out_specs=(WHOLE,) * 2,
        scratch_shapes=[pltpu.VMEM((depth + 2, rows + 2, 3 * outs, cols), BF16)],
        compiler_params=PARAMS,
    )(vol, grad, before, after, taps)
    parts = lax.all_to_all(sums, "space", 0, 0, axis_index_groups=XY_GROUPS)
    shares = lax.all_to_all(pack, "filt", 0, 0)
    mine = lax.psum(jnp.sum(parts, axis=0), "space", axis_index_groups=Z_GROUPS)
    mine, shares = lax.optimization_barrier((mine, shares))
    every = lax.all_to_all(
        jnp.broadcast_to(mine[None], (16,) + mine.shape), "space", 0, 0, axis_index_groups=XY_GROUPS
    )
    output, grad_volume = pl.pallas_call(
        finish,
        out_shape=(
            jax.ShapeDtypeStruct((outs, depth, rows, cols), BF16),
            jax.ShapeDtypeStruct((share, depth, rows, cols), BF16),
        ),
        in_specs=[WHOLE] * 4,
        out_specs=(WHOLE,) * 2,
        scratch_shapes=[pltpu.VMEM((depth + 2, rows + 2, chans, cols), BF16)],
        compiler_params=PARAMS,
    )(vol, shares, taps, bias[:, None])
    scale = 1.0 / math.sqrt(depth * lax.axis_size("space") * rows * cols)
    grad_taps, grad_bias = pl.pallas_call(
        lambda *refs: unpack(scale, *refs),
        out_shape=(
            jax.ShapeDtypeStruct((27, outs, cols // 2), F32),
            jax.ShapeDtypeStruct((1, outs), F32),
        ),
        in_specs=[WHOLE],
        out_specs=(WHOLE,) * 2,
        compiler_params=PARAMS,
    )(every)
    return (output, grad_volume, grad_taps.transpose(0, 2, 1), grad_bias.reshape(outs))


def solution(mesh):
    in_specs = (
        P("filt", "space", None, None),
        P(None, None, "filt"),
        P("filt"),
        P("filt", "space", None, None),
    )
    out_specs = (
        P("filt", "space", None, None),
        P("filt", "space", None, None),
        P(None, None, "filt"),
        P("filt"),
    )
    return jax.shard_map(local, mesh=mesh, in_specs=in_specs, out_specs=out_specs, check_vma=False)
```

```python
import math

import jax
import jax.numpy as jnp
from jax import lax
from jax.experimental import pallas as pl
from jax.experimental.pallas import tpu as pltpu
from jax.sharding import PartitionSpec as P

F32 = jnp.float32
BF16 = jnp.bfloat16
WHOLE = pl.BlockSpec(memory_space=pltpu.VMEM)
PARAMS = pltpu.CompilerParams(vmem_limit_bytes=40 * 1024 * 1024)


def dot(left, right):
    return lax.dot_general(left, right, (((1,), (0,)), ((), ())), preferred_element_type=F32)


def dot_lanes(left, right):
    return lax.dot_general(left, right, (((1,), (1,)), ((), ())), preferred_element_type=F32)


def slide(rows, step):
    size = rows.shape[-1]
    axis = rows.ndim - 1
    turned = pltpu.roll(rows, (-step) % size, axis)
    lane = lax.broadcasted_iota(jnp.int32, rows.shape, axis)
    edge = size - 1 if step > 0 else 0
    return jnp.where(lane == edge, 0.0, turned)


def weight_sums(vol_ref, grad_ref, before_ref, after_ref, sums_ref, gpad):
    peers, depth, rows, share, cols = vol_ref.shape
    outs = grad_ref.shape[2]
    chans = peers * share
    blank = jnp.zeros((3 * outs, cols), BF16)
    bias_sum = jnp.zeros((outs, cols), F32)
    for p in range(depth + 2):
        gpad[p, 0] = blank
        gpad[p, rows + 1] = blank
        for h in range(rows):
            if p == 0:
                line = before_ref[h, 0:outs]
            elif p == depth + 1:
                line = after_ref[h, 0:outs]
            else:
                line = grad_ref[p - 1, h]
            wide = line.astype(F32)
            if 0 < p < depth + 1:
                bias_sum = bias_sum + wide
            gpad[p, h + 1, 0:outs] = slide(wide, 1).astype(BF16)
            gpad[p, h + 1, outs : 2 * outs] = line
            gpad[p, h + 1, 2 * outs : 3 * outs] = slide(wide, -1).astype(BF16)
    acc = jnp.zeros((27 * outs, chans), F32)
    for d in range(depth):
        for h in range(0, rows, 2):
            cells = jnp.concatenate(
                [
                    jnp.concatenate([vol_ref[s, d, h + k] for s in range(peers)], axis=0)
                    for k in range(2)
                ],
                axis=1,
            )
            acc = acc + dot_lanes(moved_rows(gpad, d, h), cells)
    half = cols // 2
    bias_half = bias_sum[:, :half] + bias_sum[:, half:]
    for r in range(14):
        first = acc[2 * r * outs : (2 * r + 1) * outs]
        second = bias_half if r == 13 else acc[(2 * r + 1) * outs : (2 * r + 2) * outs]
        sums_ref[r] = jnp.concatenate([first, second], axis=1)
    for r in range(14, 16):
        sums_ref[r] = jnp.zeros((outs, cols), F32)


def moved_rows(gpad, d, h):
    return jnp.concatenate(
        [
            jnp.concatenate(
                [gpad[d + 2 - a, h + k + 2 - b] for a in range(3) for b in range(3)], axis=0
            )
            for k in range(2)
        ],
        axis=1,
    )


def split(value):
    high = value.astype(BF16)
    return high, (value - high.astype(F32)).astype(BF16)


def shares_first(
    me_ref, moved_ref, taps_ref, before_ref, after_ref, keep_ref, send_ref, turned
):
    _, depth, rows, share, cols = keep_ref.shape
    outs, chans = taps_ref.shape[1:]
    turned[...] = taps_ref[...].reshape(27 * outs, chans).astype(F32).T
    me = me_ref[0]
    behind = jnp.concatenate(
        [
            turned[pl.ds(pl.multiple_of(share * jnp.bitwise_xor(me, r), share), share)]
            for r in range(8)
        ],
        axis=0,
    ).astype(BF16)
    for d in range(depth):
        for h in range(0, rows, 2):
            back = dot(behind, moved_rows(moved_ref, d, h))
            for k in range(2):
                for r in range(8):
                    value = back[share * r : share * (r + 1), k * cols : (k + 1) * cols]
                    if r < 4:
                        keep_ref[r, d, h + k] = value
                    else:
                        high, low = split(value)
                        send_ref[2 * (r - 4), d, h + k] = high
                        send_ref[2 * (r - 4) + 1, d, h + k] = low
    for h in range(rows):
        send_ref[8, 0, h] = before_ref[h, outs : outs + share]
        send_ref[8, 1, h] = after_ref[h, outs : outs + share]


def shares_next(keep_ref, sent_ref, got_ref, kept_ref, send_ref):
    blocks = keep_ref.shape[0]
    half = blocks // 2
    for r in range(blocks):
        value = keep_ref[r] + got_ref[2 * r].astype(F32) + got_ref[2 * r + 1].astype(F32)
        if r < half:
            kept_ref[r] = value
        else:
            high, low = split(value)
            send_ref[2 * (r - half)] = high
            send_ref[2 * (r - half) + 1] = low
    place = 2 * half
    for ref in (sent_ref, got_ref):
        for n in range(2 * blocks, ref.shape[0]):
            send_ref[place] = ref[n]
            place += 1


def finish(
    me_ref, vol_ref, keep_ref, sent_ref, got_ref, taps_ref, bias_ref, out_ref, back_ref, halo, vpad
):
    peers, depth, rows, share, cols = vol_ref.shape
    taps = taps_ref[...]
    outs, chans = taps.shape[1:]
    me = me_ref[0]
    for place, r in enumerate((0, 4, 2, 6)):
        halo[jnp.bitwise_xor(me, r)] = sent_ref[2 + place]
        halo[jnp.bitwise_xor(me, r + 1)] = got_ref[2 + place]
    blank = jnp.zeros((chans, cols), BF16)
    for p in range(depth + 2):
        vpad[p, 0] = blank
        vpad[p, rows + 1] = blank
        for h in range(rows):
            if p == 0:
                lines = [halo[s, 0, h] for s in range(peers)]
            elif p == depth + 1:
                lines = [halo[s, 1, h] for s in range(peers)]
            else:
                lines = [vol_ref[s, p - 1, h] for s in range(peers)]
            vpad[p, h + 1] = jnp.concatenate(lines, axis=0)
    ahead = jnp.concatenate(
        [
            jnp.concatenate([taps[9 * a + 3 * b + c] for a in range(3) for b in range(3)], axis=1)
            for c in range(3)
        ],
        axis=0,
    )
    bias = jnp.broadcast_to(bias_ref[...], (outs, cols))
    for d in range(depth):
        lines = []
        for h in range(0, rows, 2):
            stack = jnp.concatenate(
                [
                    vpad[d : d + 3, h + k : h + k + 3].reshape(9 * chans, cols)
                    for k in range(2)
                ],
                axis=1,
            )
            part = dot(ahead, stack)
            for k in range(2):
                total = part[:, k * cols : (k + 1) * cols]
                lines.append(
                    total[outs : 2 * outs]
                    + slide(total[0:outs], -1)
                    + slide(total[2 * outs : 3 * outs], 1)
                    + bias
                )
        out_ref[:, d] = jnp.swapaxes(jnp.stack(lines), 0, 1).astype(BF16)
        total = keep_ref[0, d] + got_ref[0, d].astype(F32) + got_ref[1, d].astype(F32)
        back_ref[:, d] = jnp.swapaxes(total, 0, 1).astype(BF16)


def unpack(scale, every_ref, weight_ref, bias_ref):
    outs, cols = every_ref.shape[1:]
    half = cols // 2
    for t in range(27):
        r, side = t // 2, t % 2
        weight_ref[t] = every_ref[r, :, half * side : half * (side + 1)] * scale
    total = jnp.sum(every_ref[13, :, half:] * scale, axis=1, keepdims=True)
    wide = jnp.broadcast_to(total, (outs, cols))
    row = lax.broadcasted_iota(jnp.int32, (outs, cols), 0)
    lane = lax.broadcasted_iota(jnp.int32, (outs, cols), 1)
    flat = jnp.sum(jnp.where(row == lane, wide, 0.0), axis=0, keepdims=True)
    bias_ref[...] = flat[:, :outs]


XY_GROUPS = [[16 * z + k for k in range(16)] for z in range(4)]
Z_GROUPS = [[16 * z + k for z in range(4)] for k in range(16)]
EVEN = [(i, i ^ 1) for i in range(64)]
ODD = [(i, ((i + 1) ^ 1) - 1) for i in range(1, 63)]


def swap_edges(head, tail):
    odd = (lax.axis_index("space") % 2) == 1
    inner = lax.ppermute(jnp.where(odd, head, tail), "space", EVEN)
    outer = lax.ppermute(jnp.where(odd, tail, head), "space", ODD)
    return jnp.where(odd, inner, outer), jnp.where(odd, outer, inner)


def swap_pairs(bit):
    return [(f, f ^ bit) for f in range(8)]


def shares_step(blocks, block):
    return pl.pallas_call(
        shares_next,
        out_shape=(
            jax.ShapeDtypeStruct((blocks,) + block, F32),
            jax.ShapeDtypeStruct((6,) + block, BF16),
        ),
        in_specs=[WHOLE] * 3,
        out_specs=(WHOLE,) * 2,
        compiler_params=PARAMS,
    )


def local(volume, weight, bias, grad_out):
    share, depth, rows, cols = volume.shape
    outs = grad_out.shape[0]
    chans = weight.shape[1]
    taps = weight.transpose(0, 2, 1)
    grad = grad_out.transpose(1, 2, 0, 3)
    own = volume.transpose(1, 2, 0, 3)
    me = lax.axis_index("filt").astype(jnp.int32).reshape(1)
    both = jnp.concatenate([grad, own], axis=2)
    before, after = swap_edges(both[0], both[depth - 1])
    vol = lax.all_to_all(jnp.broadcast_to(own[None], (8,) + own.shape), "filt", 0, 0)
    block = (depth, rows, share, cols)
    sums, moved = pl.pallas_call(
        weight_sums,
        out_shape=(
            jax.ShapeDtypeStruct((16, outs, cols), F32),
            jax.ShapeDtypeStruct((depth + 2, rows + 2, 3 * outs, cols), BF16),
        ),
        in_specs=[WHOLE] * 4,
        out_specs=(WHOLE,) * 2,
        compiler_params=PARAMS,
    )(vol, grad, before, after)
    parts = lax.all_to_all(sums, "space", 0, 0, axis_index_groups=XY_GROUPS)
    keep, send = pl.pallas_call(
        shares_first,
        out_shape=(
            jax.ShapeDtypeStruct((4,) + block, F32),
            jax.ShapeDtypeStruct((9,) + block, BF16),
        ),
        in_specs=[pl.BlockSpec(memory_space=pltpu.SMEM)] + [WHOLE] * 4,
        out_specs=(WHOLE,) * 2,
        scratch_shapes=[pltpu.VMEM((chans, 27 * outs), F32)],
        compiler_params=PARAMS,
    )(me, moved, taps, before, after)
    got = lax.ppermute(send, "filt", swap_pairs(4))
    mine = jnp.sum(parts, axis=0)
    mine, got = lax.optimization_barrier((mine, got))
    keep, send = shares_step(2, block)(keep, send, got)
    got = lax.ppermute(send, "filt", swap_pairs(2))
    mine = lax.psum(mine, "space", axis_index_groups=Z_GROUPS)
    mine, got = lax.optimization_barrier((mine, got))
    keep, send = shares_step(1, block)(keep, send, got)
    got = lax.ppermute(send, "filt", swap_pairs(1))
    every = lax.all_to_all(
        jnp.broadcast_to(mine[None], (16,) + mine.shape), "space", 0, 0, axis_index_groups=XY_GROUPS
    )
    output, grad_volume = pl.pallas_call(
        finish,
        out_shape=(
            jax.ShapeDtypeStruct((outs, depth, rows, cols), BF16),
            jax.ShapeDtypeStruct((share, depth, rows, cols), BF16),
        ),
        in_specs=[pl.BlockSpec(memory_space=pltpu.SMEM)] + [WHOLE] * 6,
        out_specs=(WHOLE,) * 2,
        scratch_shapes=[
            pltpu.VMEM((8,) + block, BF16),
            pltpu.VMEM((depth + 2, rows + 2, chans, cols), BF16),
        ],
        compiler_params=PARAMS,
    )(me, vol, keep, send, got, taps, bias[:, None])
    every, output, grad_volume = lax.optimization_barrier((every, output, grad_volume))
    scale = 1.0 / math.sqrt(depth * lax.axis_size("space") * rows * cols)
    grad_taps, grad_bias = pl.pallas_call(
        lambda *refs: unpack(scale, *refs),
        out_shape=(
            jax.ShapeDtypeStruct((27, outs, cols // 2), F32),
            jax.ShapeDtypeStruct((1, outs), F32),
        ),
        in_specs=[WHOLE],
        out_specs=(WHOLE,) * 2,
        compiler_params=PARAMS,
    )(every)
    return (output, grad_volume, grad_taps.transpose(0, 2, 1), grad_bias.reshape(outs))


def solution(mesh):
    in_specs = (
        P("filt", "space", None, None),
        P(None, None, "filt"),
        P("filt"),
        P("filt", "space", None, None),
    )
    out_specs = (
        P("filt", "space", None, None),
        P("filt", "space", None, None),
        P(None, None, "filt"),
        P("filt"),
    )
    return jax.shard_map(local, mesh=mesh, in_specs=in_specs, out_specs=out_specs, check_vma=False)
```

```python
import math

import jax
import jax.numpy as jnp
from jax import lax
from jax.experimental import pallas as pl
from jax.experimental.pallas import tpu as pltpu
from jax.sharding import PartitionSpec as P

F32 = jnp.float32
BF16 = jnp.bfloat16
WHOLE = pl.BlockSpec(memory_space=pltpu.VMEM)
PARAMS = pltpu.CompilerParams(vmem_limit_bytes=40 * 1024 * 1024)


def dot(left, right):
    return lax.dot_general(left, right, (((1,), (0,)), ((), ())), preferred_element_type=F32)


def dot_lanes(left, right):
    return lax.dot_general(left, right, (((1,), (1,)), ((), ())), preferred_element_type=F32)


def slide(rows, step):
    size = rows.shape[-1]
    axis = rows.ndim - 1
    turned = pltpu.roll(rows, (-step) % size, axis)
    lane = lax.broadcasted_iota(jnp.int32, rows.shape, axis)
    edge = size - 1 if step > 0 else 0
    return jnp.where(lane == edge, 0.0, turned)


def weight_sums(vol_ref, grad_ref, before_ref, after_ref, sums_ref, gpad):
    peers, depth, rows, share, cols = vol_ref.shape
    outs = grad_ref.shape[2]
    chans = peers * share
    blank = jnp.zeros((3 * outs, cols), BF16)
    bias_sum = jnp.zeros((outs, cols), F32)
    for p in range(depth + 2):
        gpad[p, 0] = blank
        gpad[p, rows + 1] = blank
        for h in range(rows):
            if p == 0:
                line = before_ref[h, 0:outs]
            elif p == depth + 1:
                line = after_ref[h, 0:outs]
            else:
                line = grad_ref[p - 1, h]
            wide = line.astype(F32)
            if 0 < p < depth + 1:
                bias_sum = bias_sum + wide
            gpad[p, h + 1, 0:outs] = slide(wide, 1).astype(BF16)
            gpad[p, h + 1, outs : 2 * outs] = line
            gpad[p, h + 1, 2 * outs : 3 * outs] = slide(wide, -1).astype(BF16)
    acc = jnp.zeros((27 * outs, chans), F32)
    for d in range(depth):
        for h in range(0, rows, 2):
            cells = jnp.concatenate(
                [
                    jnp.concatenate([vol_ref[s, d, h + k] for s in range(peers)], axis=0)
                    for k in range(2)
                ],
                axis=1,
            )
            acc = acc + dot_lanes(moved_rows(gpad, d, h), cells)
    half = cols // 2
    bias_half = bias_sum[:, :half] + bias_sum[:, half:]
    for r in range(14):
        first = acc[2 * r * outs : (2 * r + 1) * outs]
        second = bias_half if r == 13 else acc[(2 * r + 1) * outs : (2 * r + 2) * outs]
        sums_ref[r, 0:outs] = jnp.concatenate([first, second], axis=1)
    for r in range(14, 16):
        sums_ref[r, 0:outs] = jnp.zeros((outs, cols), F32)


def moved_rows(gpad, d, h):
    return jnp.concatenate(
        [
            jnp.concatenate(
                [gpad[d + 2 - a, h + k + 2 - b] for a in range(3) for b in range(3)], axis=0
            )
            for k in range(2)
        ],
        axis=1,
    )


def split(value):
    high = value.astype(BF16)
    return high, (value - high.astype(F32)).astype(BF16)


def shares_first(
    me_ref, moved_ref, taps_ref, before_ref, after_ref, keep_ref, send_ref, turned
):
    _, depth, rows, share, cols = keep_ref.shape
    outs, chans = taps_ref.shape[1:]
    turned[...] = taps_ref[...].reshape(27 * outs, chans).astype(F32).T
    me = me_ref[0]
    behind = jnp.concatenate(
        [
            turned[pl.ds(pl.multiple_of(share * jnp.bitwise_xor(me, r), share), share)]
            for r in range(8)
        ],
        axis=0,
    ).astype(BF16)
    for d in range(depth):
        for h in range(0, rows, 2):
            back = dot(behind, moved_rows(moved_ref, d, h))
            for k in range(2):
                for r in range(8):
                    value = back[share * r : share * (r + 1), k * cols : (k + 1) * cols]
                    if r < 4:
                        keep_ref[r, d, h + k] = value
                    else:
                        high, low = split(value)
                        send_ref[2 * (r - 4), d, h + k] = high
                        send_ref[2 * (r - 4) + 1, d, h + k] = low
    for h in range(rows):
        send_ref[8, 0, h] = before_ref[h, outs : outs + share]
        send_ref[8, 1, h] = after_ref[h, outs : outs + share]


def shares_next(keep_ref, sent_ref, got_ref, kept_ref, send_ref):
    blocks = keep_ref.shape[0]
    half = blocks // 2
    for r in range(blocks):
        value = keep_ref[r] + got_ref[2 * r].astype(F32) + got_ref[2 * r + 1].astype(F32)
        if r < half:
            kept_ref[r] = value
        else:
            high, low = split(value)
            send_ref[2 * (r - half)] = high
            send_ref[2 * (r - half) + 1] = low
    place = 2 * half
    for ref in (sent_ref, got_ref):
        for n in range(2 * blocks, ref.shape[0]):
            send_ref[place] = ref[n]
            place += 1


def finish(
    me_ref, vol_ref, keep_ref, sent_ref, got_ref, taps_ref, bias_ref, out_ref, back_ref, halo, vpad
):
    peers, depth, rows, share, cols = vol_ref.shape
    taps = taps_ref[...]
    outs, chans = taps.shape[1:]
    me = me_ref[0]
    for place, r in enumerate((0, 4, 2, 6)):
        halo[jnp.bitwise_xor(me, r)] = sent_ref[2 + place]
        halo[jnp.bitwise_xor(me, r + 1)] = got_ref[2 + place]
    blank = jnp.zeros((chans, cols), BF16)
    for p in range(depth + 2):
        vpad[p, 0] = blank
        vpad[p, rows + 1] = blank
        for h in range(rows):
            if p == 0:
                lines = [halo[s, 0, h] for s in range(peers)]
            elif p == depth + 1:
                lines = [halo[s, 1, h] for s in range(peers)]
            else:
                lines = [vol_ref[s, p - 1, h] for s in range(peers)]
            vpad[p, h + 1] = jnp.concatenate(lines, axis=0)
    ahead = jnp.concatenate(
        [
            jnp.concatenate([taps[9 * a + 3 * b + c] for a in range(3) for b in range(3)], axis=1)
            for c in range(3)
        ],
        axis=0,
    )
    bias = jnp.broadcast_to(bias_ref[...], (outs, cols))
    for d in range(depth):
        lines = []
        for h in range(0, rows, 2):
            stack = jnp.concatenate(
                [
                    vpad[d : d + 3, h + k : h + k + 3].reshape(9 * chans, cols)
                    for k in range(2)
                ],
                axis=1,
            )
            part = dot(ahead, stack)
            for k in range(2):
                total = part[:, k * cols : (k + 1) * cols]
                lines.append(
                    total[outs : 2 * outs]
                    + slide(total[0:outs], -1)
                    + slide(total[2 * outs : 3 * outs], 1)
                    + bias
                )
        out_ref[:, d] = jnp.swapaxes(jnp.stack(lines), 0, 1).astype(BF16)
        total = keep_ref[0, d] + got_ref[0, d].astype(F32) + got_ref[1, d].astype(F32)
        back_ref[:, d] = jnp.swapaxes(total, 0, 1).astype(BF16)


def unpack(scale, every_ref, weight_ref, bias_ref):
    outs, cols = every_ref.shape[2:]
    half = cols // 2
    for t in range(27):
        r, side = t // 2, t % 2
        weight_ref[t] = every_ref[r, 0, :, half * side : half * (side + 1)] * scale
    total = jnp.sum(every_ref[13, 0, :, half:] * scale, axis=1, keepdims=True)
    wide = jnp.broadcast_to(total, (outs, cols))
    row = lax.broadcasted_iota(jnp.int32, (outs, cols), 0)
    lane = lax.broadcasted_iota(jnp.int32, (outs, cols), 1)
    flat = jnp.sum(jnp.where(row == lane, wide, 0.0), axis=0, keepdims=True)
    bias_ref[...] = flat[:, :outs]


XY_GROUPS = [[16 * z + k for k in range(16)] for z in range(4)]
Z_GROUPS = [[16 * z + k for z in range(4)] for k in range(16)]
EVEN = [(i, i ^ 1) for i in range(64)]
ODD = [(i, ((i + 1) ^ 1) - 1) for i in range(1, 63)]


def swap_edges(head, tail):
    odd = (lax.axis_index("space") % 2) == 1
    inner = lax.ppermute(jnp.where(odd, head, tail), "space", EVEN)
    outer = lax.ppermute(jnp.where(odd, tail, head), "space", ODD)
    return jnp.where(odd, inner, outer), jnp.where(odd, outer, inner)


def swap_pairs(bit):
    return [(f, f ^ bit) for f in range(8)]


def shares_step(blocks, block):
    return pl.pallas_call(
        shares_next,
        out_shape=(
            jax.ShapeDtypeStruct((blocks,) + block, F32),
            jax.ShapeDtypeStruct((6,) + block, BF16),
        ),
        in_specs=[WHOLE] * 3,
        out_specs=(WHOLE,) * 2,
        compiler_params=PARAMS,
    )


def local(volume, weight, bias, grad_out):
    share, depth, rows, cols = volume.shape
    outs = grad_out.shape[0]
    chans = weight.shape[1]
    taps = weight.transpose(0, 2, 1)
    grad = grad_out.transpose(1, 2, 0, 3)
    own = volume.transpose(1, 2, 0, 3)
    me = lax.axis_index("filt").astype(jnp.int32).reshape(1)
    both = jnp.concatenate([grad, own], axis=2)
    before, after = swap_edges(both[0], both[depth - 1])
    vol = lax.all_to_all(jnp.broadcast_to(own[None], (8,) + own.shape), "filt", 0, 0)
    block = (depth, rows, share, cols)
    sums, moved = pl.pallas_call(
        weight_sums,
        out_shape=(
            jax.ShapeDtypeStruct((16, 3 * outs, cols), F32),
            jax.ShapeDtypeStruct((depth + 2, rows + 2, 3 * outs, cols), BF16),
        ),
        in_specs=[WHOLE] * 4,
        out_specs=(WHOLE,) * 2,
        compiler_params=PARAMS,
    )(vol, grad, before, after)
    parts = lax.all_to_all(sums, "space", 0, 0, axis_index_groups=XY_GROUPS)
    keep, send = pl.pallas_call(
        shares_first,
        out_shape=(
            jax.ShapeDtypeStruct((4,) + block, F32),
            jax.ShapeDtypeStruct((9,) + block, BF16),
        ),
        in_specs=[pl.BlockSpec(memory_space=pltpu.SMEM)] + [WHOLE] * 4,
        out_specs=(WHOLE,) * 2,
        scratch_shapes=[pltpu.VMEM((chans, 27 * outs), F32)],
        compiler_params=PARAMS,
    )(me, moved, taps, before, after)
    got = lax.ppermute(send, "filt", swap_pairs(4))
    mine = jnp.sum(parts[:, :outs], axis=0)
    mine, got = lax.optimization_barrier((mine, got))
    keep, send = shares_step(2, block)(keep, send, got)
    got = lax.ppermute(send, "filt", swap_pairs(2))
    mine = lax.psum(mine, "space", axis_index_groups=Z_GROUPS)
    mine, got = lax.optimization_barrier((mine, got))
    keep, send = shares_step(1, block)(keep, send, got)
    got = lax.ppermute(send, "filt", swap_pairs(1))
    every = lax.all_to_all(
        jnp.broadcast_to(mine[None, None], (16, 3) + mine.shape), "space", 0, 0, axis_index_groups=XY_GROUPS
    )
    output, grad_volume = pl.pallas_call(
        finish,
        out_shape=(
            jax.ShapeDtypeStruct((outs, depth, rows, cols), BF16),
            jax.ShapeDtypeStruct((share, depth, rows, cols), BF16),
        ),
        in_specs=[pl.BlockSpec(memory_space=pltpu.SMEM)] + [WHOLE] * 6,
        out_specs=(WHOLE,) * 2,
        scratch_shapes=[
            pltpu.VMEM((8,) + block, BF16),
            pltpu.VMEM((depth + 2, rows + 2, chans, cols), BF16),
        ],
        compiler_params=PARAMS,
    )(me, vol, keep, send, got, taps, bias[:, None])
    every, output, grad_volume = lax.optimization_barrier((every, output, grad_volume))
    scale = 1.0 / math.sqrt(depth * lax.axis_size("space") * rows * cols)
    grad_taps, grad_bias = pl.pallas_call(
        lambda *refs: unpack(scale, *refs),
        out_shape=(
            jax.ShapeDtypeStruct((27, outs, cols // 2), F32),
            jax.ShapeDtypeStruct((1, outs), F32),
        ),
        in_specs=[WHOLE],
        out_specs=(WHOLE,) * 2,
        compiler_params=PARAMS,
    )(every)
    return (output, grad_volume, grad_taps.transpose(0, 2, 1), grad_bias.reshape(outs))


def solution(mesh):
    in_specs = (
        P("filt", "space", None, None),
        P(None, None, "filt"),
        P("filt"),
        P("filt", "space", None, None),
    )
    out_specs = (
        P("filt", "space", None, None),
        P("filt", "space", None, None),
        P(None, None, "filt"),
        P("filt"),
    )
    return jax.shard_map(local, mesh=mesh, in_specs=in_specs, out_specs=out_specs, check_vma=False)
```

```python
import math

import jax
import jax.numpy as jnp
from jax import lax
from jax.experimental import pallas as pl
from jax.experimental.pallas import tpu as pltpu
from jax.sharding import PartitionSpec as P

F32 = jnp.float32
BF16 = jnp.bfloat16
WHOLE = pl.BlockSpec(memory_space=pltpu.VMEM)
SCALAR = pl.BlockSpec(memory_space=pltpu.SMEM)
PARAMS = pltpu.CompilerParams(vmem_limit_bytes=40 * 1024 * 1024)


def dot(left, right):
    return lax.dot_general(left, right, (((1,), (0,)), ((), ())), preferred_element_type=F32)


def dot_lanes(left, right):
    return lax.dot_general(left, right, (((1,), (1,)), ((), ())), preferred_element_type=F32)


def slide(rows, step):
    size = rows.shape[-1]
    axis = rows.ndim - 1
    turned = pltpu.roll(rows, (-step) % size, axis)
    lane = lax.broadcasted_iota(jnp.int32, rows.shape, axis)
    edge = size - 1 if step > 0 else 0
    return jnp.where(lane == edge, 0.0, turned)


def weight_sums(odd_ref, vol_ref, grad_ref, outer_ref, inner_ref, sums_ref, gpad):
    peers, depth, rows, share, cols = vol_ref.shape
    outs = grad_ref.shape[0]
    chans = peers * share
    odd = odd_ref[0] == 1
    inner = inner_ref[0:outs].astype(F32)
    outer = outer_ref[0:outs].astype(F32)
    planes = [
        jnp.where(odd, inner, outer),
        *[grad_ref[:, d].astype(F32) for d in range(depth)],
        jnp.where(odd, outer, inner),
    ]
    blank = jnp.zeros((3 * outs, cols), BF16)
    bias_sum = jnp.zeros((outs, cols), F32)
    for p in range(depth + 2):
        gpad[p, 0] = blank
        gpad[p, rows + 1] = blank
        plane = jnp.swapaxes(planes[p], 0, 1)
        for h in range(rows):
            wide = plane[h]
            if 0 < p < depth + 1:
                bias_sum = bias_sum + wide
            gpad[p, h + 1, 0:outs] = slide(wide, 1).astype(BF16)
            gpad[p, h + 1, outs : 2 * outs] = wide.astype(BF16)
            gpad[p, h + 1, 2 * outs : 3 * outs] = slide(wide, -1).astype(BF16)
    acc = jnp.zeros((27 * outs, chans), F32)
    for d in range(depth):
        for h in range(0, rows, 2):
            cells = jnp.concatenate(
                [
                    jnp.concatenate([vol_ref[s, d, h + k] for s in range(peers)], axis=0)
                    for k in range(2)
                ],
                axis=1,
            )
            acc = acc + dot_lanes(moved_rows(gpad, d, h), cells)
    half = cols // 2
    bias_half = bias_sum[:, :half] + bias_sum[:, half:]
    for r in range(14):
        first = acc[2 * r * outs : (2 * r + 1) * outs]
        second = bias_half if r == 13 else acc[(2 * r + 1) * outs : (2 * r + 2) * outs]
        sums_ref[r] = jnp.concatenate([first, second], axis=1)
    for r in range(14, 16):
        sums_ref[r] = jnp.zeros((outs, cols), F32)


def moved_rows(gpad, d, h):
    return jnp.concatenate(
        [
            jnp.concatenate(
                [gpad[d + 2 - a, h + k + 2 - b] for a in range(3) for b in range(3)], axis=0
            )
            for k in range(2)
        ],
        axis=1,
    )


def split(value):
    high = value.astype(BF16)
    return high, (value - high.astype(F32)).astype(BF16)


def shares_first(
    odd_ref, me_ref, moved_ref, taps_ref, outer_ref, inner_ref, keep_ref, send_ref, turned
):
    _, depth, rows, share, cols = keep_ref.shape
    outs, chans = taps_ref.shape[1:]
    turned[...] = taps_ref[...].reshape(27 * outs, chans).astype(F32).T
    me = me_ref[0]
    behind = jnp.concatenate(
        [
            turned[pl.ds(pl.multiple_of(share * jnp.bitwise_xor(me, r), share), share)]
            for r in ORDER
        ],
        axis=0,
    ).astype(BF16)
    for d in range(depth):
        for h in range(0, rows, 2):
            back = dot(behind, moved_rows(moved_ref, d, h))
            for k in range(2):
                for r in range(8):
                    value = back[share * r : share * (r + 1), k * cols : (k + 1) * cols]
                    if r < 4:
                        keep_ref[r, d, h + k] = value
                    else:
                        high, low = split(value)
                        send_ref[2 * (r - 4), d, h + k] = high
                        send_ref[2 * (r - 4) + 1, d, h + k] = low
    odd = odd_ref[0] == 1
    inner = inner_ref[outs : outs + share].astype(F32)
    outer = outer_ref[outs : outs + share].astype(F32)
    send_ref[8, 0] = jnp.swapaxes(jnp.where(odd, inner, outer), 0, 1).astype(BF16)
    send_ref[8, 1] = jnp.swapaxes(jnp.where(odd, outer, inner), 0, 1).astype(BF16)


def shares_next(keep_ref, sent_ref, got_ref, kept_ref, send_ref):
    blocks = keep_ref.shape[0]
    half = blocks // 2
    for r in range(blocks):
        value = keep_ref[r] + got_ref[2 * r].astype(F32) + got_ref[2 * r + 1].astype(F32)
        if r < half:
            kept_ref[r] = value
        else:
            high, low = split(value)
            send_ref[2 * (r - half)] = high
            send_ref[2 * (r - half) + 1] = low
    place = 2 * half
    for ref in (sent_ref, got_ref):
        for n in range(2 * blocks, ref.shape[0]):
            send_ref[place] = ref[n]
            place += 1


def shares_last(keep_ref, sent_ref, got_ref, mine_ref, kept_ref, send_ref, spread_ref):
    shares_next(keep_ref, sent_ref, got_ref, kept_ref, send_ref)
    for k in range(spread_ref.shape[0]):
        spread_ref[k] = mine_ref[...]


def finish(
    me_ref, vol_ref, keep_ref, sent_ref, got_ref, taps_ref, bias_ref, out_ref, back_ref, halo, vpad
):
    peers, depth, rows, share, cols = vol_ref.shape
    taps = taps_ref[...]
    outs, chans = taps.shape[1:]
    me = me_ref[0]
    first, second, third = SWAPS
    for place, r in enumerate((0, first, second, first ^ second)):
        halo[jnp.bitwise_xor(me, r)] = sent_ref[2 + place]
        halo[jnp.bitwise_xor(me, r ^ third)] = got_ref[2 + place]
    blank = jnp.zeros((chans, cols), BF16)
    for p in range(depth + 2):
        vpad[p, 0] = blank
        vpad[p, rows + 1] = blank
        for h in range(rows):
            if p == 0:
                lines = [halo[s, 0, h] for s in range(peers)]
            elif p == depth + 1:
                lines = [halo[s, 1, h] for s in range(peers)]
            else:
                lines = [vol_ref[s, p - 1, h] for s in range(peers)]
            vpad[p, h + 1] = jnp.concatenate(lines, axis=0)
    ahead = jnp.concatenate(
        [
            jnp.concatenate([taps[9 * a + 3 * b + c] for a in range(3) for b in range(3)], axis=1)
            for c in range(3)
        ],
        axis=0,
    )
    bias = jnp.broadcast_to(bias_ref[...], (outs, cols))
    for d in range(depth):
        lines = []
        for h in range(0, rows, 2):
            stack = jnp.concatenate(
                [
                    vpad[d : d + 3, h + k : h + k + 3].reshape(9 * chans, cols)
                    for k in range(2)
                ],
                axis=1,
            )
            part = dot(ahead, stack)
            for k in range(2):
                total = part[:, k * cols : (k + 1) * cols]
                lines.append(
                    total[outs : 2 * outs]
                    + slide(total[0:outs], -1)
                    + slide(total[2 * outs : 3 * outs], 1)
                    + bias
                )
        out_ref[:, d] = jnp.swapaxes(jnp.stack(lines), 0, 1).astype(BF16)
        total = keep_ref[0, d] + got_ref[0, d].astype(F32) + got_ref[1, d].astype(F32)
        back_ref[:, d] = jnp.swapaxes(total, 0, 1).astype(BF16)


def unpack(scale, every_ref, weight_ref, bias_ref):
    outs, cols = every_ref.shape[1:]
    half = cols // 2
    for t in range(27):
        r, side = t // 2, t % 2
        weight_ref[t] = every_ref[r, :, half * side : half * (side + 1)] * scale
    total = jnp.sum(every_ref[13, :, half:] * scale, axis=1, keepdims=True)
    wide = jnp.broadcast_to(total, (outs, cols))
    row = lax.broadcasted_iota(jnp.int32, (outs, cols), 0)
    lane = lax.broadcasted_iota(jnp.int32, (outs, cols), 1)
    flat = jnp.sum(jnp.where(row == lane, wide, 0.0), axis=0, keepdims=True)
    bias_ref[...] = flat[:, :outs]


SWAPS = (2, 1, 4)
ORDER = [sum(bit for k, bit in enumerate(SWAPS) if n & (4 >> k)) for n in range(8)]
XY_GROUPS = [[16 * z + k for k in range(16)] for z in range(4)]
Z_GROUPS = [[16 * z + k for z in range(4)] for k in range(16)]
EVEN = [(i, i ^ 1) for i in range(64)]
ODD = [(i, ((i + 1) ^ 1) - 1) for i in range(1, 63)]


def swap_edges(odd, head, tail):
    inner = lax.ppermute(jnp.where(odd, head, tail), "space", EVEN)
    outer = lax.ppermute(jnp.where(odd, tail, head), "space", ODD)
    return inner, outer


def swap_pairs(bit):
    return [(f, f ^ bit) for f in range(8)]


def local(volume, weight, bias, grad_out):
    share, depth, rows, cols = volume.shape
    outs = grad_out.shape[0]
    chans = weight.shape[1]
    taps = weight.transpose(0, 2, 1)
    own = volume.transpose(1, 2, 0, 3)
    odd = jnp.bitwise_and(lax.axis_index("space").astype(jnp.int32), 1)
    me = lax.axis_index("filt").astype(jnp.int32).reshape(1)
    head, tail = (
        jnp.concatenate([grad_out[:, d], volume[:, d]], axis=0) for d in (0, depth - 1)
    )
    inner, outer = swap_edges(odd == 1, head, tail)
    odd = odd.reshape(1)
    vol = lax.all_to_all(jnp.broadcast_to(own[None], (8,) + own.shape), "filt", 0, 0)
    block = (depth, rows, share, cols)
    sums, moved = pl.pallas_call(
        weight_sums,
        out_shape=(
            jax.ShapeDtypeStruct((16, outs, cols), F32),
            jax.ShapeDtypeStruct((depth + 2, rows + 2, 3 * outs, cols), BF16),
        ),
        in_specs=[SCALAR] + [WHOLE] * 4,
        out_specs=(WHOLE,) * 2,
        compiler_params=PARAMS,
    )(odd, vol, grad_out, outer, inner)
    parts = lax.all_to_all(sums, "space", 0, 0, axis_index_groups=XY_GROUPS)
    keep, send = pl.pallas_call(
        shares_first,
        out_shape=(
            jax.ShapeDtypeStruct((4,) + block, F32),
            jax.ShapeDtypeStruct((9,) + block, BF16),
        ),
        in_specs=[SCALAR] * 2 + [WHOLE] * 4,
        out_specs=(WHOLE,) * 2,
        scratch_shapes=[pltpu.VMEM((chans, 27 * outs), F32)],
        compiler_params=PARAMS,
    )(odd, me, moved, taps, outer, inner)
    got = lax.ppermute(send, "filt", swap_pairs(SWAPS[0]))
    mine = jnp.sum(parts, axis=0)
    mine, got = lax.optimization_barrier((mine, got))
    keep, send = pl.pallas_call(
        shares_next,
        out_shape=(
            jax.ShapeDtypeStruct((2,) + block, F32),
            jax.ShapeDtypeStruct((6,) + block, BF16),
        ),
        in_specs=[WHOLE] * 3,
        out_specs=(WHOLE,) * 2,
        compiler_params=PARAMS,
    )(keep, send, got)
    got = lax.ppermute(send, "filt", swap_pairs(SWAPS[1]))
    mine = lax.psum(mine, "space", axis_index_groups=Z_GROUPS)
    mine, got = lax.optimization_barrier((mine, got))
    keep, send, spread = pl.pallas_call(
        shares_last,
        out_shape=(
            jax.ShapeDtypeStruct((1,) + block, F32),
            jax.ShapeDtypeStruct((6,) + block, BF16),
            jax.ShapeDtypeStruct((16, outs, cols), F32),
        ),
        in_specs=[WHOLE] * 4,
        out_specs=(WHOLE,) * 3,
        compiler_params=PARAMS,
    )(keep, send, got, mine)
    got = lax.ppermute(send, "filt", swap_pairs(SWAPS[2]))
    every = lax.all_to_all(spread, "space", 0, 0, axis_index_groups=XY_GROUPS)
    output, grad_volume = pl.pallas_call(
        finish,
        out_shape=(
            jax.ShapeDtypeStruct((outs, depth, rows, cols), BF16),
            jax.ShapeDtypeStruct((share, depth, rows, cols), BF16),
        ),
        in_specs=[SCALAR] + [WHOLE] * 6,
        out_specs=(WHOLE,) * 2,
        scratch_shapes=[
            pltpu.VMEM((8,) + block, BF16),
            pltpu.VMEM((depth + 2, rows + 2, chans, cols), BF16),
        ],
        compiler_params=PARAMS,
    )(me, vol, keep, send, got, taps, bias[:, None])
    every, output, grad_volume = lax.optimization_barrier((every, output, grad_volume))
    scale = 1.0 / math.sqrt(depth * lax.axis_size("space") * rows * cols)
    grad_taps, grad_bias = pl.pallas_call(
        lambda *refs: unpack(scale, *refs),
        out_shape=(
            jax.ShapeDtypeStruct((27, outs, cols // 2), F32),
            jax.ShapeDtypeStruct((1, outs), F32),
        ),
        in_specs=[WHOLE],
        out_specs=(WHOLE,) * 2,
        compiler_params=PARAMS,
    )(every)
    return (output, grad_volume, grad_taps.transpose(0, 2, 1), grad_bias.reshape(outs))


def solution(mesh):
    in_specs = (
        P("filt", "space", None, None),
        P(None, None, "filt"),
        P("filt"),
        P("filt", "space", None, None),
    )
    out_specs = (
        P("filt", "space", None, None),
        P("filt", "space", None, None),
        P(None, None, "filt"),
        P("filt"),
    )
    return jax.shard_map(local, mesh=mesh, in_specs=in_specs, out_specs=out_specs, check_vma=False)
```

```python
import math

import jax
import jax.numpy as jnp
from jax import lax
from jax.experimental import pallas as pl
from jax.experimental.pallas import tpu as pltpu
from jax.sharding import PartitionSpec as P

F32 = jnp.float32
BF16 = jnp.bfloat16
WHOLE = pl.BlockSpec(memory_space=pltpu.VMEM)
SCALAR = pl.BlockSpec(memory_space=pltpu.SMEM)
PARAMS = pltpu.CompilerParams(vmem_limit_bytes=40 * 1024 * 1024)


def dot(left, right):
    return lax.dot_general(left, right, (((1,), (0,)), ((), ())), preferred_element_type=F32)


def dot_lanes(left, right):
    return lax.dot_general(left, right, (((1,), (1,)), ((), ())), preferred_element_type=F32)


def slide(rows, step):
    size = rows.shape[-1]
    axis = rows.ndim - 1
    turned = pltpu.roll(rows, (-step) % size, axis)
    lane = lax.broadcasted_iota(jnp.int32, rows.shape, axis)
    edge = size - 1 if step > 0 else 0
    return jnp.where(lane == edge, 0.0, turned)


def shifted(plane, target):
    outs, rows, cols = plane.shape
    blank = jnp.zeros((3 * outs, cols), BF16)
    target[0] = blank
    target[rows + 1] = blank
    turned = jnp.swapaxes(plane, 0, 1)
    for h in range(rows):
        wide = turned[h]
        target[h + 1, 0:outs] = slide(wide, 1).astype(BF16)
        target[h + 1, outs : 2 * outs] = wide.astype(BF16)
        target[h + 1, 2 * outs : 3 * outs] = slide(wide, -1).astype(BF16)


def ready_planes(grad_ref, outer_ref, planes_ref, bias_ref):
    outs, depth, rows, cols = grad_ref.shape
    total = None
    for d in range(depth):
        plane = grad_ref[:, d].astype(F32)
        shifted(plane, planes_ref.at[d])
        part = jnp.sum(plane, axis=1)
        total = part if total is None else total + part
    shifted(outer_ref[0:outs].astype(F32), planes_ref.at[depth])
    half = cols // 2
    bias_ref[...] = total[:, :half] + total[:, half:]


def weight_sums(odd_ref, vol_ref, planes_ref, bias_ref, inner_ref, sums_ref, gpad):
    peers, depth, rows, share, cols = vol_ref.shape
    outs = bias_ref.shape[0]
    chans = peers * share
    odd = odd_ref[0]
    for d in range(depth):
        gpad[d + 1] = planes_ref[d]
    gpad[(depth + 1) * odd] = planes_ref[depth]
    shifted(inner_ref[0:outs].astype(F32), gpad.at[(depth + 1) * (1 - odd)])
    acc = jnp.zeros((27 * outs, chans), F32)
    for d in range(depth):
        for h in range(0, rows, 2):
            cells = jnp.concatenate(
                [
                    jnp.concatenate([vol_ref[s, d, h + k] for s in range(peers)], axis=0)
                    for k in range(2)
                ],
                axis=1,
            )
            acc = acc + dot_lanes(moved_rows(gpad, d, h), cells)
    for r in range(14):
        first = acc[2 * r * outs : (2 * r + 1) * outs]
        second = bias_ref[...] if r == 13 else acc[(2 * r + 1) * outs : (2 * r + 2) * outs]
        sums_ref[r] = jnp.concatenate([first, second], axis=1)
    for r in range(14, 16):
        sums_ref[r] = jnp.zeros((outs, cols), F32)


def moved_rows(gpad, d, h):
    return jnp.concatenate(
        [
            jnp.concatenate(
                [gpad[d + 2 - a, h + k + 2 - b] for a in range(3) for b in range(3)], axis=0
            )
            for k in range(2)
        ],
        axis=1,
    )


def split(value):
    high = value.astype(BF16)
    return high, (value - high.astype(F32)).astype(BF16)


def shares_first(
    odd_ref, me_ref, moved_ref, taps_ref, outer_ref, inner_ref, keep_ref, send_ref, turned
):
    _, depth, rows, share, cols = keep_ref.shape
    outs, chans = taps_ref.shape[1:]
    turned[...] = taps_ref[...].reshape(27 * outs, chans).astype(F32).T
    me = me_ref[0]
    behind = jnp.concatenate(
        [
            turned[pl.ds(pl.multiple_of(share * jnp.bitwise_xor(me, r), share), share)]
            for r in ORDER
        ],
        axis=0,
    ).astype(BF16)
    for d in range(depth):
        for h in range(0, rows, 2):
            back = dot(behind, moved_rows(moved_ref, d, h))
            for k in range(2):
                for r in range(8):
                    value = back[share * r : share * (r + 1), k * cols : (k + 1) * cols]
                    if r < 4:
                        keep_ref[r, d, h + k] = value
                    else:
                        high, low = split(value)
                        send_ref[2 * (r - 4), d, h + k] = high
                        send_ref[2 * (r - 4) + 1, d, h + k] = low
    odd = odd_ref[0] == 1
    inner = inner_ref[outs : outs + share].astype(F32)
    outer = outer_ref[outs : outs + share].astype(F32)
    send_ref[8, 0] = jnp.swapaxes(jnp.where(odd, inner, outer), 0, 1).astype(BF16)
    send_ref[8, 1] = jnp.swapaxes(jnp.where(odd, outer, inner), 0, 1).astype(BF16)


def shares_next(keep_ref, sent_ref, got_ref, kept_ref, send_ref):
    blocks = keep_ref.shape[0]
    half = blocks // 2
    for r in range(blocks):
        value = keep_ref[r] + got_ref[2 * r].astype(F32) + got_ref[2 * r + 1].astype(F32)
        if r < half:
            kept_ref[r] = value
        else:
            high, low = split(value)
            send_ref[2 * (r - half)] = high
            send_ref[2 * (r - half) + 1] = low
    place = 2 * half
    for ref in (sent_ref, got_ref):
        for n in range(2 * blocks, ref.shape[0]):
            send_ref[place] = ref[n]
            place += 1


def shares_last(keep_ref, sent_ref, got_ref, mine_ref, kept_ref, send_ref, spread_ref):
    shares_next(keep_ref, sent_ref, got_ref, kept_ref, send_ref)
    for k in range(spread_ref.shape[0]):
        spread_ref[k] = mine_ref[...]


def finish(
    me_ref, vol_ref, keep_ref, sent_ref, got_ref, taps_ref, bias_ref, out_ref, back_ref, halo, vpad
):
    peers, depth, rows, share, cols = vol_ref.shape
    taps = taps_ref[...]
    outs, chans = taps.shape[1:]
    me = me_ref[0]
    first, second, third = SWAPS
    for place, r in enumerate((0, first, second, first ^ second)):
        halo[jnp.bitwise_xor(me, r)] = sent_ref[2 + place]
        halo[jnp.bitwise_xor(me, r ^ third)] = got_ref[2 + place]
    blank = jnp.zeros((chans, cols), BF16)
    for p in range(depth + 2):
        vpad[p, 0] = blank
        vpad[p, rows + 1] = blank
        for h in range(rows):
            if p == 0:
                lines = [halo[s, 0, h] for s in range(peers)]
            elif p == depth + 1:
                lines = [halo[s, 1, h] for s in range(peers)]
            else:
                lines = [vol_ref[s, p - 1, h] for s in range(peers)]
            vpad[p, h + 1] = jnp.concatenate(lines, axis=0)
    ahead = jnp.concatenate(
        [
            jnp.concatenate([taps[9 * a + 3 * b + c] for a in range(3) for b in range(3)], axis=1)
            for c in range(3)
        ],
        axis=0,
    )
    bias = jnp.broadcast_to(bias_ref[...], (outs, cols))
    for d in range(depth):
        lines = []
        for h in range(0, rows, 2):
            stack = jnp.concatenate(
                [
                    vpad[d : d + 3, h + k : h + k + 3].reshape(9 * chans, cols)
                    for k in range(2)
                ],
                axis=1,
            )
            part = dot(ahead, stack)
            for k in range(2):
                total = part[:, k * cols : (k + 1) * cols]
                lines.append(
                    total[outs : 2 * outs]
                    + slide(total[0:outs], -1)
                    + slide(total[2 * outs : 3 * outs], 1)
                    + bias
                )
        out_ref[:, d] = jnp.swapaxes(jnp.stack(lines), 0, 1).astype(BF16)
        total = keep_ref[0, d] + got_ref[0, d].astype(F32) + got_ref[1, d].astype(F32)
        back_ref[:, d] = jnp.swapaxes(total, 0, 1).astype(BF16)


def unpack(scale, every_ref, weight_ref, bias_ref):
    outs, cols = every_ref.shape[1:]
    half = cols // 2
    for t in range(27):
        r, side = t // 2, t % 2
        weight_ref[t] = every_ref[r, :, half * side : half * (side + 1)] * scale
    total = jnp.sum(every_ref[13, :, half:] * scale, axis=1, keepdims=True)
    wide = jnp.broadcast_to(total, (outs, cols))
    row = lax.broadcasted_iota(jnp.int32, (outs, cols), 0)
    lane = lax.broadcasted_iota(jnp.int32, (outs, cols), 1)
    flat = jnp.sum(jnp.where(row == lane, wide, 0.0), axis=0, keepdims=True)
    bias_ref[...] = flat[:, :outs]


SWAPS = (2, 1, 4)
ORDER = [sum(bit for k, bit in enumerate(SWAPS) if n & (4 >> k)) for n in range(8)]
XY_GROUPS = [[16 * z + k for k in range(16)] for z in range(4)]
Z_GROUPS = [[16 * z + k for z in range(4)] for k in range(16)]
EVEN = [(i, i ^ 1) for i in range(64)]
ODD = [(i, ((i + 1) ^ 1) - 1) for i in range(1, 63)]


def swap_edges(odd, head, tail):
    inner = lax.ppermute(jnp.where(odd, head, tail), "space", EVEN)
    outer = lax.ppermute(jnp.where(odd, tail, head), "space", ODD)
    return inner, outer


def swap_pairs(bit):
    return [(f, f ^ bit) for f in range(8)]


def local(volume, weight, bias, grad_out):
    share, depth, rows, cols = volume.shape
    outs = grad_out.shape[0]
    chans = weight.shape[1]
    taps = weight.transpose(0, 2, 1)
    own = volume.transpose(1, 2, 0, 3)
    odd = jnp.bitwise_and(lax.axis_index("space").astype(jnp.int32), 1)
    me = lax.axis_index("filt").astype(jnp.int32).reshape(1)
    head, tail = (
        jnp.concatenate([grad_out[:, d], volume[:, d]], axis=0) for d in (0, depth - 1)
    )
    inner, outer = swap_edges(odd == 1, head, tail)
    odd = odd.reshape(1)
    vol = lax.all_to_all(jnp.broadcast_to(own[None], (8,) + own.shape), "filt", 0, 0)
    block = (depth, rows, share, cols)
    planes, bias_sums = pl.pallas_call(
        ready_planes,
        out_shape=(
            jax.ShapeDtypeStruct((depth + 1, rows + 2, 3 * outs, cols), BF16),
            jax.ShapeDtypeStruct((outs, cols // 2), F32),
        ),
        in_specs=[WHOLE] * 2,
        out_specs=(WHOLE,) * 2,
        compiler_params=PARAMS,
        cost_estimate=pl.CostEstimate(flops=9_500_000_000, bytes_accessed=0, transcendentals=0),
    )(grad_out, outer)
    sums, moved = pl.pallas_call(
        weight_sums,
        out_shape=(
            jax.ShapeDtypeStruct((16, outs, cols), F32),
            jax.ShapeDtypeStruct((depth + 2, rows + 2, 3 * outs, cols), BF16),
        ),
        in_specs=[SCALAR] + [WHOLE] * 4,
        out_specs=(WHOLE,) * 2,
        compiler_params=PARAMS,
    )(odd, vol, planes, bias_sums, inner)
    parts = lax.all_to_all(sums, "space", 0, 0, axis_index_groups=XY_GROUPS)
    keep, send = pl.pallas_call(
        shares_first,
        out_shape=(
            jax.ShapeDtypeStruct((4,) + block, F32),
            jax.ShapeDtypeStruct((9,) + block, BF16),
        ),
        in_specs=[SCALAR] * 2 + [WHOLE] * 4,
        out_specs=(WHOLE,) * 2,
        scratch_shapes=[pltpu.VMEM((chans, 27 * outs), F32)],
        compiler_params=PARAMS,
    )(odd, me, moved, taps, outer, inner)
    got = lax.ppermute(send, "filt", swap_pairs(SWAPS[0]))
    mine = jnp.sum(parts, axis=0)
    mine, got = lax.optimization_barrier((mine, got))
    keep, send = pl.pallas_call(
        shares_next,
        out_shape=(
            jax.ShapeDtypeStruct((2,) + block, F32),
            jax.ShapeDtypeStruct((6,) + block, BF16),
        ),
        in_specs=[WHOLE] * 3,
        out_specs=(WHOLE,) * 2,
        compiler_params=PARAMS,
    )(keep, send, got)
    got = lax.ppermute(send, "filt", swap_pairs(SWAPS[1]))
    mine = lax.psum(mine, "space", axis_index_groups=Z_GROUPS)
    mine, got = lax.optimization_barrier((mine, got))
    keep, send, spread = pl.pallas_call(
        shares_last,
        out_shape=(
            jax.ShapeDtypeStruct((1,) + block, F32),
            jax.ShapeDtypeStruct((6,) + block, BF16),
            jax.ShapeDtypeStruct((16, outs, cols), F32),
        ),
        in_specs=[WHOLE] * 4,
        out_specs=(WHOLE,) * 3,
        compiler_params=PARAMS,
    )(keep, send, got, mine)
    got = lax.ppermute(send, "filt", swap_pairs(SWAPS[2]))
    every = lax.all_to_all(spread, "space", 0, 0, axis_index_groups=XY_GROUPS)
    output, grad_volume = pl.pallas_call(
        finish,
        out_shape=(
            jax.ShapeDtypeStruct((outs, depth, rows, cols), BF16),
            jax.ShapeDtypeStruct((share, depth, rows, cols), BF16),
        ),
        in_specs=[SCALAR] + [WHOLE] * 6,
        out_specs=(WHOLE,) * 2,
        scratch_shapes=[
            pltpu.VMEM((8,) + block, BF16),
            pltpu.VMEM((depth + 2, rows + 2, chans, cols), BF16),
        ],
        compiler_params=PARAMS,
    )(me, vol, keep, send, got, taps, bias[:, None])
    every, output, grad_volume = lax.optimization_barrier((every, output, grad_volume))
    scale = 1.0 / math.sqrt(depth * lax.axis_size("space") * rows * cols)
    grad_taps, grad_bias = pl.pallas_call(
        lambda *refs: unpack(scale, *refs),
        out_shape=(
            jax.ShapeDtypeStruct((27, outs, cols // 2), F32),
            jax.ShapeDtypeStruct((1, outs), F32),
        ),
        in_specs=[WHOLE],
        out_specs=(WHOLE,) * 2,
        compiler_params=PARAMS,
    )(every)
    return (output, grad_volume, grad_taps.transpose(0, 2, 1), grad_bias.reshape(outs))


def solution(mesh):
    in_specs = (
        P("filt", "space", None, None),
        P(None, None, "filt"),
        P("filt"),
        P("filt", "space", None, None),
    )
    out_specs = (
        P("filt", "space", None, None),
        P("filt", "space", None, None),
        P(None, None, "filt"),
        P("filt"),
    )
    return jax.shard_map(local, mesh=mesh, in_specs=in_specs, out_specs=out_specs, check_vma=False)
```

```python
import math

import jax
import jax.numpy as jnp
from jax import lax
from jax.experimental import pallas as pl
from jax.experimental.pallas import tpu as pltpu
from jax.sharding import PartitionSpec as P

F32 = jnp.float32
BF16 = jnp.bfloat16
WHOLE = pl.BlockSpec(memory_space=pltpu.VMEM)
SCALAR = pl.BlockSpec(memory_space=pltpu.SMEM)
PARAMS = pltpu.CompilerParams(vmem_limit_bytes=40 * 1024 * 1024)


def dot(left, right):
    return lax.dot_general(left, right, (((1,), (0,)), ((), ())), preferred_element_type=F32)


def dot_lanes(left, right):
    return lax.dot_general(left, right, (((1,), (1,)), ((), ())), preferred_element_type=F32)


def slide(rows, step):
    size = rows.shape[-1]
    axis = rows.ndim - 1
    turned = pltpu.roll(rows, (-step) % size, axis)
    lane = lax.broadcasted_iota(jnp.int32, rows.shape, axis)
    edge = size - 1 if step > 0 else 0
    return jnp.where(lane == edge, 0.0, turned)


def shifted(plane, target):
    outs, rows, cols = plane.shape
    blank = jnp.zeros((3 * outs, cols), BF16)
    target[0] = blank
    target[rows + 1] = blank
    turned = jnp.swapaxes(plane, 0, 1)
    for h in range(rows):
        wide = turned[h]
        target[h + 1, 0:outs] = slide(wide, 1).astype(BF16)
        target[h + 1, outs : 2 * outs] = wide.astype(BF16)
        target[h + 1, 2 * outs : 3 * outs] = slide(wide, -1).astype(BF16)


def ready_planes(grad_ref, outer_ref, planes_ref, bias_ref):
    outs, depth, rows, cols = grad_ref.shape
    total = None
    for d in range(depth):
        plane = grad_ref[:, d].astype(F32)
        shifted(plane, planes_ref.at[d])
        part = jnp.sum(plane, axis=1)
        total = part if total is None else total + part
    shifted(outer_ref[0:outs].astype(F32), planes_ref.at[depth])
    half = cols // 2
    bias_ref[...] = total[:, :half] + total[:, half:]


def weight_sums(vol_ref, gpad, bias_ref, sums_ref):
    peers, depth, rows, share, cols = vol_ref.shape
    outs = bias_ref.shape[0]
    chans = peers * share
    acc = jnp.zeros((27 * outs, chans), F32)
    for d in range(depth):
        for h in range(0, rows, 2):
            cells = jnp.concatenate(
                [
                    jnp.concatenate([vol_ref[s, d, h + k] for s in range(peers)], axis=0)
                    for k in range(2)
                ],
                axis=1,
            )
            acc = acc + dot_lanes(moved_rows(gpad, d, h), cells)
    for r in range(14):
        first = acc[2 * r * outs : (2 * r + 1) * outs]
        second = bias_ref[...] if r == 13 else acc[(2 * r + 1) * outs : (2 * r + 2) * outs]
        sums_ref[r] = jnp.concatenate([first, second], axis=1)
    for r in range(14, 16):
        sums_ref[r] = jnp.zeros((outs, cols), F32)


def moved_rows(gpad, d, h):
    return jnp.concatenate(
        [
            jnp.concatenate(
                [gpad[d + 2 - a, h + k + 2 - b] for a in range(3) for b in range(3)], axis=0
            )
            for k in range(2)
        ],
        axis=1,
    )


def split(value):
    high = value.astype(BF16)
    return high, (value - high.astype(F32)).astype(BF16)


def shares_first(
    odd_ref, me_ref, planes_ref, taps_ref, outer_ref, inner_ref, gpad, keep_ref, send_ref, turned
):
    _, depth, rows, share, cols = keep_ref.shape
    outs, chans = taps_ref.shape[1:]
    for d in range(depth):
        gpad[d + 1] = planes_ref[d]
    gpad[(depth + 1) * odd_ref[0]] = planes_ref[depth]
    shifted(inner_ref[0:outs].astype(F32), gpad.at[(depth + 1) * (1 - odd_ref[0])])
    turned[...] = taps_ref[...].reshape(27 * outs, chans).astype(F32).T
    me = me_ref[0]
    behind = jnp.concatenate(
        [
            turned[pl.ds(pl.multiple_of(share * jnp.bitwise_xor(me, r), share), share)]
            for r in ORDER
        ],
        axis=0,
    ).astype(BF16)
    for d in range(depth):
        for h in range(0, rows, 2):
            back = dot(behind, moved_rows(gpad, d, h))
            for k in range(2):
                for r in range(8):
                    value = back[share * r : share * (r + 1), k * cols : (k + 1) * cols]
                    if r < 4:
                        keep_ref[r, d, h + k] = value
                    else:
                        high, low = split(value)
                        send_ref[2 * (r - 4), d, h + k] = high
                        send_ref[2 * (r - 4) + 1, d, h + k] = low
    odd = odd_ref[0] == 1
    inner = inner_ref[outs : outs + share].astype(F32)
    outer = outer_ref[outs : outs + share].astype(F32)
    send_ref[8, 0] = jnp.swapaxes(jnp.where(odd, inner, outer), 0, 1).astype(BF16)
    send_ref[8, 1] = jnp.swapaxes(jnp.where(odd, outer, inner), 0, 1).astype(BF16)


def add_parts(parts_ref, mine_ref):
    mine_ref[...] = jnp.sum(parts_ref[...], axis=0)


def shares_next(keep_ref, sent_ref, got_ref, kept_ref, send_ref):
    blocks = keep_ref.shape[0]
    half = blocks // 2
    for r in range(blocks):
        value = keep_ref[r] + got_ref[2 * r].astype(F32) + got_ref[2 * r + 1].astype(F32)
        if r < half:
            kept_ref[r] = value
        else:
            high, low = split(value)
            send_ref[2 * (r - half)] = high
            send_ref[2 * (r - half) + 1] = low
    place = 2 * half
    for ref in (sent_ref, got_ref):
        for n in range(2 * blocks, ref.shape[0]):
            send_ref[place] = ref[n]
            place += 1


def shares_last(keep_ref, sent_ref, got_ref, mine_ref, kept_ref, send_ref, spread_ref):
    shares_next(keep_ref, sent_ref, got_ref, kept_ref, send_ref)
    for k in range(spread_ref.shape[0]):
        spread_ref[k] = mine_ref[...]


def finish(
    me_ref, vol_ref, keep_ref, sent_ref, got_ref, taps_ref, bias_ref, out_ref, back_ref, halo, vpad
):
    peers, depth, rows, share, cols = vol_ref.shape
    taps = taps_ref[...]
    outs, chans = taps.shape[1:]
    me = me_ref[0]
    first, second, third = SWAPS
    for place, r in enumerate((0, first, second, first ^ second)):
        halo[jnp.bitwise_xor(me, r)] = sent_ref[2 + place]
        halo[jnp.bitwise_xor(me, r ^ third)] = got_ref[2 + place]
    blank = jnp.zeros((chans, cols), BF16)
    for p in range(depth + 2):
        vpad[p, 0] = blank
        vpad[p, rows + 1] = blank
        for h in range(rows):
            if p == 0:
                lines = [halo[s, 0, h] for s in range(peers)]
            elif p == depth + 1:
                lines = [halo[s, 1, h] for s in range(peers)]
            else:
                lines = [vol_ref[s, p - 1, h] for s in range(peers)]
            vpad[p, h + 1] = jnp.concatenate(lines, axis=0)
    ahead = jnp.concatenate(
        [
            jnp.concatenate([taps[9 * a + 3 * b + c] for a in range(3) for b in range(3)], axis=1)
            for c in range(3)
        ],
        axis=0,
    )
    bias = jnp.broadcast_to(bias_ref[...], (outs, cols))
    for d in range(depth):
        lines = []
        for h in range(0, rows, 2):
            stack = jnp.concatenate(
                [
                    vpad[d : d + 3, h + k : h + k + 3].reshape(9 * chans, cols)
                    for k in range(2)
                ],
                axis=1,
            )
            part = dot(ahead, stack)
            for k in range(2):
                total = part[:, k * cols : (k + 1) * cols]
                lines.append(
                    total[outs : 2 * outs]
                    + slide(total[0:outs], -1)
                    + slide(total[2 * outs : 3 * outs], 1)
                    + bias
                )
        out_ref[:, d] = jnp.swapaxes(jnp.stack(lines), 0, 1).astype(BF16)
        total = keep_ref[0, d] + got_ref[0, d].astype(F32) + got_ref[1, d].astype(F32)
        back_ref[:, d] = jnp.swapaxes(total, 0, 1).astype(BF16)


def unpack(scale, every_ref, weight_ref, bias_ref):
    outs, cols = every_ref.shape[1:]
    half = cols // 2
    for t in range(27):
        r, side = t // 2, t % 2
        weight_ref[t] = every_ref[r, :, half * side : half * (side + 1)] * scale
    total = jnp.sum(every_ref[13, :, half:] * scale, axis=1, keepdims=True)
    wide = jnp.broadcast_to(total, (outs, cols))
    row = lax.broadcasted_iota(jnp.int32, (outs, cols), 0)
    lane = lax.broadcasted_iota(jnp.int32, (outs, cols), 1)
    flat = jnp.sum(jnp.where(row == lane, wide, 0.0), axis=0, keepdims=True)
    bias_ref[...] = flat[:, :outs]


SWAPS = (2, 4, 1)
ORDER = [sum(bit for k, bit in enumerate(SWAPS) if n & (4 >> k)) for n in range(8)]
XY_GROUPS = [[16 * z + k for k in range(16)] for z in range(4)]
Z_GROUPS = [[16 * z + k for z in range(4)] for k in range(16)]
EVEN = [(i, i ^ 1) for i in range(64)]
ODD = [(i, ((i + 1) ^ 1) - 1) for i in range(1, 63)]


def swap_edges(odd, head, tail):
    inner = lax.ppermute(jnp.where(odd, head, tail), "space", EVEN)
    outer = lax.ppermute(jnp.where(odd, tail, head), "space", ODD)
    return inner, outer


def swap_pairs(bit):
    return [(f, f ^ bit) for f in range(8)]


def local(volume, weight, bias, grad_out):
    share, depth, rows, cols = volume.shape
    outs = grad_out.shape[0]
    chans = weight.shape[1]
    taps = weight.transpose(0, 2, 1)
    own = volume.transpose(1, 2, 0, 3)
    odd = jnp.bitwise_and(lax.axis_index("space").astype(jnp.int32), 1)
    me = lax.axis_index("filt").astype(jnp.int32).reshape(1)
    head, tail = (
        jnp.concatenate([grad_out[:, d], volume[:, d]], axis=0) for d in (0, depth - 1)
    )
    inner, outer = swap_edges(odd == 1, head, tail)
    odd = odd.reshape(1)
    vol = lax.all_to_all(jnp.broadcast_to(own[None], (8,) + own.shape), "filt", 0, 0)
    block = (depth, rows, share, cols)
    planes, bias_sums = pl.pallas_call(
        ready_planes,
        out_shape=(
            jax.ShapeDtypeStruct((depth + 1, rows + 2, 3 * outs, cols), BF16),
            jax.ShapeDtypeStruct((outs, cols // 2), F32),
        ),
        in_specs=[WHOLE] * 2,
        out_specs=(WHOLE,) * 2,
        compiler_params=PARAMS,
        cost_estimate=pl.CostEstimate(flops=9_500_000_000, bytes_accessed=0, transcendentals=0),
    )(grad_out, outer)
    moved, keep, send = pl.pallas_call(
        shares_first,
        out_shape=(
            jax.ShapeDtypeStruct((depth + 2, rows + 2, 3 * outs, cols), BF16),
            jax.ShapeDtypeStruct((4,) + block, F32),
            jax.ShapeDtypeStruct((9,) + block, BF16),
        ),
        in_specs=[SCALAR] * 2 + [WHOLE] * 4,
        out_specs=(WHOLE,) * 3,
        scratch_shapes=[pltpu.VMEM((chans, 27 * outs), F32)],
        compiler_params=PARAMS,
    )(odd, me, planes, taps, outer, inner)
    got = lax.ppermute(send, "filt", swap_pairs(SWAPS[0]))
    sums = pl.pallas_call(
        weight_sums,
        out_shape=jax.ShapeDtypeStruct((16, outs, cols), F32),
        in_specs=[WHOLE] * 3,
        out_specs=WHOLE,
        compiler_params=PARAMS,
        cost_estimate=pl.CostEstimate(flops=6_000_000_000, bytes_accessed=0, transcendentals=0),
    )(vol, moved, bias_sums)
    parts = lax.all_to_all(sums, "space", 0, 0, axis_index_groups=XY_GROUPS)
    keep, send = pl.pallas_call(
        shares_next,
        out_shape=(
            jax.ShapeDtypeStruct((2,) + block, F32),
            jax.ShapeDtypeStruct((6,) + block, BF16),
        ),
        in_specs=[WHOLE] * 3,
        out_specs=(WHOLE,) * 2,
        compiler_params=PARAMS,
        cost_estimate=pl.CostEstimate(flops=1000, bytes_accessed=0, transcendentals=0),
    )(keep, send, got)
    got = lax.ppermute(send, "filt", swap_pairs(SWAPS[1]))
    mine = pl.pallas_call(
        add_parts,
        out_shape=jax.ShapeDtypeStruct((outs, cols), F32),
        in_specs=[WHOLE],
        out_specs=WHOLE,
        compiler_params=PARAMS,
        cost_estimate=pl.CostEstimate(flops=10_000_000_000, bytes_accessed=0, transcendentals=0),
    )(parts)
    mine = lax.psum(mine, "space", axis_index_groups=Z_GROUPS)
    mine, got = lax.optimization_barrier((mine, got))
    keep, send, spread = pl.pallas_call(
        shares_last,
        out_shape=(
            jax.ShapeDtypeStruct((1,) + block, F32),
            jax.ShapeDtypeStruct((6,) + block, BF16),
            jax.ShapeDtypeStruct((16, outs, cols), F32),
        ),
        in_specs=[WHOLE] * 4,
        out_specs=(WHOLE,) * 3,
        compiler_params=PARAMS,
    )(keep, send, got, mine)
    got = lax.ppermute(send, "filt", swap_pairs(SWAPS[2]))
    every = lax.all_to_all(spread, "space", 0, 0, axis_index_groups=XY_GROUPS)
    output, grad_volume = pl.pallas_call(
        finish,
        out_shape=(
            jax.ShapeDtypeStruct((outs, depth, rows, cols), BF16),
            jax.ShapeDtypeStruct((share, depth, rows, cols), BF16),
        ),
        in_specs=[SCALAR] + [WHOLE] * 6,
        out_specs=(WHOLE,) * 2,
        scratch_shapes=[
            pltpu.VMEM((8,) + block, BF16),
            pltpu.VMEM((depth + 2, rows + 2, chans, cols), BF16),
        ],
        compiler_params=PARAMS,
    )(me, vol, keep, send, got, taps, bias[:, None])
    every, output, grad_volume = lax.optimization_barrier((every, output, grad_volume))
    scale = 1.0 / math.sqrt(depth * lax.axis_size("space") * rows * cols)
    grad_taps, grad_bias = pl.pallas_call(
        lambda *refs: unpack(scale, *refs),
        out_shape=(
            jax.ShapeDtypeStruct((27, outs, cols // 2), F32),
            jax.ShapeDtypeStruct((1, outs), F32),
        ),
        in_specs=[WHOLE],
        out_specs=(WHOLE,) * 2,
        compiler_params=PARAMS,
    )(every)
    return (output, grad_volume, grad_taps.transpose(0, 2, 1), grad_bias.reshape(outs))


def solution(mesh):
    in_specs = (
        P("filt", "space", None, None),
        P(None, None, "filt"),
        P("filt"),
        P("filt", "space", None, None),
    )
    out_specs = (
        P("filt", "space", None, None),
        P("filt", "space", None, None),
        P(None, None, "filt"),
        P("filt"),
    )
    return jax.shard_map(local, mesh=mesh, in_specs=in_specs, out_specs=out_specs, check_vma=False)
```

```python
import math

import jax
import jax.numpy as jnp
from jax import lax
from jax.experimental import pallas as pl
from jax.experimental.pallas import tpu as pltpu
from jax.sharding import PartitionSpec as P

F32 = jnp.float32
BF16 = jnp.bfloat16
WHOLE = pl.BlockSpec(memory_space=pltpu.VMEM)
SCALAR = pl.BlockSpec(memory_space=pltpu.SMEM)
PARAMS = pltpu.CompilerParams(vmem_limit_bytes=40 * 1024 * 1024)


def dot(left, right):
    return lax.dot_general(left, right, (((1,), (0,)), ((), ())), preferred_element_type=F32)


def dot_lanes(left, right):
    return lax.dot_general(left, right, (((1,), (1,)), ((), ())), preferred_element_type=F32)


def slide(rows, step):
    size = rows.shape[-1]
    axis = rows.ndim - 1
    turned = pltpu.roll(rows, (-step) % size, axis)
    lane = lax.broadcasted_iota(jnp.int32, rows.shape, axis)
    edge = size - 1 if step > 0 else 0
    return jnp.where(lane == edge, 0.0, turned)


def shifted(plane, target):
    outs, rows, cols = plane.shape
    blank = jnp.zeros((3 * outs, cols), BF16)
    target[0] = blank
    target[rows + 1] = blank
    turned = jnp.swapaxes(plane, 0, 1)
    for h in range(rows):
        wide = turned[h]
        target[h + 1, 0:outs] = slide(wide, 1).astype(BF16)
        target[h + 1, outs : 2 * outs] = wide.astype(BF16)
        target[h + 1, 2 * outs : 3 * outs] = slide(wide, -1).astype(BF16)


def ready_planes(grad_ref, outer_ref, planes_ref, bias_ref):
    outs, depth, rows, cols = grad_ref.shape
    total = None
    for d in range(depth):
        plane = grad_ref[:, d].astype(F32)
        shifted(plane, planes_ref.at[d])
        part = jnp.sum(plane, axis=1)
        total = part if total is None else total + part
    shifted(outer_ref[0:outs].astype(F32), planes_ref.at[depth])
    half = cols // 2
    bias_ref[...] = total[:, :half] + total[:, half:]


def weight_sums(vol_ref, gpad, bias_ref, sums_ref):
    peers, depth, rows, share, cols = vol_ref.shape
    outs = bias_ref.shape[0]
    chans = peers * share
    acc = jnp.zeros((27 * outs, chans), F32)
    for d in range(depth):
        for h in range(0, rows, 2):
            cells = jnp.concatenate(
                [
                    jnp.concatenate([vol_ref[s, d, h + k] for s in range(peers)], axis=0)
                    for k in range(2)
                ],
                axis=1,
            )
            acc = acc + dot_lanes(moved_rows(gpad, d, h), cells)
    for r in range(14):
        first = acc[2 * r * outs : (2 * r + 1) * outs]
        second = bias_ref[...] if r == 13 else acc[(2 * r + 1) * outs : (2 * r + 2) * outs]
        sums_ref[r] = jnp.concatenate([first, second], axis=1)
    for r in range(14, 16):
        sums_ref[r] = jnp.zeros((outs, cols), F32)


def moved_rows(gpad, d, h):
    return jnp.concatenate(
        [
            jnp.concatenate(
                [gpad[d + 2 - a, h + k + 2 - b] for a in range(3) for b in range(3)], axis=0
            )
            for k in range(2)
        ],
        axis=1,
    )


def split(value):
    high = value.astype(BF16)
    return high, (value - high.astype(F32)).astype(BF16)


def shares_first(
    planes_ref, taps_ref, outer_ref, inner_ref, gpad, keep_ref, send_ref, turned
):
    _, depth, rows, share, cols = keep_ref.shape
    outs, chans = taps_ref.shape[1:]
    for d in range(depth):
        gpad[d + 1] = planes_ref[d]
    parity = jnp.bitwise_and(lax.axis_index("space"), 1)
    gpad[(depth + 1) * parity] = planes_ref[depth]
    shifted(inner_ref[0:outs].astype(F32), gpad.at[(depth + 1) * (1 - parity)])
    turned[...] = taps_ref[...].reshape(27 * outs, chans).astype(F32).T
    me = lax.axis_index("filt")
    behind = jnp.concatenate(
        [
            turned[pl.ds(pl.multiple_of(share * jnp.bitwise_xor(me, r), share), share)]
            for r in ORDER
        ],
        axis=0,
    ).astype(BF16)
    for d in range(depth):
        for h in range(0, rows, 2):
            back = dot(behind, moved_rows(gpad, d, h))
            for k in range(2):
                for r in range(8):
                    value = back[share * r : share * (r + 1), k * cols : (k + 1) * cols]
                    if r < 4:
                        keep_ref[r, d, h + k] = value
                    else:
                        high, low = split(value)
                        send_ref[2 * (r - 4), d, h + k] = high
                        send_ref[2 * (r - 4) + 1, d, h + k] = low
    odd = parity == 1
    inner = inner_ref[outs : outs + share].astype(F32)
    outer = outer_ref[outs : outs + share].astype(F32)
    send_ref[8, 0] = jnp.swapaxes(jnp.where(odd, inner, outer), 0, 1).astype(BF16)
    send_ref[8, 1] = jnp.swapaxes(jnp.where(odd, outer, inner), 0, 1).astype(BF16)


def add_parts(parts_ref, mine_ref):
    mine_ref[...] = jnp.sum(parts_ref[...], axis=0)


def shares_next(keep_ref, sent_ref, got_ref, kept_ref, send_ref):
    blocks = keep_ref.shape[0]
    half = blocks // 2
    for r in range(blocks):
        value = keep_ref[r] + got_ref[2 * r].astype(F32) + got_ref[2 * r + 1].astype(F32)
        if r < half:
            kept_ref[r] = value
        else:
            high, low = split(value)
            send_ref[2 * (r - half)] = high
            send_ref[2 * (r - half) + 1] = low
    place = 2 * half
    for ref in (sent_ref, got_ref):
        for n in range(2 * blocks, ref.shape[0]):
            send_ref[place] = ref[n]
            place += 1


def spread_sums(mine_ref, spread_ref):
    for k in range(spread_ref.shape[0]):
        spread_ref[k] = mine_ref[...]


def padded_plane(target, lines):
    rows = len(lines)
    blank = jnp.zeros(target.shape[1:], BF16)
    target[0] = blank
    target[rows + 1] = blank
    for h in range(rows):
        target[h + 1] = jnp.concatenate(lines[h], axis=0)


def weights_ahead(taps, depths):
    return jnp.concatenate(
        [
            jnp.concatenate([taps[9 * a + 3 * b + c] for a in depths for b in range(3)], axis=1)
            for c in range(3)
        ],
        axis=0,
    )


def own_output(bias_ref, vol_ref, taps_ref, part_ref, vpad):
    peers, depth, rows, _, cols = vol_ref.shape
    taps = taps_ref[...]
    outs, chans = taps.shape[1:]
    row = lax.broadcasted_iota(jnp.int32, (3 * outs, 2 * cols), 0)
    bias = jnp.zeros(row.shape, F32)
    for o in range(outs):
        bias = jnp.where(row == outs + o, bias_ref[o], bias)
    for d in range(depth):
        padded_plane(vpad.at[d], [[vol_ref[s, d, h] for s in range(peers)] for h in range(rows)])
    for d in range(depth):
        ahead = weights_ahead(taps, [e - d + 1 for e in range(depth)])
        for h in range(0, rows, 2):
            stack = jnp.concatenate(
                [
                    vpad[0:depth, h + k : h + k + 3].reshape(3 * depth * chans, cols)
                    for k in range(2)
                ],
                axis=1,
            )
            part = dot(ahead, stack) + bias
            for k in range(2):
                part_ref[d, h + k] = part[:, k * cols : (k + 1) * cols]


def finish(
    part_ref, keep_ref, sent_ref, got_ref, taps_ref, out_ref, back_ref, halo, vpad
):
    depth, rows, _, cols = part_ref.shape
    taps = taps_ref[...]
    outs, chans = taps.shape[1:]
    me = lax.axis_index("filt")
    first, second, third = SWAPS
    for place, r in enumerate((0, first, second, first ^ second)):
        halo[jnp.bitwise_xor(me, r)] = sent_ref[2 + place]
        halo[jnp.bitwise_xor(me, r ^ third)] = got_ref[2 + place]
    for d in range(depth):
        padded_plane(vpad.at[d], [[halo[s, d, h] for s in range(8)] for h in range(rows)])
        ahead = weights_ahead(taps, [2 * d])
        lines = []
        for h in range(0, rows, 2):
            stack = jnp.concatenate(
                [vpad[d, h + k : h + k + 3].reshape(3 * chans, cols) for k in range(2)], axis=1
            )
            part = dot(ahead, stack)
            for k in range(2):
                total = part[:, k * cols : (k + 1) * cols] + part_ref[d, h + k]
                lines.append(
                    total[outs : 2 * outs]
                    + slide(total[0:outs], -1)
                    + slide(total[2 * outs : 3 * outs], 1)
                )
        out_ref[:, d] = jnp.swapaxes(jnp.stack(lines), 0, 1).astype(BF16)
        total = keep_ref[0, d] + got_ref[0, d].astype(F32) + got_ref[1, d].astype(F32)
        back_ref[:, d] = jnp.swapaxes(total, 0, 1).astype(BF16)


def unpack(scale, every_ref, weight_ref, bias_ref):
    outs, cols = every_ref.shape[1:]
    half = cols // 2
    for t in range(27):
        r, side = t // 2, t % 2
        weight_ref[t] = every_ref[r, :, half * side : half * (side + 1)] * scale
    total = jnp.sum(every_ref[13, :, half:] * scale, axis=1, keepdims=True)
    wide = jnp.broadcast_to(total, (outs, cols))
    row = lax.broadcasted_iota(jnp.int32, (outs, cols), 0)
    lane = lax.broadcasted_iota(jnp.int32, (outs, cols), 1)
    flat = jnp.sum(jnp.where(row == lane, wide, 0.0), axis=0, keepdims=True)
    bias_ref[...] = flat[:, :outs]


SWAPS = (2, 4, 1)
ORDER = [sum(bit for k, bit in enumerate(SWAPS) if n & (4 >> k)) for n in range(8)]
XY_GROUPS = [[16 * z + k for k in range(16)] for z in range(4)]
Z_GROUPS = [[16 * z + k for z in range(4)] for k in range(16)]
EVEN = [(i, i ^ 1) for i in range(64)]
ODD = [(i, ((i + 1) ^ 1) - 1) for i in range(1, 63)]


def swap_edges(odd, head, tail):
    inner = lax.ppermute(jnp.where(odd, head, tail), "space", EVEN)
    outer = lax.ppermute(jnp.where(odd, tail, head), "space", ODD)
    return inner, outer


def swap_pairs(bit):
    return [(f, f ^ bit) for f in range(8)]


def local(volume, weight, bias, grad_out):
    share, depth, rows, cols = volume.shape
    outs = grad_out.shape[0]
    chans = weight.shape[1]
    taps = weight.transpose(0, 2, 1)
    own = volume.transpose(1, 2, 0, 3)
    odd = jnp.bitwise_and(lax.axis_index("space").astype(jnp.int32), 1)
    head, tail = (
        jnp.concatenate([grad_out[:, d], volume[:, d]], axis=0) for d in (0, depth - 1)
    )
    inner, outer = swap_edges(odd == 1, head, tail)
    vol = lax.all_to_all(jnp.broadcast_to(own[None], (8,) + own.shape), "filt", 0, 0)
    block = (depth, rows, share, cols)
    planes, bias_sums = pl.pallas_call(
        ready_planes,
        out_shape=(
            jax.ShapeDtypeStruct((depth + 1, rows + 2, 3 * outs, cols), BF16),
            jax.ShapeDtypeStruct((outs, cols // 2), F32),
        ),
        in_specs=[WHOLE] * 2,
        out_specs=(WHOLE,) * 2,
        compiler_params=PARAMS,
        cost_estimate=pl.CostEstimate(flops=9_500_000_000, bytes_accessed=0, transcendentals=0),
    )(grad_out, outer)
    moved, keep, send = pl.pallas_call(
        shares_first,
        out_shape=(
            jax.ShapeDtypeStruct((depth + 2, rows + 2, 3 * outs, cols), BF16),
            jax.ShapeDtypeStruct((4,) + block, F32),
            jax.ShapeDtypeStruct((9,) + block, BF16),
        ),
        in_specs=[WHOLE] * 4,
        out_specs=(WHOLE,) * 3,
        scratch_shapes=[pltpu.VMEM((chans, 27 * outs), F32)],
        compiler_params=PARAMS,
    )(planes, taps, outer, inner)
    got = lax.ppermute(send, "filt", swap_pairs(SWAPS[0]))
    sums = pl.pallas_call(
        weight_sums,
        out_shape=jax.ShapeDtypeStruct((16, outs, cols), F32),
        in_specs=[WHOLE] * 3,
        out_specs=WHOLE,
        compiler_params=PARAMS,
        cost_estimate=pl.CostEstimate(flops=6_000_000_000, bytes_accessed=0, transcendentals=0),
    )(vol, moved, bias_sums)
    parts = lax.all_to_all(sums, "space", 0, 0, axis_index_groups=XY_GROUPS)
    keep, send = pl.pallas_call(
        shares_next,
        out_shape=(
            jax.ShapeDtypeStruct((2,) + block, F32),
            jax.ShapeDtypeStruct((6,) + block, BF16),
        ),
        in_specs=[WHOLE] * 3,
        out_specs=(WHOLE,) * 2,
        compiler_params=PARAMS,
        cost_estimate=pl.CostEstimate(flops=1000, bytes_accessed=0, transcendentals=0),
    )(keep, send, got)
    got = lax.ppermute(send, "filt", swap_pairs(SWAPS[1]))
    mine = pl.pallas_call(
        add_parts,
        out_shape=jax.ShapeDtypeStruct((outs, cols), F32),
        in_specs=[WHOLE],
        out_specs=WHOLE,
        compiler_params=PARAMS,
        cost_estimate=pl.CostEstimate(flops=10_000_000_000, bytes_accessed=0, transcendentals=0),
    )(parts)
    mine = lax.psum(mine, "space", axis_index_groups=Z_GROUPS)
    mine, got, held = lax.optimization_barrier((mine, got, vol))
    spread = pl.pallas_call(
        spread_sums,
        out_shape=jax.ShapeDtypeStruct((16, outs, cols), F32),
        in_specs=[WHOLE],
        out_specs=WHOLE,
        compiler_params=PARAMS,
    )(mine)
    keep, send = pl.pallas_call(
        shares_next,
        out_shape=(
            jax.ShapeDtypeStruct((1,) + block, F32),
            jax.ShapeDtypeStruct((6,) + block, BF16),
        ),
        in_specs=[WHOLE] * 3,
        out_specs=(WHOLE,) * 2,
        compiler_params=PARAMS,
    )(keep, send, got)
    got = lax.ppermute(send, "filt", swap_pairs(SWAPS[2]))
    every = lax.all_to_all(spread, "space", 0, 0, axis_index_groups=XY_GROUPS)
    part = pl.pallas_call(
        own_output,
        out_shape=jax.ShapeDtypeStruct((depth, rows, 3 * outs, cols), F32),
        in_specs=[SCALAR] + [WHOLE] * 2,
        out_specs=WHOLE,
        scratch_shapes=[pltpu.VMEM((depth, rows + 2, chans, cols), BF16)],
        compiler_params=PARAMS,
    )(bias, held, taps)
    every, part = lax.optimization_barrier((every, part))
    output, grad_volume = pl.pallas_call(
        finish,
        out_shape=(
            jax.ShapeDtypeStruct((outs, depth, rows, cols), BF16),
            jax.ShapeDtypeStruct((share, depth, rows, cols), BF16),
        ),
        in_specs=[WHOLE] * 5,
        out_specs=(WHOLE,) * 2,
        scratch_shapes=[
            pltpu.VMEM((8,) + block, BF16),
            pltpu.VMEM((depth, rows + 2, chans, cols), BF16),
        ],
        compiler_params=PARAMS,
    )(part, keep, send, got, taps)
    scale = 1.0 / math.sqrt(depth * lax.axis_size("space") * rows * cols)
    grad_taps, grad_bias = pl.pallas_call(
        lambda *refs: unpack(scale, *refs),
        out_shape=(
            jax.ShapeDtypeStruct((27, outs, cols // 2), F32),
            jax.ShapeDtypeStruct((1, outs), F32),
        ),
        in_specs=[WHOLE],
        out_specs=(WHOLE,) * 2,
        compiler_params=PARAMS,
        cost_estimate=pl.CostEstimate(flops=10_000_000_000, bytes_accessed=0, transcendentals=0),
    )(every)
    return (output, grad_volume, grad_taps.transpose(0, 2, 1), grad_bias.reshape(outs))


def solution(mesh):
    in_specs = (
        P("filt", "space", None, None),
        P(None, None, "filt"),
        P("filt"),
        P("filt", "space", None, None),
    )
    out_specs = (
        P("filt", "space", None, None),
        P("filt", "space", None, None),
        P(None, None, "filt"),
        P("filt"),
    )
    return jax.shard_map(local, mesh=mesh, in_specs=in_specs, out_specs=out_specs, check_vma=False)
```

```python
import math

import jax
import jax.numpy as jnp
from jax import lax
from jax.experimental import pallas as pl
from jax.experimental.pallas import tpu as pltpu
from jax.sharding import PartitionSpec as P

F32 = jnp.float32
BF16 = jnp.bfloat16
WHOLE = pl.BlockSpec(memory_space=pltpu.VMEM)
SCALAR = pl.BlockSpec(memory_space=pltpu.SMEM)
PARAMS = pltpu.CompilerParams(vmem_limit_bytes=40 * 1024 * 1024)


def dot(left, right):
    return lax.dot_general(left, right, (((1,), (0,)), ((), ())), preferred_element_type=F32)


def dot_lanes(left, right):
    return lax.dot_general(left, right, (((1,), (1,)), ((), ())), preferred_element_type=F32)


def slide(rows, step):
    size = rows.shape[-1]
    axis = rows.ndim - 1
    turned = pltpu.roll(rows, (-step) % size, axis)
    lane = lax.broadcasted_iota(jnp.int32, rows.shape, axis)
    edge = size - 1 if step > 0 else 0
    return jnp.where(lane == edge, 0.0, turned)


def shifted(plane, target):
    outs, rows, cols = plane.shape
    blank = jnp.zeros((3 * outs, cols), BF16)
    target[0] = blank
    target[rows + 1] = blank
    turned = jnp.swapaxes(plane, 0, 1)
    for h in range(rows):
        wide = turned[h]
        target[h + 1, 0:outs] = slide(wide, 1).astype(BF16)
        target[h + 1, outs : 2 * outs] = wide.astype(BF16)
        target[h + 1, 2 * outs : 3 * outs] = slide(wide, -1).astype(BF16)


def ready_planes(grad_ref, outer_ref, taps_ref, planes_ref, bias_ref, behind_ref, turned):
    outs, depth, rows, cols = grad_ref.shape
    total = None
    for d in range(depth):
        plane = grad_ref[:, d].astype(F32)
        shifted(plane, planes_ref.at[d])
        part = jnp.sum(plane, axis=1)
        total = part if total is None else total + part
    shifted(outer_ref[0:outs].astype(F32), planes_ref.at[depth])
    half = cols // 2
    bias_ref[...] = total[:, :half] + total[:, half:]
    chans = taps_ref.shape[2]
    share = chans // 8
    turned[...] = taps_ref[...].reshape(27 * outs, chans).astype(F32).T
    me = lax.axis_index("filt")
    behind_ref[...] = jnp.concatenate(
        [
            turned[pl.ds(pl.multiple_of(share * jnp.bitwise_xor(me, r), share), share)]
            for r in ORDER
        ],
        axis=0,
    ).astype(BF16)


def weight_sums(vol_ref, gpad, bias_ref, sums_ref):
    peers, depth, rows, share, cols = vol_ref.shape
    outs = bias_ref.shape[0]
    chans = peers * share
    acc = jnp.zeros((27 * outs, chans), F32)
    for d in range(depth):
        for h in range(0, rows, 2):
            cells = jnp.concatenate(
                [
                    jnp.concatenate([vol_ref[s, d, h + k] for s in range(peers)], axis=0)
                    for k in range(2)
                ],
                axis=1,
            )
            acc = acc + dot_lanes(moved_rows(gpad, d, h), cells)
    for r in range(14):
        first = acc[2 * r * outs : (2 * r + 1) * outs]
        second = bias_ref[...] if r == 13 else acc[(2 * r + 1) * outs : (2 * r + 2) * outs]
        sums_ref[r] = jnp.concatenate([first, second], axis=1)
    for r in range(14, 16):
        sums_ref[r] = jnp.zeros((outs, cols), F32)


def moved_rows(gpad, d, h):
    return jnp.concatenate(
        [
            jnp.concatenate(
                [gpad[d + 2 - a, h + k + 2 - b] for a in range(3) for b in range(3)], axis=0
            )
            for k in range(2)
        ],
        axis=1,
    )


def split(value):
    high = value.astype(BF16)
    return high, (value - high.astype(F32)).astype(BF16)


def shares_first(
    planes_ref, behind_ref, outer_ref, inner_ref, gpad, keep_ref, send_ref
):
    _, depth, rows, share, cols = keep_ref.shape
    outs = inner_ref.shape[0] - share
    for d in range(depth):
        gpad[d + 1] = planes_ref[d]
    parity = jnp.bitwise_and(lax.axis_index("space"), 1)
    gpad[(depth + 1) * parity] = planes_ref[depth]
    shifted(inner_ref[0:outs].astype(F32), gpad.at[(depth + 1) * (1 - parity)])
    behind = behind_ref[...]
    for d in range(depth):
        for h in range(0, rows, 2):
            back = dot(behind, moved_rows(gpad, d, h))
            for k in range(2):
                for r in range(8):
                    value = back[share * r : share * (r + 1), k * cols : (k + 1) * cols]
                    if r < 4:
                        keep_ref[r, d, h + k] = value
                    else:
                        high, low = split(value)
                        send_ref[2 * (r - 4), d, h + k] = high
                        send_ref[2 * (r - 4) + 1, d, h + k] = low
    odd = parity == 1
    inner = inner_ref[outs : outs + share].astype(F32)
    outer = outer_ref[outs : outs + share].astype(F32)
    send_ref[8, 0] = jnp.swapaxes(jnp.where(odd, inner, outer), 0, 1).astype(BF16)
    send_ref[8, 1] = jnp.swapaxes(jnp.where(odd, outer, inner), 0, 1).astype(BF16)


def add_parts(parts_ref, mine_ref):
    mine_ref[...] = jnp.sum(parts_ref[...], axis=0)


def shares_next(keep_ref, sent_ref, got_ref, kept_ref, send_ref):
    blocks = keep_ref.shape[0]
    half = blocks // 2
    for r in range(blocks):
        value = keep_ref[r] + got_ref[2 * r].astype(F32) + got_ref[2 * r + 1].astype(F32)
        if r < half:
            kept_ref[r] = value
        else:
            high, low = split(value)
            send_ref[2 * (r - half)] = high
            send_ref[2 * (r - half) + 1] = low
    place = 2 * half
    for ref in (sent_ref, got_ref):
        for n in range(2 * blocks, ref.shape[0]):
            send_ref[place] = ref[n]
            place += 1


def spread_sums(mine_ref, spread_ref):
    for k in range(spread_ref.shape[0]):
        spread_ref[k] = mine_ref[...]


def padded_plane(target, lines):
    rows = len(lines)
    blank = jnp.zeros(target.shape[1:], BF16)
    target[0] = blank
    target[rows + 1] = blank
    for h in range(rows):
        target[h + 1] = jnp.concatenate(lines[h], axis=0)


def weights_ahead(taps, depths):
    return jnp.concatenate(
        [
            jnp.concatenate([taps[9 * a + 3 * b + c] for a in depths for b in range(3)], axis=1)
            for c in range(3)
        ],
        axis=0,
    )


def own_output(bias_ref, vol_ref, taps_ref, part_ref, vpad):
    peers, depth, rows, _, cols = vol_ref.shape
    taps = taps_ref[...]
    outs, chans = taps.shape[1:]
    row = lax.broadcasted_iota(jnp.int32, (3 * outs, 2 * cols), 0)
    bias = jnp.zeros(row.shape, F32)
    for o in range(outs):
        bias = jnp.where(row == outs + o, bias_ref[o], bias)
    for d in range(depth):
        padded_plane(vpad.at[d], [[vol_ref[s, d, h] for s in range(peers)] for h in range(rows)])
    for d in range(depth):
        ahead = weights_ahead(taps, [e - d + 1 for e in range(depth)])
        for h in range(0, rows, 2):
            stack = jnp.concatenate(
                [
                    vpad[0:depth, h + k : h + k + 3].reshape(3 * depth * chans, cols)
                    for k in range(2)
                ],
                axis=1,
            )
            part = dot(ahead, stack) + bias
            for k in range(2):
                part_ref[d, h + k] = part[:, k * cols : (k + 1) * cols]


def finish(
    sums_ref, part_ref, keep_ref, sent_ref, got_ref, taps_ref,
    weight_ref, bias_ref, out_ref, back_ref, halo, vpad,
):
    depth, rows, _, cols = part_ref.shape
    taps = taps_ref[...]
    outs, chans = taps.shape[1:]
    half = cols // 2
    for t in range(27):
        r, side = t // 2, t % 2
        weight_ref[t] = sums_ref[r, :, half * side : half * (side + 1)]
    total = jnp.sum(sums_ref[13, :, half:], axis=1, keepdims=True)
    wide = jnp.broadcast_to(total, (outs, cols))
    row = lax.broadcasted_iota(jnp.int32, (outs, cols), 0)
    lane = lax.broadcasted_iota(jnp.int32, (outs, cols), 1)
    flat = jnp.sum(jnp.where(row == lane, wide, 0.0), axis=0, keepdims=True)
    bias_ref[...] = flat[:, :outs]
    me = lax.axis_index("filt")
    first, second, third = SWAPS
    for place, r in enumerate((0, first, second, first ^ second)):
        halo[jnp.bitwise_xor(me, r)] = sent_ref[2 + place]
        halo[jnp.bitwise_xor(me, r ^ third)] = got_ref[2 + place]
    for d in range(depth):
        padded_plane(vpad.at[d], [[halo[s, d, h] for s in range(8)] for h in range(rows)])
        ahead = weights_ahead(taps, [2 * d])
        lines = []
        for h in range(0, rows, 2):
            stack = jnp.concatenate(
                [vpad[d, h + k : h + k + 3].reshape(3 * chans, cols) for k in range(2)], axis=1
            )
            part = dot(ahead, stack)
            for k in range(2):
                total = part[:, k * cols : (k + 1) * cols] + part_ref[d, h + k]
                lines.append(
                    total[outs : 2 * outs]
                    + slide(total[0:outs], -1)
                    + slide(total[2 * outs : 3 * outs], 1)
                )
        out_ref[:, d] = jnp.swapaxes(jnp.stack(lines), 0, 1).astype(BF16)
        total = keep_ref[0, d] + got_ref[0, d].astype(F32) + got_ref[1, d].astype(F32)
        back_ref[:, d] = jnp.swapaxes(total, 0, 1).astype(BF16)


def scaled(scale, every_ref, sums_ref):
    sums_ref[...] = every_ref[...] * scale


SWAPS = (2, 4, 1)
ORDER = [sum(bit for k, bit in enumerate(SWAPS) if n & (4 >> k)) for n in range(8)]
XY_GROUPS = [[16 * z + k for k in range(16)] for z in range(4)]
Z_GROUPS = [[16 * z + k for z in range(4)] for k in range(16)]
EVEN = [(i, i ^ 1) for i in range(64)]
ODD = [(i, ((i + 1) ^ 1) - 1) for i in range(1, 63)]


def swap_edges(odd, head, tail):
    inner = lax.ppermute(jnp.where(odd, head, tail), "space", EVEN)
    outer = lax.ppermute(jnp.where(odd, tail, head), "space", ODD)
    return inner, outer


def swap_pairs(bit):
    return [(f, f ^ bit) for f in range(8)]


def local(volume, weight, bias, grad_out):
    share, depth, rows, cols = volume.shape
    outs = grad_out.shape[0]
    chans = weight.shape[1]
    taps = weight.transpose(0, 2, 1)
    own = volume.transpose(1, 2, 0, 3)
    odd = jnp.bitwise_and(lax.axis_index("space").astype(jnp.int32), 1)
    head, tail = (
        jnp.concatenate([grad_out[:, d], volume[:, d]], axis=0) for d in (0, depth - 1)
    )
    inner, outer = swap_edges(odd == 1, head, tail)
    vol = lax.all_to_all(jnp.broadcast_to(own[None], (8,) + own.shape), "filt", 0, 0)
    block = (depth, rows, share, cols)
    planes, bias_sums, behind = pl.pallas_call(
        ready_planes,
        out_shape=(
            jax.ShapeDtypeStruct((depth + 1, rows + 2, 3 * outs, cols), BF16),
            jax.ShapeDtypeStruct((outs, cols // 2), F32),
            jax.ShapeDtypeStruct((chans, 27 * outs), BF16),
        ),
        in_specs=[WHOLE] * 3,
        out_specs=(WHOLE,) * 3,
        scratch_shapes=[pltpu.VMEM((chans, 27 * outs), F32)],
        compiler_params=PARAMS,
        cost_estimate=pl.CostEstimate(flops=9_500_000_000, bytes_accessed=0, transcendentals=0),
    )(grad_out, outer, taps)
    moved, keep, send = pl.pallas_call(
        shares_first,
        out_shape=(
            jax.ShapeDtypeStruct((depth + 2, rows + 2, 3 * outs, cols), BF16),
            jax.ShapeDtypeStruct((4,) + block, F32),
            jax.ShapeDtypeStruct((9,) + block, BF16),
        ),
        in_specs=[WHOLE] * 4,
        out_specs=(WHOLE,) * 3,
        compiler_params=PARAMS,
    )(planes, behind, outer, inner)
    got = lax.ppermute(send, "filt", swap_pairs(SWAPS[0]))
    sums = pl.pallas_call(
        weight_sums,
        out_shape=jax.ShapeDtypeStruct((16, outs, cols), F32),
        in_specs=[WHOLE] * 3,
        out_specs=WHOLE,
        compiler_params=PARAMS,
        cost_estimate=pl.CostEstimate(flops=6_000_000_000, bytes_accessed=0, transcendentals=0),
    )(vol, moved, bias_sums)
    parts = lax.all_to_all(sums, "space", 0, 0, axis_index_groups=XY_GROUPS)
    keep, send = pl.pallas_call(
        shares_next,
        out_shape=(
            jax.ShapeDtypeStruct((2,) + block, F32),
            jax.ShapeDtypeStruct((6,) + block, BF16),
        ),
        in_specs=[WHOLE] * 3,
        out_specs=(WHOLE,) * 2,
        compiler_params=PARAMS,
        cost_estimate=pl.CostEstimate(flops=1000, bytes_accessed=0, transcendentals=0),
    )(keep, send, got)
    got = lax.ppermute(send, "filt", swap_pairs(SWAPS[1]))
    mine = pl.pallas_call(
        add_parts,
        out_shape=jax.ShapeDtypeStruct((outs, cols), F32),
        in_specs=[WHOLE],
        out_specs=WHOLE,
        compiler_params=PARAMS,
        cost_estimate=pl.CostEstimate(flops=10_000_000_000, bytes_accessed=0, transcendentals=0),
    )(parts)
    mine = lax.psum(mine, "space", axis_index_groups=Z_GROUPS)
    mine, got, held = lax.optimization_barrier((mine, got, vol))
    spread = pl.pallas_call(
        spread_sums,
        out_shape=jax.ShapeDtypeStruct((16, outs, cols), F32),
        in_specs=[WHOLE],
        out_specs=WHOLE,
        compiler_params=PARAMS,
    )(mine)
    keep, send = pl.pallas_call(
        shares_next,
        out_shape=(
            jax.ShapeDtypeStruct((1,) + block, F32),
            jax.ShapeDtypeStruct((6,) + block, BF16),
        ),
        in_specs=[WHOLE] * 3,
        out_specs=(WHOLE,) * 2,
        compiler_params=PARAMS,
    )(keep, send, got)
    got = lax.ppermute(send, "filt", swap_pairs(SWAPS[2]))
    every = lax.all_to_all(spread, "space", 0, 0, axis_index_groups=XY_GROUPS)
    part = pl.pallas_call(
        own_output,
        out_shape=jax.ShapeDtypeStruct((depth, rows, 3 * outs, cols), F32),
        in_specs=[SCALAR] + [WHOLE] * 2,
        out_specs=WHOLE,
        scratch_shapes=[pltpu.VMEM((depth, rows + 2, chans, cols), BF16)],
        compiler_params=PARAMS,
    )(bias, held, taps)
    every, part = lax.optimization_barrier((every, part))
    scale = 1.0 / math.sqrt(depth * lax.axis_size("space") * rows * cols)
    every = pl.pallas_call(
        lambda *refs: scaled(scale, *refs),
        out_shape=jax.ShapeDtypeStruct((16, outs, cols), F32),
        in_specs=[WHOLE],
        out_specs=WHOLE,
        compiler_params=PARAMS,
        cost_estimate=pl.CostEstimate(flops=10_000_000_000, bytes_accessed=0, transcendentals=0),
    )(every)
    grad_taps, grad_bias, output, grad_volume = pl.pallas_call(
        finish,
        out_shape=(
            jax.ShapeDtypeStruct((27, outs, cols // 2), F32),
            jax.ShapeDtypeStruct((1, outs), F32),
            jax.ShapeDtypeStruct((outs, depth, rows, cols), BF16),
            jax.ShapeDtypeStruct((share, depth, rows, cols), BF16),
        ),
        in_specs=[WHOLE] * 6,
        out_specs=(WHOLE,) * 4,
        scratch_shapes=[
            pltpu.VMEM((8,) + block, BF16),
            pltpu.VMEM((depth, rows + 2, chans, cols), BF16),
        ],
        compiler_params=PARAMS,
    )(every, part, keep, send, got, taps)
    return (output, grad_volume, grad_taps.transpose(0, 2, 1), grad_bias.reshape(outs))


def solution(mesh):
    in_specs = (
        P("filt", "space", None, None),
        P(None, None, "filt"),
        P("filt"),
        P("filt", "space", None, None),
    )
    out_specs = (
        P("filt", "space", None, None),
        P("filt", "space", None, None),
        P(None, None, "filt"),
        P("filt"),
    )
    return jax.shard_map(local, mesh=mesh, in_specs=in_specs, out_specs=out_specs, check_vma=False)
```

```python
import math

import jax
import jax.numpy as jnp
from jax import lax
from jax.experimental import pallas as pl
from jax.experimental.pallas import tpu as pltpu
from jax.sharding import PartitionSpec as P

F32 = jnp.float32
BF16 = jnp.bfloat16
WHOLE = pl.BlockSpec(memory_space=pltpu.VMEM)
SCALAR = pl.BlockSpec(memory_space=pltpu.SMEM)
PARAMS = pltpu.CompilerParams(vmem_limit_bytes=40 * 1024 * 1024)


def dot(left, right):
    return lax.dot_general(left, right, (((1,), (0,)), ((), ())), preferred_element_type=F32)


def dot_lanes(left, right):
    return lax.dot_general(left, right, (((1,), (1,)), ((), ())), preferred_element_type=F32)


def slide(rows, step):
    size = rows.shape[-1]
    axis = rows.ndim - 1
    turned = pltpu.roll(rows, (-step) % size, axis)
    lane = lax.broadcasted_iota(jnp.int32, rows.shape, axis)
    edge = size - 1 if step > 0 else 0
    return jnp.where(lane == edge, 0.0, turned)


def shifted(plane, target):
    outs, rows, cols = plane.shape
    blank = jnp.zeros((3 * outs, cols), BF16)
    target[0] = blank
    target[rows + 1] = blank
    turned = jnp.swapaxes(plane, 0, 1)
    for h in range(rows):
        wide = turned[h]
        target[h + 1, 0:outs] = slide(wide, 1).astype(BF16)
        target[h + 1, outs : 2 * outs] = wide.astype(BF16)
        target[h + 1, 2 * outs : 3 * outs] = slide(wide, -1).astype(BF16)


def ready_planes(
    grad_ref, outer_ref, taps_ref, planes_ref, bias_ref, edge_ref, back_ref, turned
):
    outs, depth, rows, cols = grad_ref.shape
    odd = jnp.bitwise_and(lax.axis_index("space"), 1)
    planes_ref[(depth + 1) * (1 - odd)] = jnp.zeros(planes_ref.shape[1:], BF16)
    total = None
    for d in range(depth):
        plane = grad_ref[:, d].astype(F32)
        shifted(plane, planes_ref.at[d + 1])
        part = jnp.sum(plane, axis=1)
        total = part if total is None else total + part
    shifted(outer_ref[0:outs].astype(F32), planes_ref.at[(depth + 1) * odd])
    half = cols // 2
    bias_ref[...] = total[:, :half] + total[:, half:]
    chans = taps_ref.shape[2]
    share = chans // 8
    turned[...] = taps_ref[...].reshape(27 * outs, chans).astype(F32).T
    me = lax.axis_index("filt")
    behind = jnp.concatenate(
        [
            turned[pl.ds(pl.multiple_of(share * jnp.bitwise_xor(me, r), share), share)]
            for r in ORDER
        ],
        axis=0,
    )
    edge_ref[...] = jnp.where(odd == 1, behind[:, 18 * outs :], behind[:, : 9 * outs]).astype(BF16)
    behind = behind.astype(BF16)
    for d in range(depth):
        for h in range(0, rows, 2):
            back = dot(behind, moved_rows(planes_ref, d, h))
            for k in range(2):
                back_ref[d, h + k] = back[:, k * cols : (k + 1) * cols]


def weight_sums(vol_ref, gpad, bias_ref, sums_ref):
    peers, depth, rows, share, cols = vol_ref.shape
    outs = bias_ref.shape[0]
    chans = peers * share
    acc = jnp.zeros((27 * outs, chans), F32)
    for d in range(depth):
        for h in range(0, rows, 2):
            cells = jnp.concatenate(
                [
                    jnp.concatenate([vol_ref[s, d, h + k] for s in range(peers)], axis=0)
                    for k in range(2)
                ],
                axis=1,
            )
            acc = acc + dot_lanes(moved_rows(gpad, d, h), cells)
    for r in range(14):
        first = acc[2 * r * outs : (2 * r + 1) * outs]
        second = bias_ref[...] if r == 13 else acc[(2 * r + 1) * outs : (2 * r + 2) * outs]
        sums_ref[r] = jnp.concatenate([first, second], axis=1)
    for r in range(14, 16):
        sums_ref[r] = jnp.zeros((outs, cols), F32)


def moved_rows(gpad, d, h):
    return jnp.concatenate(
        [
            jnp.concatenate(
                [gpad[d + 2 - a, h + k + 2 - b] for a in range(3) for b in range(3)], axis=0
            )
            for k in range(2)
        ],
        axis=1,
    )


def split(value):
    high = value.astype(BF16)
    return high, (value - high.astype(F32)).astype(BF16)


def shares_first(
    planes_ref, edge_ref, back_ref, outer_ref, inner_ref, gpad, keep_ref, send_ref
):
    _, depth, rows, share, cols = keep_ref.shape
    outs = inner_ref.shape[0] - share
    parity = jnp.bitwise_and(lax.axis_index("space"), 1)
    gpad[...] = planes_ref[...]
    even = gpad.at[(depth + 1) * (1 - parity)]
    shifted(inner_ref[0:outs].astype(F32), even)
    edge = edge_ref[...]
    near = (depth - 1) * (1 - parity)
    for h in range(0, rows, 2):
        moved = jnp.concatenate(
            [
                jnp.concatenate([even[h + k + 2 - b] for b in range(3)], axis=0)
                for k in range(2)
            ],
            axis=1,
        )
        part = dot(edge, moved)
        for k in range(2):
            for d, back in (
                (near, back_ref[near, h + k] + part[:, k * cols : (k + 1) * cols]),
                (depth - 1 - near, back_ref[depth - 1 - near, h + k]),
            ):
                for r in range(8):
                    value = back[share * r : share * (r + 1)]
                    if r < 4:
                        keep_ref[r, d, h + k] = value
                    else:
                        high, low = split(value)
                        send_ref[2 * (r - 4), d, h + k] = high
                        send_ref[2 * (r - 4) + 1, d, h + k] = low
    odd = parity == 1
    inner = inner_ref[outs : outs + share].astype(F32)
    outer = outer_ref[outs : outs + share].astype(F32)
    send_ref[8, 0] = jnp.swapaxes(jnp.where(odd, inner, outer), 0, 1).astype(BF16)
    send_ref[8, 1] = jnp.swapaxes(jnp.where(odd, outer, inner), 0, 1).astype(BF16)


def add_parts(parts_ref, mine_ref):
    mine_ref[...] = jnp.sum(parts_ref[...], axis=0)


def shares_next(keep_ref, sent_ref, got_ref, kept_ref, send_ref):
    blocks = keep_ref.shape[0]
    half = blocks // 2
    for r in range(blocks):
        value = keep_ref[r] + got_ref[2 * r].astype(F32) + got_ref[2 * r + 1].astype(F32)
        if r < half:
            kept_ref[r] = value
        else:
            high, low = split(value)
            send_ref[2 * (r - half)] = high
            send_ref[2 * (r - half) + 1] = low
    place = 2 * half
    for ref in (sent_ref, got_ref):
        for n in range(2 * blocks, ref.shape[0]):
            send_ref[place] = ref[n]
            place += 1


def spread_sums(mine_ref, spread_ref):
    for k in range(spread_ref.shape[0]):
        spread_ref[k] = mine_ref[...]


def padded_plane(target, lines):
    rows = len(lines)
    blank = jnp.zeros(target.shape[1:], BF16)
    target[0] = blank
    target[rows + 1] = blank
    for h in range(rows):
        target[h + 1] = jnp.concatenate(lines[h], axis=0)


def weights_ahead(taps, depths):
    return jnp.concatenate(
        [
            jnp.concatenate([taps[9 * a + 3 * b + c] for a in depths for b in range(3)], axis=1)
            for c in range(3)
        ],
        axis=0,
    )


def own_output(bias_ref, vol_ref, taps_ref, part_ref, vpad):
    peers, depth, rows, _, cols = vol_ref.shape
    taps = taps_ref[...]
    outs, chans = taps.shape[1:]
    row = lax.broadcasted_iota(jnp.int32, (3 * outs, 2 * cols), 0)
    bias = jnp.zeros(row.shape, F32)
    for o in range(outs):
        bias = jnp.where(row == outs + o, bias_ref[o], bias)
    for d in range(depth):
        padded_plane(vpad.at[d], [[vol_ref[s, d, h] for s in range(peers)] for h in range(rows)])
    for d in range(depth):
        ahead = weights_ahead(taps, [e - d + 1 for e in range(depth)])
        for h in range(0, rows, 2):
            stack = jnp.concatenate(
                [
                    vpad[0:depth, h + k : h + k + 3].reshape(3 * depth * chans, cols)
                    for k in range(2)
                ],
                axis=1,
            )
            part = dot(ahead, stack) + bias
            for k in range(2):
                part_ref[d, h + k] = part[:, k * cols : (k + 1) * cols]


def finish(
    sums_ref, part_ref, keep_ref, sent_ref, got_ref, taps_ref,
    weight_ref, bias_ref, out_ref, back_ref, halo, vpad,
):
    depth, rows, _, cols = part_ref.shape
    taps = taps_ref[...]
    outs, chans = taps.shape[1:]
    half = cols // 2
    for t in range(27):
        r, side = t // 2, t % 2
        weight_ref[t] = sums_ref[r, :, half * side : half * (side + 1)]
    total = jnp.sum(sums_ref[13, :, half:], axis=1, keepdims=True)
    wide = jnp.broadcast_to(total, (outs, cols))
    row = lax.broadcasted_iota(jnp.int32, (outs, cols), 0)
    lane = lax.broadcasted_iota(jnp.int32, (outs, cols), 1)
    flat = jnp.sum(jnp.where(row == lane, wide, 0.0), axis=0, keepdims=True)
    bias_ref[...] = flat[:, :outs]
    me = lax.axis_index("filt")
    first, second, third = SWAPS
    for place, r in enumerate((0, first, second, first ^ second)):
        halo[jnp.bitwise_xor(me, r)] = sent_ref[2 + place]
        halo[jnp.bitwise_xor(me, r ^ third)] = got_ref[2 + place]
    for d in range(depth):
        padded_plane(vpad.at[d], [[halo[s, d, h] for s in range(8)] for h in range(rows)])
        ahead = weights_ahead(taps, [2 * d])
        lines = []
        for h in range(0, rows, 2):
            stack = jnp.concatenate(
                [vpad[d, h + k : h + k + 3].reshape(3 * chans, cols) for k in range(2)], axis=1
            )
            part = dot(ahead, stack)
            for k in range(2):
                total = part[:, k * cols : (k + 1) * cols] + part_ref[d, h + k]
                lines.append(
                    total[outs : 2 * outs]
                    + slide(total[0:outs], -1)
                    + slide(total[2 * outs : 3 * outs], 1)
                )
        out_ref[:, d] = jnp.swapaxes(jnp.stack(lines), 0, 1).astype(BF16)
        total = keep_ref[0, d] + got_ref[0, d].astype(F32) + got_ref[1, d].astype(F32)
        back_ref[:, d] = jnp.swapaxes(total, 0, 1).astype(BF16)


def scaled(scale, every_ref, sums_ref):
    sums_ref[...] = every_ref[...] * scale


SWAPS = (2, 4, 1)
ORDER = [sum(bit for k, bit in enumerate(SWAPS) if n & (4 >> k)) for n in range(8)]
XY_GROUPS = [[16 * z + k for k in range(16)] for z in range(4)]
Z_GROUPS = [[16 * z + k for z in range(4)] for k in range(16)]
EVEN = [(i, i ^ 1) for i in range(64)]
ODD = [(i, ((i + 1) ^ 1) - 1) for i in range(1, 63)]


def swap_edges(odd, head, tail):
    inner = lax.ppermute(jnp.where(odd, head, tail), "space", EVEN)
    outer = lax.ppermute(jnp.where(odd, tail, head), "space", ODD)
    return inner, outer


def swap_pairs(bit):
    return [(f, f ^ bit) for f in range(8)]


def local(volume, weight, bias, grad_out):
    share, depth, rows, cols = volume.shape
    outs = grad_out.shape[0]
    chans = weight.shape[1]
    taps = weight.transpose(0, 2, 1)
    own = volume.transpose(1, 2, 0, 3)
    odd = jnp.bitwise_and(lax.axis_index("space").astype(jnp.int32), 1)
    head, tail = (
        jnp.concatenate([grad_out[:, d], volume[:, d]], axis=0) for d in (0, depth - 1)
    )
    inner, outer = swap_edges(odd == 1, head, tail)
    vol = lax.all_to_all(jnp.broadcast_to(own[None], (8,) + own.shape), "filt", 0, 0)
    block = (depth, rows, share, cols)
    planes, bias_sums, edge, known = pl.pallas_call(
        ready_planes,
        out_shape=(
            jax.ShapeDtypeStruct((depth + 2, rows + 2, 3 * outs, cols), BF16),
            jax.ShapeDtypeStruct((outs, cols // 2), F32),
            jax.ShapeDtypeStruct((chans, 9 * outs), BF16),
            jax.ShapeDtypeStruct((depth, rows, chans, cols), F32),
        ),
        in_specs=[WHOLE] * 3,
        out_specs=(WHOLE,) * 4,
        scratch_shapes=[pltpu.VMEM((chans, 27 * outs), F32)],
        compiler_params=PARAMS,
        cost_estimate=pl.CostEstimate(flops=9_500_000_000, bytes_accessed=0, transcendentals=0),
    )(grad_out, outer, taps)
    moved, keep, send = pl.pallas_call(
        shares_first,
        out_shape=(
            jax.ShapeDtypeStruct((depth + 2, rows + 2, 3 * outs, cols), BF16),
            jax.ShapeDtypeStruct((4,) + block, F32),
            jax.ShapeDtypeStruct((9,) + block, BF16),
        ),
        in_specs=[WHOLE] * 5,
        out_specs=(WHOLE,) * 3,
        compiler_params=PARAMS,
    )(planes, edge, known, outer, inner)
    got = lax.ppermute(send, "filt", swap_pairs(SWAPS[0]))
    sums = pl.pallas_call(
        weight_sums,
        out_shape=jax.ShapeDtypeStruct((16, outs, cols), F32),
        in_specs=[WHOLE] * 3,
        out_specs=WHOLE,
        compiler_params=PARAMS,
        cost_estimate=pl.CostEstimate(flops=6_000_000_000, bytes_accessed=0, transcendentals=0),
    )(vol, moved, bias_sums)
    parts = lax.all_to_all(sums, "space", 0, 0, axis_index_groups=XY_GROUPS)
    keep, send = pl.pallas_call(
        shares_next,
        out_shape=(
            jax.ShapeDtypeStruct((2,) + block, F32),
            jax.ShapeDtypeStruct((6,) + block, BF16),
        ),
        in_specs=[WHOLE] * 3,
        out_specs=(WHOLE,) * 2,
        compiler_params=PARAMS,
        cost_estimate=pl.CostEstimate(flops=1000, bytes_accessed=0, transcendentals=0),
    )(keep, send, got)
    got = lax.ppermute(send, "filt", swap_pairs(SWAPS[1]))
    mine = pl.pallas_call(
        add_parts,
        out_shape=jax.ShapeDtypeStruct((outs, cols), F32),
        in_specs=[WHOLE],
        out_specs=WHOLE,
        compiler_params=PARAMS,
        cost_estimate=pl.CostEstimate(flops=10_000_000_000, bytes_accessed=0, transcendentals=0),
    )(parts)
    mine = lax.psum(mine, "space", axis_index_groups=Z_GROUPS)
    mine, got, held = lax.optimization_barrier((mine, got, vol))
    spread = pl.pallas_call(
        spread_sums,
        out_shape=jax.ShapeDtypeStruct((16, outs, cols), F32),
        in_specs=[WHOLE],
        out_specs=WHOLE,
        compiler_params=PARAMS,
    )(mine)
    keep, send = pl.pallas_call(
        shares_next,
        out_shape=(
            jax.ShapeDtypeStruct((1,) + block, F32),
            jax.ShapeDtypeStruct((6,) + block, BF16),
        ),
        in_specs=[WHOLE] * 3,
        out_specs=(WHOLE,) * 2,
        compiler_params=PARAMS,
    )(keep, send, got)
    got = lax.ppermute(send, "filt", swap_pairs(SWAPS[2]))
    every = lax.all_to_all(spread, "space", 0, 0, axis_index_groups=XY_GROUPS)
    part = pl.pallas_call(
        own_output,
        out_shape=jax.ShapeDtypeStruct((depth, rows, 3 * outs, cols), F32),
        in_specs=[SCALAR] + [WHOLE] * 2,
        out_specs=WHOLE,
        scratch_shapes=[pltpu.VMEM((depth, rows + 2, chans, cols), BF16)],
        compiler_params=PARAMS,
    )(bias, held, taps)
    every, part = lax.optimization_barrier((every, part))
    scale = 1.0 / math.sqrt(depth * lax.axis_size("space") * rows * cols)
    every = pl.pallas_call(
        lambda *refs: scaled(scale, *refs),
        out_shape=jax.ShapeDtypeStruct((16, outs, cols), F32),
        in_specs=[WHOLE],
        out_specs=WHOLE,
        compiler_params=PARAMS,
        cost_estimate=pl.CostEstimate(flops=10_000_000_000, bytes_accessed=0, transcendentals=0),
    )(every)
    grad_taps, grad_bias, output, grad_volume = pl.pallas_call(
        finish,
        out_shape=(
            jax.ShapeDtypeStruct((27, outs, cols // 2), F32),
            jax.ShapeDtypeStruct((1, outs), F32),
            jax.ShapeDtypeStruct((outs, depth, rows, cols), BF16),
            jax.ShapeDtypeStruct((share, depth, rows, cols), BF16),
        ),
        in_specs=[WHOLE] * 6,
        out_specs=(WHOLE,) * 4,
        scratch_shapes=[
            pltpu.VMEM((8,) + block, BF16),
            pltpu.VMEM((depth, rows + 2, chans, cols), BF16),
        ],
        compiler_params=PARAMS,
    )(every, part, keep, send, got, taps)
    return (output, grad_volume, grad_taps.transpose(0, 2, 1), grad_bias.reshape(outs))


def solution(mesh):
    in_specs = (
        P("filt", "space", None, None),
        P(None, None, "filt"),
        P("filt"),
        P("filt", "space", None, None),
    )
    out_specs = (
        P("filt", "space", None, None),
        P("filt", "space", None, None),
        P(None, None, "filt"),
        P("filt"),
    )
    return jax.shard_map(local, mesh=mesh, in_specs=in_specs, out_specs=out_specs, check_vma=False)
```

```python
import math

import jax
import jax.numpy as jnp
from jax import lax
from jax.experimental import pallas as pl
from jax.experimental.pallas import tpu as pltpu
from jax.sharding import PartitionSpec as P

F32 = jnp.float32
BF16 = jnp.bfloat16
WHOLE = pl.BlockSpec(memory_space=pltpu.VMEM)
SCALAR = pl.BlockSpec(memory_space=pltpu.SMEM)
PARAMS = pltpu.CompilerParams(vmem_limit_bytes=40 * 1024 * 1024)


def dot(left, right):
    return lax.dot_general(left, right, (((1,), (0,)), ((), ())), preferred_element_type=F32)


def dot_lanes(left, right):
    return lax.dot_general(left, right, (((1,), (1,)), ((), ())), preferred_element_type=F32)


def slide(rows, step):
    size = rows.shape[-1]
    axis = rows.ndim - 1
    turned = pltpu.roll(rows, (-step) % size, axis)
    lane = lax.broadcasted_iota(jnp.int32, rows.shape, axis)
    edge = size - 1 if step > 0 else 0
    return jnp.where(lane == edge, 0.0, turned)


def shifted(plane, target):
    outs, rows, cols = plane.shape
    blank = jnp.zeros((3 * outs, cols), BF16)
    target[0] = blank
    target[rows + 1] = blank
    turned = jnp.swapaxes(plane, 0, 1)
    for h in range(rows):
        wide = turned[h]
        target[h + 1, 0:outs] = slide(wide, 1).astype(BF16)
        target[h + 1, outs : 2 * outs] = wide.astype(BF16)
        target[h + 1, 2 * outs : 3 * outs] = slide(wide, -1).astype(BF16)


def ready_planes(
    grad_ref, outer_ref, taps_ref, planes_ref, bias_ref, edge_ref, back_ref, turned
):
    outs, depth, rows, cols = grad_ref.shape
    odd = jnp.bitwise_and(lax.axis_index("space"), 1)
    planes_ref[(depth + 1) * (1 - odd)] = jnp.zeros(planes_ref.shape[1:], BF16)
    total = None
    for d in range(depth):
        plane = grad_ref[:, d].astype(F32)
        shifted(plane, planes_ref.at[d + 1])
        part = jnp.sum(plane, axis=1)
        total = part if total is None else total + part
    shifted(outer_ref[0:outs].astype(F32), planes_ref.at[(depth + 1) * odd])
    half = cols // 2
    bias_ref[...] = total[:, :half] + total[:, half:]
    chans = taps_ref.shape[2]
    share = chans // 8
    turned[...] = taps_ref[...].reshape(27 * outs, chans).astype(F32).T
    me = lax.axis_index("filt")
    behind = jnp.concatenate(
        [
            turned[pl.ds(pl.multiple_of(share * jnp.bitwise_xor(me, r), share), share)]
            for r in ORDER
        ],
        axis=0,
    )
    edge_ref[...] = jnp.where(odd == 1, behind[:, 18 * outs :], behind[:, : 9 * outs]).astype(BF16)
    behind = behind.astype(BF16)
    for d in range(depth):
        for h in range(0, rows, 2):
            back = dot(behind, moved_rows(planes_ref, d, h))
            for k in range(2):
                back_ref[d, h + k] = back[:, k * cols : (k + 1) * cols]


def weight_sums(vol_ref, gpad, bias_ref, sums_ref):
    peers, depth, rows, share, cols = vol_ref.shape
    outs = bias_ref.shape[0]
    chans = peers * share
    acc = None
    for places in [[(d, h) for h in range(0, rows, 2)] for d in range(depth)]:
        cells = jnp.concatenate(
            [
                jnp.concatenate([vol_ref[s, d, h + k] for s in range(peers)], axis=0)
                for d, h in places
                for k in range(2)
            ],
            axis=1,
        )
        moved = jnp.concatenate([moved_rows(gpad, d, h) for d, h in places], axis=1)
        part = dot_lanes(moved, cells)
        acc = part if acc is None else acc + part
    for r in range(14):
        first = acc[2 * r * outs : (2 * r + 1) * outs]
        second = bias_ref[...] if r == 13 else acc[(2 * r + 1) * outs : (2 * r + 2) * outs]
        sums_ref[r] = jnp.concatenate([first, second], axis=1)
    for r in range(14, 16):
        sums_ref[r] = jnp.zeros((outs, cols), F32)


def moved_rows(gpad, d, h):
    return jnp.concatenate(
        [
            jnp.concatenate(
                [gpad[d + 2 - a, h + k + 2 - b] for a in range(3) for b in range(3)], axis=0
            )
            for k in range(2)
        ],
        axis=1,
    )


def split(value):
    high = value.astype(BF16)
    return high, (value - high.astype(F32)).astype(BF16)


def shares_first(
    planes_ref, edge_ref, back_ref, outer_ref, inner_ref, gpad, keep_ref, send_ref
):
    _, depth, rows, share, cols = keep_ref.shape
    outs = inner_ref.shape[0] - share
    parity = jnp.bitwise_and(lax.axis_index("space"), 1)
    gpad[...] = planes_ref[...]
    even = gpad.at[(depth + 1) * (1 - parity)]
    shifted(inner_ref[0:outs].astype(F32), even)
    edge = edge_ref[...]
    near = (depth - 1) * (1 - parity)
    for h in range(0, rows, 2):
        moved = jnp.concatenate(
            [
                jnp.concatenate([even[h + k + 2 - b] for b in range(3)], axis=0)
                for k in range(2)
            ],
            axis=1,
        )
        part = dot(edge, moved)
        for k in range(2):
            for d, back in (
                (near, back_ref[near, h + k] + part[:, k * cols : (k + 1) * cols]),
                (depth - 1 - near, back_ref[depth - 1 - near, h + k]),
            ):
                for r in range(8):
                    value = back[share * r : share * (r + 1)]
                    if r < 4:
                        keep_ref[r, d, h + k] = value
                    else:
                        high, low = split(value)
                        send_ref[2 * (r - 4), d, h + k] = high
                        send_ref[2 * (r - 4) + 1, d, h + k] = low
    odd = parity == 1
    inner = inner_ref[outs : outs + share].astype(F32)
    outer = outer_ref[outs : outs + share].astype(F32)
    send_ref[8, 0] = jnp.swapaxes(jnp.where(odd, inner, outer), 0, 1).astype(BF16)
    send_ref[8, 1] = jnp.swapaxes(jnp.where(odd, outer, inner), 0, 1).astype(BF16)


def add_parts(parts_ref, mine_ref):
    mine_ref[...] = jnp.sum(parts_ref[...], axis=0)


def shares_next(keep_ref, sent_ref, got_ref, kept_ref, send_ref):
    blocks = keep_ref.shape[0]
    half = blocks // 2
    for r in range(blocks):
        value = keep_ref[r] + got_ref[2 * r].astype(F32) + got_ref[2 * r + 1].astype(F32)
        if r < half:
            kept_ref[r] = value
        else:
            high, low = split(value)
            send_ref[2 * (r - half)] = high
            send_ref[2 * (r - half) + 1] = low
    place = 2 * half
    for ref in (sent_ref, got_ref):
        for n in range(2 * blocks, ref.shape[0]):
            send_ref[place] = ref[n]
            place += 1


def spread_sums(mine_ref, spread_ref):
    for k in range(spread_ref.shape[0]):
        spread_ref[k] = mine_ref[...]


def padded_plane(target, lines):
    rows = len(lines)
    blank = jnp.zeros(target.shape[1:], BF16)
    target[0] = blank
    target[rows + 1] = blank
    for h in range(rows):
        target[h + 1] = jnp.concatenate(lines[h], axis=0)


def weights_ahead(taps, depths):
    return jnp.concatenate(
        [
            jnp.concatenate([taps[9 * a + 3 * b + c] for a in depths for b in range(3)], axis=1)
            for c in range(3)
        ],
        axis=0,
    )


def own_output(bias_ref, vol_ref, taps_ref, part_ref, edges_ref, vpad, turned):
    peers, depth, rows, _, cols = vol_ref.shape
    taps = taps_ref[...]
    outs, chans = taps.shape[1:]
    row = lax.broadcasted_iota(jnp.int32, (3 * outs, 2 * cols), 0)
    bias = jnp.zeros(row.shape, F32)
    for o in range(outs):
        bias = jnp.where(row == outs + o, bias_ref[o], bias)
    for d in range(depth):
        padded_plane(vpad.at[d], [[vol_ref[s, d, h] for s in range(peers)] for h in range(rows)])
    for d in range(depth):
        ahead = weights_ahead(taps, [e - d + 1 for e in range(depth)])
        for h in range(0, rows, 2):
            stack = jnp.concatenate(
                [
                    vpad[0:depth, h + k : h + k + 3].reshape(3 * depth * chans, cols)
                    for k in range(2)
                ],
                axis=1,
            )
            part = dot(ahead, stack) + bias
            for k in range(2):
                part_ref[d, h + k] = part[:, k * cols : (k + 1) * cols]
    share = chans // peers
    turned[...] = taps.reshape(27 * outs, chans).astype(F32).T
    me = lax.axis_index("filt")
    first, second, third = SWAPS
    near = (0, first, second, first ^ second)
    lines = jnp.concatenate(
        [
            turned[pl.ds(pl.multiple_of(share * jnp.bitwise_xor(me, r), share), share)]
            for r in near + tuple(r ^ third for r in near)
        ],
        axis=0,
    ).T.astype(BF16)
    lines = [lines[outs * t : outs * (t + 1)] for t in range(27)]
    for d in range(depth):
        edges_ref[d] = weights_ahead(lines, [2 * d])


def finish(
    sums_ref, part_ref, keep_ref, sent_ref, got_ref, edges_ref,
    weight_ref, bias_ref, out_ref, back_ref, vpad,
):
    depth, rows, _, cols = part_ref.shape
    outs = sums_ref.shape[1]
    chans = vpad.shape[2]
    half = cols // 2
    for t in range(27):
        r, side = t // 2, t % 2
        weight_ref[t] = sums_ref[r, :, half * side : half * (side + 1)]
    total = jnp.sum(sums_ref[13, :, half:], axis=1, keepdims=True)
    wide = jnp.broadcast_to(total, (outs, cols))
    row = lax.broadcasted_iota(jnp.int32, (outs, cols), 0)
    lane = lax.broadcasted_iota(jnp.int32, (outs, cols), 1)
    flat = jnp.sum(jnp.where(row == lane, wide, 0.0), axis=0, keepdims=True)
    bias_ref[...] = flat[:, :outs]
    for d in range(depth):
        blocks = [ref.at[2 + n, d] for ref in (sent_ref, got_ref) for n in range(4)]
        padded_plane(vpad.at[d], [[block[h] for block in blocks] for h in range(rows)])
        ahead = edges_ref[d]
        lines = []
        for h in range(0, rows, 2):
            stack = jnp.concatenate(
                [vpad[d, h + k : h + k + 3].reshape(3 * chans, cols) for k in range(2)], axis=1
            )
            part = dot(ahead, stack)
            for k in range(2):
                total = part[:, k * cols : (k + 1) * cols] + part_ref[d, h + k]
                lines.append(
                    total[outs : 2 * outs]
                    + slide(total[0:outs], -1)
                    + slide(total[2 * outs : 3 * outs], 1)
                )
        out_ref[:, d] = jnp.swapaxes(jnp.stack(lines), 0, 1).astype(BF16)
        total = keep_ref[0, d] + got_ref[0, d].astype(F32) + got_ref[1, d].astype(F32)
        back_ref[:, d] = jnp.swapaxes(total, 0, 1).astype(BF16)


def scaled(scale, every_ref, sums_ref):
    sums_ref[...] = every_ref[...] * scale


SWAPS = (2, 4, 1)
ORDER = [sum(bit for k, bit in enumerate(SWAPS) if n & (4 >> k)) for n in range(8)]
XY_GROUPS = [[16 * z + k for k in range(16)] for z in range(4)]
Z_GROUPS = [[16 * z + k for z in range(4)] for k in range(16)]
EVEN = [(i, i ^ 1) for i in range(64)]
ODD = [(i, ((i + 1) ^ 1) - 1) for i in range(1, 63)]


def swap_edges(odd, head, tail):
    inner = lax.ppermute(jnp.where(odd, head, tail), "space", EVEN)
    outer = lax.ppermute(jnp.where(odd, tail, head), "space", ODD)
    return inner, outer


def swap_pairs(bit):
    return [(f, f ^ bit) for f in range(8)]


def local(volume, weight, bias, grad_out):
    share, depth, rows, cols = volume.shape
    outs = grad_out.shape[0]
    chans = weight.shape[1]
    taps = weight.transpose(0, 2, 1)
    own = volume.transpose(1, 2, 0, 3)
    odd = jnp.bitwise_and(lax.axis_index("space").astype(jnp.int32), 1)
    head, tail = (
        jnp.concatenate([grad_out[:, d], volume[:, d]], axis=0) for d in (0, depth - 1)
    )
    inner, outer = swap_edges(odd == 1, head, tail)
    vol = lax.all_to_all(jnp.broadcast_to(own[None], (8,) + own.shape), "filt", 0, 0)
    block = (depth, rows, share, cols)
    planes, bias_sums, edge, known = pl.pallas_call(
        ready_planes,
        out_shape=(
            jax.ShapeDtypeStruct((depth + 2, rows + 2, 3 * outs, cols), BF16),
            jax.ShapeDtypeStruct((outs, cols // 2), F32),
            jax.ShapeDtypeStruct((chans, 9 * outs), BF16),
            jax.ShapeDtypeStruct((depth, rows, chans, cols), F32),
        ),
        in_specs=[WHOLE] * 3,
        out_specs=(WHOLE,) * 4,
        scratch_shapes=[pltpu.VMEM((chans, 27 * outs), F32)],
        compiler_params=PARAMS,
        cost_estimate=pl.CostEstimate(flops=9_500_000_000, bytes_accessed=0, transcendentals=0),
    )(grad_out, outer, taps)
    moved, keep, send = pl.pallas_call(
        shares_first,
        out_shape=(
            jax.ShapeDtypeStruct((depth + 2, rows + 2, 3 * outs, cols), BF16),
            jax.ShapeDtypeStruct((4,) + block, F32),
            jax.ShapeDtypeStruct((9,) + block, BF16),
        ),
        in_specs=[WHOLE] * 5,
        out_specs=(WHOLE,) * 3,
        compiler_params=PARAMS,
    )(planes, edge, known, outer, inner)
    got = lax.ppermute(send, "filt", swap_pairs(SWAPS[0]))
    sums = pl.pallas_call(
        weight_sums,
        out_shape=jax.ShapeDtypeStruct((16, outs, cols), F32),
        in_specs=[WHOLE] * 3,
        out_specs=WHOLE,
        compiler_params=PARAMS,
        cost_estimate=pl.CostEstimate(flops=6_000_000_000, bytes_accessed=0, transcendentals=0),
    )(vol, moved, bias_sums)
    parts = lax.all_to_all(sums, "space", 0, 0, axis_index_groups=XY_GROUPS)
    keep, send = pl.pallas_call(
        shares_next,
        out_shape=(
            jax.ShapeDtypeStruct((2,) + block, F32),
            jax.ShapeDtypeStruct((6,) + block, BF16),
        ),
        in_specs=[WHOLE] * 3,
        out_specs=(WHOLE,) * 2,
        compiler_params=PARAMS,
        cost_estimate=pl.CostEstimate(flops=1000, bytes_accessed=0, transcendentals=0),
    )(keep, send, got)
    got = lax.ppermute(send, "filt", swap_pairs(SWAPS[1]))
    mine = pl.pallas_call(
        add_parts,
        out_shape=jax.ShapeDtypeStruct((outs, cols), F32),
        in_specs=[WHOLE],
        out_specs=WHOLE,
        compiler_params=PARAMS,
        cost_estimate=pl.CostEstimate(flops=10_000_000_000, bytes_accessed=0, transcendentals=0),
    )(parts)
    mine = lax.psum(mine, "space", axis_index_groups=Z_GROUPS)
    mine, got, held = lax.optimization_barrier((mine, got, vol))
    spread = pl.pallas_call(
        spread_sums,
        out_shape=jax.ShapeDtypeStruct((16, outs, cols), F32),
        in_specs=[WHOLE],
        out_specs=WHOLE,
        compiler_params=PARAMS,
    )(mine)
    keep, send = pl.pallas_call(
        shares_next,
        out_shape=(
            jax.ShapeDtypeStruct((1,) + block, F32),
            jax.ShapeDtypeStruct((6,) + block, BF16),
        ),
        in_specs=[WHOLE] * 3,
        out_specs=(WHOLE,) * 2,
        compiler_params=PARAMS,
    )(keep, send, got)
    got = lax.ppermute(send, "filt", swap_pairs(SWAPS[2]))
    every = lax.all_to_all(spread, "space", 0, 0, axis_index_groups=XY_GROUPS)
    part, edges = pl.pallas_call(
        own_output,
        out_shape=(
            jax.ShapeDtypeStruct((depth, rows, 3 * outs, cols), F32),
            jax.ShapeDtypeStruct((depth, 3 * outs, 3 * chans), BF16),
        ),
        in_specs=[SCALAR] + [WHOLE] * 2,
        out_specs=(WHOLE,) * 2,
        scratch_shapes=[
            pltpu.VMEM((depth, rows + 2, chans, cols), BF16),
            pltpu.VMEM((chans, 27 * outs), F32),
        ],
        compiler_params=PARAMS,
    )(bias, held, taps)
    every, part = lax.optimization_barrier((every, part))
    scale = 1.0 / math.sqrt(depth * lax.axis_size("space") * rows * cols)
    every = pl.pallas_call(
        lambda *refs: scaled(scale, *refs),
        out_shape=jax.ShapeDtypeStruct((16, outs, cols), F32),
        in_specs=[WHOLE],
        out_specs=WHOLE,
        compiler_params=PARAMS,
        cost_estimate=pl.CostEstimate(flops=10_000_000_000, bytes_accessed=0, transcendentals=0),
    )(every)
    grad_taps, grad_bias, output, grad_volume = pl.pallas_call(
        finish,
        out_shape=(
            jax.ShapeDtypeStruct((27, outs, cols // 2), F32),
            jax.ShapeDtypeStruct((1, outs), F32),
            jax.ShapeDtypeStruct((outs, depth, rows, cols), BF16),
            jax.ShapeDtypeStruct((share, depth, rows, cols), BF16),
        ),
        in_specs=[WHOLE] * 6,
        out_specs=(WHOLE,) * 4,
        scratch_shapes=[pltpu.VMEM((depth, rows + 2, chans, cols), BF16)],
        compiler_params=PARAMS,
    )(every, part, keep, send, got, edges)
    return (output, grad_volume, grad_taps.transpose(0, 2, 1), grad_bias.reshape(outs))


def solution(mesh):
    in_specs = (
        P("filt", "space", None, None),
        P(None, None, "filt"),
        P("filt"),
        P("filt", "space", None, None),
    )
    out_specs = (
        P("filt", "space", None, None),
        P("filt", "space", None, None),
        P(None, None, "filt"),
        P("filt"),
    )
    return jax.shard_map(local, mesh=mesh, in_specs=in_specs, out_specs=out_specs, check_vma=False)
```

```python
import math

import jax
import jax.numpy as jnp
from jax import lax
from jax.experimental import pallas as pl
from jax.experimental.pallas import tpu as pltpu
from jax.sharding import PartitionSpec as P

F32 = jnp.float32
BF16 = jnp.bfloat16
WHOLE = pl.BlockSpec(memory_space=pltpu.VMEM)
SCALAR = pl.BlockSpec(memory_space=pltpu.SMEM)
PARAMS = pltpu.CompilerParams(vmem_limit_bytes=40 * 1024 * 1024)


def dot(left, right):
    return lax.dot_general(left, right, (((1,), (0,)), ((), ())), preferred_element_type=F32)


def dot_lanes(left, right):
    return lax.dot_general(left, right, (((1,), (1,)), ((), ())), preferred_element_type=F32)


def slide(rows, step):
    size = rows.shape[-1]
    axis = rows.ndim - 1
    turned = pltpu.roll(rows, (-step) % size, axis)
    lane = lax.broadcasted_iota(jnp.int32, rows.shape, axis)
    edge = size - 1 if step > 0 else 0
    return jnp.where(lane == edge, 0.0, turned)


def shifted(plane, target):
    outs, rows, cols = plane.shape
    blank = jnp.zeros((3 * outs, cols), BF16)
    target[0] = blank
    target[rows + 1] = blank
    turned = jnp.swapaxes(plane, 0, 1)
    for h in range(rows):
        wide = turned[h]
        target[h + 1, 0:outs] = slide(wide, 1).astype(BF16)
        target[h + 1, outs : 2 * outs] = wide.astype(BF16)
        target[h + 1, 2 * outs : 3 * outs] = slide(wide, -1).astype(BF16)


def ready_planes(
    grad_ref, outer_ref, taps_ref, planes_ref, bias_ref, edge_ref, back_ref, turned
):
    outs, depth, rows, cols = grad_ref.shape
    odd = jnp.bitwise_and(lax.axis_index("space"), 1)
    planes_ref[(depth + 1) * (1 - odd)] = jnp.zeros(planes_ref.shape[1:], BF16)
    total = None
    for d in range(depth):
        plane = grad_ref[:, d].astype(F32)
        shifted(plane, planes_ref.at[d + 1])
        part = jnp.sum(plane, axis=1)
        total = part if total is None else total + part
    shifted(outer_ref[0:outs].astype(F32), planes_ref.at[(depth + 1) * odd])
    half = cols // 2
    bias_ref[...] = total[:, :half] + total[:, half:]
    chans = taps_ref.shape[2]
    share = chans // 8
    turned[...] = taps_ref[...].reshape(27 * outs, chans).astype(F32).T
    me = lax.axis_index("filt")
    behind = jnp.concatenate(
        [
            turned[pl.ds(pl.multiple_of(share * jnp.bitwise_xor(me, r), share), share)]
            for r in ORDER
        ],
        axis=0,
    )
    edge_ref[...] = jnp.where(odd == 1, behind[:, 18 * outs :], behind[:, : 9 * outs]).astype(BF16)
    behind = behind.astype(BF16)
    for d in range(depth):
        for h in range(0, rows, 2):
            back = dot(behind, moved_rows(planes_ref, d, h))
            for k in range(2):
                back_ref[d, h + k] = back[:, k * cols : (k + 1) * cols]


def weight_sums(vol_ref, gpad, bias_ref, sums_ref):
    peers, depth, rows, share, cols = vol_ref.shape
    outs = bias_ref.shape[0]
    chans = peers * share
    acc = jnp.zeros((27 * outs, chans), F32)
    for d in range(depth):
        for h in range(0, rows, 2):
            cells = jnp.concatenate(
                [
                    jnp.concatenate([vol_ref[s, d, h + k] for s in range(peers)], axis=0)
                    for k in range(2)
                ],
                axis=1,
            )
            acc = acc + dot_lanes(moved_rows(gpad, d, h), cells)
    for r in range(14):
        first = acc[2 * r * outs : (2 * r + 1) * outs]
        second = bias_ref[...] if r == 13 else acc[(2 * r + 1) * outs : (2 * r + 2) * outs]
        sums_ref[r] = jnp.concatenate([first, second], axis=1)
    for r in range(14, 16):
        sums_ref[r] = jnp.zeros((outs, cols), F32)


def moved_rows(gpad, d, h):
    return jnp.concatenate(
        [
            jnp.concatenate(
                [gpad[d + 2 - a, h + k + 2 - b] for a in range(3) for b in range(3)], axis=0
            )
            for k in range(2)
        ],
        axis=1,
    )


def split(value):
    high = value.astype(BF16)
    return high, (value - high.astype(F32)).astype(BF16)


def shares_first(
    planes_ref, edge_ref, back_ref, outer_ref, inner_ref, gpad, keep_ref, send_ref
):
    _, depth, rows, share, cols = keep_ref.shape
    outs = inner_ref.shape[0] - share
    parity = jnp.bitwise_and(lax.axis_index("space"), 1)
    gpad[...] = planes_ref[...]
    even = gpad.at[(depth + 1) * (1 - parity)]
    shifted(inner_ref[0:outs].astype(F32), even)
    edge = edge_ref[...]
    near = (depth - 1) * (1 - parity)
    for h in range(0, rows, 2):
        moved = jnp.concatenate(
            [
                jnp.concatenate([even[h + k + 2 - b] for b in range(3)], axis=0)
                for k in range(2)
            ],
            axis=1,
        )
        part = dot(edge, moved)
        for k in range(2):
            for d, back in (
                (near, back_ref[near, h + k] + part[:, k * cols : (k + 1) * cols]),
                (depth - 1 - near, back_ref[depth - 1 - near, h + k]),
            ):
                for r in range(8):
                    value = back[share * r : share * (r + 1)]
                    if r < 4:
                        keep_ref[r, d, h + k] = value
                    else:
                        high, low = split(value)
                        send_ref[2 * (r - 4), d, h + k] = high
                        send_ref[2 * (r - 4) + 1, d, h + k] = low
    odd = parity == 1
    inner = inner_ref[outs : outs + share].astype(F32)
    outer = outer_ref[outs : outs + share].astype(F32)
    send_ref[8, 0] = jnp.swapaxes(jnp.where(odd, inner, outer), 0, 1).astype(BF16)
    send_ref[8, 1] = jnp.swapaxes(jnp.where(odd, outer, inner), 0, 1).astype(BF16)


def add_parts(parts_ref, mine_ref):
    mine_ref[...] = jnp.sum(parts_ref[...], axis=0)


def shares_next(keep_ref, sent_ref, got_ref, kept_ref, send_ref):
    blocks = keep_ref.shape[0]
    half = blocks // 2
    for r in range(blocks):
        value = keep_ref[r] + got_ref[2 * r].astype(F32) + got_ref[2 * r + 1].astype(F32)
        if r < half:
            kept_ref[r] = value
        else:
            high, low = split(value)
            send_ref[2 * (r - half)] = high
            send_ref[2 * (r - half) + 1] = low
    place = 2 * half
    for ref in (sent_ref, got_ref):
        for n in range(2 * blocks, ref.shape[0]):
            send_ref[place] = ref[n]
            place += 1


def spread_sums(mine_ref, spread_ref):
    for k in range(spread_ref.shape[0]):
        spread_ref[k] = mine_ref[...]


def padded_plane(target, lines):
    rows = len(lines)
    blank = jnp.zeros(target.shape[1:], BF16)
    target[0] = blank
    target[rows + 1] = blank
    for h in range(rows):
        target[h + 1] = jnp.concatenate(lines[h], axis=0)


def weights_ahead(taps, depths):
    return jnp.concatenate(
        [
            jnp.concatenate([taps[9 * a + 3 * b + c] for a in depths for b in range(3)], axis=1)
            for c in range(3)
        ],
        axis=0,
    )


def own_output(bias_ref, vol_ref, taps_ref, part_ref, vpad):
    peers, depth, rows, _, cols = vol_ref.shape
    taps = taps_ref[...]
    outs, chans = taps.shape[1:]
    row = lax.broadcasted_iota(jnp.int32, (3 * outs, 2 * cols), 0)
    bias = jnp.zeros(row.shape, F32)
    for o in range(outs):
        bias = jnp.where(row == outs + o, bias_ref[o], bias)
    for d in range(depth):
        padded_plane(vpad.at[d], [[vol_ref[s, d, h] for s in range(peers)] for h in range(rows)])
    for d in range(depth):
        ahead = weights_ahead(taps, [e - d + 1 for e in range(depth)])
        for h in range(0, rows, 2):
            stack = jnp.concatenate(
                [
                    vpad[0:depth, h + k : h + k + 3].reshape(3 * depth * chans, cols)
                    for k in range(2)
                ],
                axis=1,
            )
            part = dot(ahead, stack) + bias
            for k in range(2):
                part_ref[d, h + k] = part[:, k * cols : (k + 1) * cols]


def finish(
    sums_ref, part_ref, keep_ref, sent_ref, got_ref, taps_ref,
    weight_ref, bias_ref, out_ref, back_ref, halo, vpad,
):
    depth, rows, _, cols = part_ref.shape
    taps = taps_ref[...]
    outs, chans = taps.shape[1:]
    half = cols // 2
    for t in range(27):
        r, side = t // 2, t % 2
        weight_ref[t] = sums_ref[r, :, half * side : half * (side + 1)]
    total = jnp.sum(sums_ref[13, :, half:], axis=1, keepdims=True)
    wide = jnp.broadcast_to(total, (outs, cols))
    row = lax.broadcasted_iota(jnp.int32, (outs, cols), 0)
    lane = lax.broadcasted_iota(jnp.int32, (outs, cols), 1)
    flat = jnp.sum(jnp.where(row == lane, wide, 0.0), axis=0, keepdims=True)
    bias_ref[...] = flat[:, :outs]
    me = lax.axis_index("filt")
    first, second, third = SWAPS
    for place, r in enumerate((0, first, second, first ^ second)):
        halo[jnp.bitwise_xor(me, r)] = sent_ref[2 + place]
        halo[jnp.bitwise_xor(me, r ^ third)] = got_ref[2 + place]
    for d in range(depth):
        padded_plane(vpad.at[d], [[halo[s, d, h] for s in range(8)] for h in range(rows)])
        ahead = weights_ahead(taps, [2 * d])
        lines = []
        for h in range(0, rows, 2):
            stack = jnp.concatenate(
                [vpad[d, h + k : h + k + 3].reshape(3 * chans, cols) for k in range(2)], axis=1
            )
            part = dot(ahead, stack)
            for k in range(2):
                total = part[:, k * cols : (k + 1) * cols] + part_ref[d, h + k]
                lines.append(
                    total[outs : 2 * outs]
                    + slide(total[0:outs], -1)
                    + slide(total[2 * outs : 3 * outs], 1)
                )
        out_ref[:, d] = jnp.swapaxes(jnp.stack(lines), 0, 1).astype(BF16)
        total = keep_ref[0, d] + got_ref[0, d].astype(F32) + got_ref[1, d].astype(F32)
        back_ref[:, d] = jnp.swapaxes(total, 0, 1).astype(BF16)


def scaled(scale, every_ref, sums_ref):
    sums_ref[...] = every_ref[...] * scale


SWAPS = (2, 4, 1)
ORDER = [sum(bit for k, bit in enumerate(SWAPS) if n & (4 >> k)) for n in range(8)]
XY_GROUPS = [[16 * z + k for k in range(16)] for z in range(4)]
Z_GROUPS = [[16 * z + k for z in range(4)] for k in range(16)]
EVEN = [(i, i ^ 1) for i in range(64)]
ODD = [(i, ((i + 1) ^ 1) - 1) for i in range(1, 63)]


def swap_pairs(bit):
    return [(f, f ^ bit) for f in range(8)]


def local(volume, weight, bias, grad_out):
    share, depth, rows, cols = volume.shape
    outs = grad_out.shape[0]
    chans = weight.shape[1]
    taps = weight.transpose(0, 2, 1)
    own = volume.transpose(1, 2, 0, 3)
    odd = jnp.bitwise_and(lax.axis_index("space").astype(jnp.int32), 1)
    inner, outer = (
        lax.ppermute(
            jnp.concatenate(
                [
                    lax.dynamic_index_in_dim(cells, plane, axis=1, keepdims=False)
                    for cells in (grad_out, volume)
                ],
                axis=0,
            ),
            "space",
            pairs,
        )
        for plane, pairs in (((depth - 1) * (1 - odd), EVEN), ((depth - 1) * odd, ODD))
    )
    vol = lax.all_to_all(jnp.broadcast_to(own[None], (8,) + own.shape), "filt", 0, 0)
    block = (depth, rows, share, cols)
    planes, bias_sums, edge, known = pl.pallas_call(
        ready_planes,
        out_shape=(
            jax.ShapeDtypeStruct((depth + 2, rows + 2, 3 * outs, cols), BF16),
            jax.ShapeDtypeStruct((outs, cols // 2), F32),
            jax.ShapeDtypeStruct((chans, 9 * outs), BF16),
            jax.ShapeDtypeStruct((depth, rows, chans, cols), F32),
        ),
        in_specs=[WHOLE] * 3,
        out_specs=(WHOLE,) * 4,
        scratch_shapes=[pltpu.VMEM((chans, 27 * outs), F32)],
        compiler_params=PARAMS,
        cost_estimate=pl.CostEstimate(flops=9_500_000_000, bytes_accessed=0, transcendentals=0),
    )(grad_out, outer, taps)
    moved, keep, send = pl.pallas_call(
        shares_first,
        out_shape=(
            jax.ShapeDtypeStruct((depth + 2, rows + 2, 3 * outs, cols), BF16),
            jax.ShapeDtypeStruct((4,) + block, F32),
            jax.ShapeDtypeStruct((9,) + block, BF16),
        ),
        in_specs=[WHOLE] * 5,
        out_specs=(WHOLE,) * 3,
        compiler_params=PARAMS,
    )(planes, edge, known, outer, inner)
    got = lax.ppermute(send, "filt", swap_pairs(SWAPS[0]))
    sums = pl.pallas_call(
        weight_sums,
        out_shape=jax.ShapeDtypeStruct((16, outs, cols), F32),
        in_specs=[WHOLE] * 3,
        out_specs=WHOLE,
        compiler_params=PARAMS,
        cost_estimate=pl.CostEstimate(flops=6_000_000_000, bytes_accessed=0, transcendentals=0),
    )(vol, moved, bias_sums)
    parts = lax.all_to_all(sums, "space", 0, 0, axis_index_groups=XY_GROUPS)
    keep, send = pl.pallas_call(
        shares_next,
        out_shape=(
            jax.ShapeDtypeStruct((2,) + block, F32),
            jax.ShapeDtypeStruct((6,) + block, BF16),
        ),
        in_specs=[WHOLE] * 3,
        out_specs=(WHOLE,) * 2,
        compiler_params=PARAMS,
        cost_estimate=pl.CostEstimate(flops=1000, bytes_accessed=0, transcendentals=0),
    )(keep, send, got)
    got = lax.ppermute(send, "filt", swap_pairs(SWAPS[1]))
    mine = pl.pallas_call(
        add_parts,
        out_shape=jax.ShapeDtypeStruct((outs, cols), F32),
        in_specs=[WHOLE],
        out_specs=WHOLE,
        compiler_params=PARAMS,
        cost_estimate=pl.CostEstimate(flops=10_000_000_000, bytes_accessed=0, transcendentals=0),
    )(parts)
    mine = lax.psum(mine, "space", axis_index_groups=Z_GROUPS)
    mine, got, held = lax.optimization_barrier((mine, got, vol))
    spread = pl.pallas_call(
        spread_sums,
        out_shape=jax.ShapeDtypeStruct((16, outs, cols), F32),
        in_specs=[WHOLE],
        out_specs=WHOLE,
        compiler_params=PARAMS,
    )(mine)
    keep, send = pl.pallas_call(
        shares_next,
        out_shape=(
            jax.ShapeDtypeStruct((1,) + block, F32),
            jax.ShapeDtypeStruct((6,) + block, BF16),
        ),
        in_specs=[WHOLE] * 3,
        out_specs=(WHOLE,) * 2,
        compiler_params=PARAMS,
    )(keep, send, got)
    got = lax.ppermute(send, "filt", swap_pairs(SWAPS[2]))
    every = lax.all_to_all(spread, "space", 0, 0, axis_index_groups=XY_GROUPS)
    part = pl.pallas_call(
        own_output,
        out_shape=jax.ShapeDtypeStruct((depth, rows, 3 * outs, cols), F32),
        in_specs=[SCALAR] + [WHOLE] * 2,
        out_specs=WHOLE,
        scratch_shapes=[pltpu.VMEM((depth, rows + 2, chans, cols), BF16)],
        compiler_params=PARAMS,
    )(bias, held, taps)
    every, part = lax.optimization_barrier((every, part))
    scale = 1.0 / math.sqrt(depth * lax.axis_size("space") * rows * cols)
    every = pl.pallas_call(
        lambda *refs: scaled(scale, *refs),
        out_shape=jax.ShapeDtypeStruct((16, outs, cols), F32),
        in_specs=[WHOLE],
        out_specs=WHOLE,
        compiler_params=PARAMS,
        cost_estimate=pl.CostEstimate(flops=10_000_000_000, bytes_accessed=0, transcendentals=0),
    )(every)
    grad_taps, grad_bias, output, grad_volume = pl.pallas_call(
        finish,
        out_shape=(
            jax.ShapeDtypeStruct((27, outs, cols // 2), F32),
            jax.ShapeDtypeStruct((1, outs), F32),
            jax.ShapeDtypeStruct((outs, depth, rows, cols), BF16),
            jax.ShapeDtypeStruct((share, depth, rows, cols), BF16),
        ),
        in_specs=[WHOLE] * 6,
        out_specs=(WHOLE,) * 4,
        scratch_shapes=[
            pltpu.VMEM((8,) + block, BF16),
            pltpu.VMEM((depth, rows + 2, chans, cols), BF16),
        ],
        compiler_params=PARAMS,
    )(every, part, keep, send, got, taps)
    return (output, grad_volume, grad_taps.transpose(0, 2, 1), grad_bias.reshape(outs))


def solution(mesh):
    in_specs = (
        P("filt", "space", None, None),
        P(None, None, "filt"),
        P("filt"),
        P("filt", "space", None, None),
    )
    out_specs = (
        P("filt", "space", None, None),
        P("filt", "space", None, None),
        P(None, None, "filt"),
        P("filt"),
    )
    return jax.shard_map(local, mesh=mesh, in_specs=in_specs, out_specs=out_specs, check_vma=False)
```

```python
import math

import jax
import jax.numpy as jnp
from jax import lax
from jax.experimental import pallas as pl
from jax.experimental.pallas import tpu as pltpu
from jax.sharding import PartitionSpec as P

F32 = jnp.float32
BF16 = jnp.bfloat16
WHOLE = pl.BlockSpec(memory_space=pltpu.VMEM)
SCALAR = pl.BlockSpec(memory_space=pltpu.SMEM)
PARAMS = pltpu.CompilerParams(vmem_limit_bytes=40 * 1024 * 1024)


def dot(left, right):
    return lax.dot_general(left, right, (((1,), (0,)), ((), ())), preferred_element_type=F32)


def dot_lanes(left, right):
    return lax.dot_general(left, right, (((1,), (1,)), ((), ())), preferred_element_type=F32)


def slide(rows, step):
    size = rows.shape[-1]
    axis = rows.ndim - 1
    turned = pltpu.roll(rows, (-step) % size, axis)
    lane = lax.broadcasted_iota(jnp.int32, rows.shape, axis)
    edge = size - 1 if step > 0 else 0
    return jnp.where(lane == edge, 0.0, turned)


def shifted(plane, target):
    outs, rows, cols = plane.shape
    blank = jnp.zeros((3 * outs, cols), BF16)
    target[0] = blank
    target[rows + 1] = blank
    turned = jnp.swapaxes(plane, 0, 1)
    for h in range(rows):
        wide = turned[h]
        target[h + 1, 0:outs] = slide(wide, 1).astype(BF16)
        target[h + 1, outs : 2 * outs] = wide.astype(BF16)
        target[h + 1, 2 * outs : 3 * outs] = slide(wide, -1).astype(BF16)


def ready_planes(
    grad_ref, outer_ref, taps_ref, planes_ref, bias_ref, edge_ref, back_ref, turned
):
    outs, depth, rows, cols = grad_ref.shape
    odd = jnp.bitwise_and(lax.axis_index("space"), 1)
    planes_ref[(depth + 1) * (1 - odd)] = jnp.zeros(planes_ref.shape[1:], BF16)
    total = None
    for d in range(depth):
        plane = grad_ref[:, d].astype(F32)
        shifted(plane, planes_ref.at[d + 1])
        part = jnp.sum(plane, axis=1)
        total = part if total is None else total + part
    shifted(outer_ref[0:outs].astype(F32), planes_ref.at[(depth + 1) * odd])
    half = cols // 2
    bias_ref[...] = total[:, :half] + total[:, half:]
    chans = taps_ref.shape[2]
    share = chans // 8
    turned[...] = taps_ref[...].reshape(27 * outs, chans).astype(F32).T
    me = lax.axis_index("filt")
    behind = jnp.concatenate(
        [
            turned[pl.ds(pl.multiple_of(share * jnp.bitwise_xor(me, r), share), share)]
            for r in ORDER
        ],
        axis=0,
    )
    edge_ref[...] = jnp.where(odd == 1, behind[:, 18 * outs :], behind[:, : 9 * outs]).astype(BF16)
    behind = behind.astype(BF16)
    for d in range(depth):
        for h in range(0, rows, 2):
            back = dot(behind, moved_rows(planes_ref, d, h))
            for k in range(2):
                back_ref[d, h + k] = back[:, k * cols : (k + 1) * cols]


def weight_sums(vol_ref, gpad, bias_ref, sums_ref):
    peers, depth, rows, share, cols = vol_ref.shape
    outs = bias_ref.shape[0]
    chans = peers * share
    acc = None
    for places in [[(d, h) for h in range(0, rows, 2)] for d in range(depth)]:
        cells = jnp.concatenate(
            [
                jnp.concatenate([vol_ref[s, d, h + k] for s in range(peers)], axis=0)
                for d, h in places
                for k in range(2)
            ],
            axis=1,
        )
        moved = jnp.concatenate([moved_rows(gpad, d, h) for d, h in places], axis=1)
        part = dot_lanes(moved, cells)
        acc = part if acc is None else acc + part
    for r in range(14):
        first = acc[2 * r * outs : (2 * r + 1) * outs]
        second = bias_ref[...] if r == 13 else acc[(2 * r + 1) * outs : (2 * r + 2) * outs]
        sums_ref[r] = jnp.concatenate([first, second], axis=1)
    for r in range(14, 16):
        sums_ref[r] = jnp.zeros((outs, cols), F32)


def moved_rows(gpad, d, h):
    return jnp.concatenate(
        [
            jnp.concatenate(
                [gpad[d + 2 - a, h + k + 2 - b] for a in range(3) for b in range(3)], axis=0
            )
            for k in range(2)
        ],
        axis=1,
    )


def split(value):
    high = value.astype(BF16)
    return high, (value - high.astype(F32)).astype(BF16)


def shares_first(
    planes_ref, edge_ref, back_ref, outer_ref, inner_ref, gpad, keep_ref, send_ref
):
    _, depth, rows, share, cols = keep_ref.shape
    outs = inner_ref.shape[0] - share
    parity = jnp.bitwise_and(lax.axis_index("space"), 1)
    gpad[...] = planes_ref[...]
    even = gpad.at[(depth + 1) * (1 - parity)]
    shifted(inner_ref[0:outs].astype(F32), even)
    edge = edge_ref[...]
    near = (depth - 1) * (1 - parity)
    for h in range(0, rows, 2):
        moved = jnp.concatenate(
            [
                jnp.concatenate([even[h + k + 2 - b] for b in range(3)], axis=0)
                for k in range(2)
            ],
            axis=1,
        )
        part = dot(edge, moved)
        for k in range(2):
            for d, back in (
                (near, back_ref[near, h + k] + part[:, k * cols : (k + 1) * cols]),
                (depth - 1 - near, back_ref[depth - 1 - near, h + k]),
            ):
                for r in range(8):
                    value = back[share * r : share * (r + 1)]
                    if r < 4:
                        keep_ref[r, d, h + k] = value
                    else:
                        high, low = split(value)
                        send_ref[2 * (r - 4), d, h + k] = high
                        send_ref[2 * (r - 4) + 1, d, h + k] = low
    odd = parity == 1
    inner = inner_ref[outs : outs + share].astype(F32)
    outer = outer_ref[outs : outs + share].astype(F32)
    send_ref[8, 0] = jnp.swapaxes(jnp.where(odd, inner, outer), 0, 1).astype(BF16)
    send_ref[8, 1] = jnp.swapaxes(jnp.where(odd, outer, inner), 0, 1).astype(BF16)


def add_parts(parts_ref, mine_ref):
    mine_ref[...] = jnp.sum(parts_ref[...], axis=0)


def shares_next(keep_ref, sent_ref, got_ref, kept_ref, send_ref):
    blocks = keep_ref.shape[0]
    half = blocks // 2
    for r in range(blocks):
        value = keep_ref[r] + got_ref[2 * r].astype(F32) + got_ref[2 * r + 1].astype(F32)
        if r < half:
            kept_ref[r] = value
        else:
            high, low = split(value)
            send_ref[2 * (r - half)] = high
            send_ref[2 * (r - half) + 1] = low
    place = 2 * half
    for ref in (sent_ref, got_ref):
        for n in range(2 * blocks, ref.shape[0]):
            send_ref[place] = ref[n]
            place += 1


def spread_sums(mine_ref, spread_ref):
    for k in range(spread_ref.shape[0]):
        spread_ref[k] = mine_ref[...]


def padded_plane(target, lines):
    rows = len(lines)
    blank = jnp.zeros(target.shape[1:], BF16)
    target[0] = blank
    target[rows + 1] = blank
    for h in range(rows):
        target[h + 1] = jnp.concatenate(lines[h], axis=0)


def weights_ahead(taps, depths):
    return jnp.concatenate(
        [
            jnp.concatenate([taps[9 * a + 3 * b + c] for a in depths for b in range(3)], axis=1)
            for c in range(3)
        ],
        axis=0,
    )


def own_output(bias_ref, vol_ref, taps_ref, part_ref, vpad):
    peers, depth, rows, _, cols = vol_ref.shape
    taps = taps_ref[...]
    outs, chans = taps.shape[1:]
    row = lax.broadcasted_iota(jnp.int32, (3 * outs, 2 * cols), 0)
    bias = jnp.zeros(row.shape, F32)
    for o in range(outs):
        bias = jnp.where(row == outs + o, bias_ref[o], bias)
    for d in range(depth):
        padded_plane(vpad.at[d], [[vol_ref[s, d, h] for s in range(peers)] for h in range(rows)])
    for d in range(depth):
        ahead = weights_ahead(taps, [e - d + 1 for e in range(depth)])
        for h in range(0, rows, 2):
            stack = jnp.concatenate(
                [
                    vpad[0:depth, h + k : h + k + 3].reshape(3 * depth * chans, cols)
                    for k in range(2)
                ],
                axis=1,
            )
            part = dot(ahead, stack) + bias
            for k in range(2):
                part_ref[d, h + k] = part[:, k * cols : (k + 1) * cols]


def finish(
    sums_ref, part_ref, keep_ref, sent_ref, got_ref, taps_ref,
    weight_ref, bias_ref, out_ref, back_ref, halo, vpad,
):
    depth, rows, _, cols = part_ref.shape
    taps = taps_ref[...]
    outs, chans = taps.shape[1:]
    half = cols // 2
    for t in range(27):
        r, side = t // 2, t % 2
        weight_ref[t] = sums_ref[r, :, half * side : half * (side + 1)]
    total = jnp.sum(sums_ref[13, :, half:], axis=1, keepdims=True)
    wide = jnp.broadcast_to(total, (outs, cols))
    row = lax.broadcasted_iota(jnp.int32, (outs, cols), 0)
    lane = lax.broadcasted_iota(jnp.int32, (outs, cols), 1)
    flat = jnp.sum(jnp.where(row == lane, wide, 0.0), axis=0, keepdims=True)
    bias_ref[...] = flat[:, :outs]
    me = lax.axis_index("filt")
    first, second, third = SWAPS
    for place, r in enumerate((0, first, second, first ^ second)):
        halo[jnp.bitwise_xor(me, r)] = sent_ref[2 + place]
        halo[jnp.bitwise_xor(me, r ^ third)] = got_ref[2 + place]
    for d in range(depth):
        padded_plane(vpad.at[d], [[halo[s, d, h] for s in range(8)] for h in range(rows)])
        ahead = weights_ahead(taps, [2 * d])
        lines = []
        for h in range(0, rows, 2):
            stack = jnp.concatenate(
                [vpad[d, h + k : h + k + 3].reshape(3 * chans, cols) for k in range(2)], axis=1
            )
            part = dot(ahead, stack)
            for k in range(2):
                total = part[:, k * cols : (k + 1) * cols] + part_ref[d, h + k]
                lines.append(
                    total[outs : 2 * outs]
                    + slide(total[0:outs], -1)
                    + slide(total[2 * outs : 3 * outs], 1)
                )
        out_ref[:, d] = jnp.swapaxes(jnp.stack(lines), 0, 1).astype(BF16)
        total = keep_ref[0, d] + got_ref[0, d].astype(F32) + got_ref[1, d].astype(F32)
        back_ref[:, d] = jnp.swapaxes(total, 0, 1).astype(BF16)


def scaled(scale, every_ref, sums_ref):
    sums_ref[...] = every_ref[...] * scale


SWAPS = (2, 4, 1)
ORDER = [sum(bit for k, bit in enumerate(SWAPS) if n & (4 >> k)) for n in range(8)]
XY_GROUPS = [[16 * z + k for k in range(16)] for z in range(4)]
Z_GROUPS = [[16 * z + k for z in range(4)] for k in range(16)]
EVEN = [(i, i ^ 1) for i in range(64)]
ODD = [(i, ((i + 1) ^ 1) - 1) for i in range(1, 63)]


def swap_edges(odd, head, tail):
    inner = lax.ppermute(jnp.where(odd, head, tail), "space", EVEN)
    outer = lax.ppermute(jnp.where(odd, tail, head), "space", ODD)
    return inner, outer


def swap_pairs(bit):
    return [(f, f ^ bit) for f in range(8)]


def local(volume, weight, bias, grad_out):
    share, depth, rows, cols = volume.shape
    outs = grad_out.shape[0]
    chans = weight.shape[1]
    taps = weight.transpose(0, 2, 1)
    own = volume.transpose(1, 2, 0, 3)
    odd = jnp.bitwise_and(lax.axis_index("space").astype(jnp.int32), 1)
    head, tail = (
        jnp.concatenate([grad_out[:, d], volume[:, d]], axis=0) for d in (0, depth - 1)
    )
    inner, outer = swap_edges(odd == 1, head, tail)
    vol = lax.all_to_all(jnp.broadcast_to(own[None], (8,) + own.shape), "filt", 0, 0)
    block = (depth, rows, share, cols)
    planes, bias_sums, edge, known = pl.pallas_call(
        ready_planes,
        out_shape=(
            jax.ShapeDtypeStruct((depth + 2, rows + 2, 3 * outs, cols), BF16),
            jax.ShapeDtypeStruct((outs, cols // 2), F32),
            jax.ShapeDtypeStruct((chans, 9 * outs), BF16),
            jax.ShapeDtypeStruct((depth, rows, chans, cols), F32),
        ),
        in_specs=[WHOLE] * 3,
        out_specs=(WHOLE,) * 4,
        scratch_shapes=[pltpu.VMEM((chans, 27 * outs), F32)],
        compiler_params=PARAMS,
        cost_estimate=pl.CostEstimate(flops=9_500_000_000, bytes_accessed=0, transcendentals=0),
    )(grad_out, outer, taps)
    moved, keep, send = pl.pallas_call(
        shares_first,
        out_shape=(
            jax.ShapeDtypeStruct((depth + 2, rows + 2, 3 * outs, cols), BF16),
            jax.ShapeDtypeStruct((4,) + block, F32),
            jax.ShapeDtypeStruct((9,) + block, BF16),
        ),
        in_specs=[WHOLE] * 5,
        out_specs=(WHOLE,) * 3,
        compiler_params=PARAMS,
    )(planes, edge, known, outer, inner)
    got = lax.ppermute(send, "filt", swap_pairs(SWAPS[0]))
    sums = pl.pallas_call(
        weight_sums,
        out_shape=jax.ShapeDtypeStruct((16, outs, cols), F32),
        in_specs=[WHOLE] * 3,
        out_specs=WHOLE,
        compiler_params=PARAMS,
        cost_estimate=pl.CostEstimate(flops=6_000_000_000, bytes_accessed=0, transcendentals=0),
    )(vol, moved, bias_sums)
    parts = lax.all_to_all(sums, "space", 0, 0, axis_index_groups=XY_GROUPS)
    keep, send = pl.pallas_call(
        shares_next,
        out_shape=(
            jax.ShapeDtypeStruct((2,) + block, F32),
            jax.ShapeDtypeStruct((6,) + block, BF16),
        ),
        in_specs=[WHOLE] * 3,
        out_specs=(WHOLE,) * 2,
        compiler_params=PARAMS,
        cost_estimate=pl.CostEstimate(flops=1000, bytes_accessed=0, transcendentals=0),
    )(keep, send, got)
    got = lax.ppermute(send, "filt", swap_pairs(SWAPS[1]))
    mine = pl.pallas_call(
        add_parts,
        out_shape=jax.ShapeDtypeStruct((outs, cols), F32),
        in_specs=[WHOLE],
        out_specs=WHOLE,
        compiler_params=PARAMS,
        cost_estimate=pl.CostEstimate(flops=10_000_000_000, bytes_accessed=0, transcendentals=0),
    )(parts)
    mine = lax.psum(mine, "space", axis_index_groups=Z_GROUPS)
    mine, got, held = lax.optimization_barrier((mine, got, vol))
    spread = pl.pallas_call(
        spread_sums,
        out_shape=jax.ShapeDtypeStruct((16, outs, cols), F32),
        in_specs=[WHOLE],
        out_specs=WHOLE,
        compiler_params=PARAMS,
    )(mine)
    keep, send = pl.pallas_call(
        shares_next,
        out_shape=(
            jax.ShapeDtypeStruct((1,) + block, F32),
            jax.ShapeDtypeStruct((6,) + block, BF16),
        ),
        in_specs=[WHOLE] * 3,
        out_specs=(WHOLE,) * 2,
        compiler_params=PARAMS,
    )(keep, send, got)
    got = lax.ppermute(send, "filt", swap_pairs(SWAPS[2]))
    every = lax.all_to_all(spread, "space", 0, 0, axis_index_groups=XY_GROUPS)
    part = pl.pallas_call(
        own_output,
        out_shape=jax.ShapeDtypeStruct((depth, rows, 3 * outs, cols), F32),
        in_specs=[SCALAR] + [WHOLE] * 2,
        out_specs=WHOLE,
        scratch_shapes=[pltpu.VMEM((depth, rows + 2, chans, cols), BF16)],
        compiler_params=PARAMS,
    )(bias, held, taps)
    every, part = lax.optimization_barrier((every, part))
    scale = 1.0 / math.sqrt(depth * lax.axis_size("space") * rows * cols)
    every = pl.pallas_call(
        lambda *refs: scaled(scale, *refs),
        out_shape=jax.ShapeDtypeStruct((16, outs, cols), F32),
        in_specs=[WHOLE],
        out_specs=WHOLE,
        compiler_params=PARAMS,
        cost_estimate=pl.CostEstimate(flops=10_000_000_000, bytes_accessed=0, transcendentals=0),
    )(every)
    grad_taps, grad_bias, output, grad_volume = pl.pallas_call(
        finish,
        out_shape=(
            jax.ShapeDtypeStruct((27, outs, cols // 2), F32),
            jax.ShapeDtypeStruct((1, outs), F32),
            jax.ShapeDtypeStruct((outs, depth, rows, cols), BF16),
            jax.ShapeDtypeStruct((share, depth, rows, cols), BF16),
        ),
        in_specs=[WHOLE] * 6,
        out_specs=(WHOLE,) * 4,
        scratch_shapes=[
            pltpu.VMEM((8,) + block, BF16),
            pltpu.VMEM((depth, rows + 2, chans, cols), BF16),
        ],
        compiler_params=PARAMS,
    )(every, part, keep, send, got, taps)
    return (output, grad_volume, grad_taps.transpose(0, 2, 1), grad_bias.reshape(outs))


def solution(mesh):
    in_specs = (
        P("filt", "space", None, None),
        P(None, None, "filt"),
        P("filt"),
        P("filt", "space", None, None),
    )
    out_specs = (
        P("filt", "space", None, None),
        P("filt", "space", None, None),
        P(None, None, "filt"),
        P("filt"),
    )
    return jax.shard_map(local, mesh=mesh, in_specs=in_specs, out_specs=out_specs, check_vma=False)
```
